128 devices in a mesh: gx: 8 (over z, core), gy: 16 (over y, x).
Axes of the slice: x: 4, y: 4, z: 4, core: 2. Of those that a mesh axis runs over, the one named last changes fastest.
Arguments:
- air_surface_exchanges: bfloat16 [8, 128, 1024], P(None, 'gy', 'gx'), may hold values from -6 to 6
- outbound_patch_tables: int32 [16, 8, 2, 2, 2, 64], P('gy', 'gx'), may hold values from -1 to 63, as said below
- outbound_coefficient_panels: bfloat16 [16, 8, 2, 2, 64, 16, 128], P('gy', 'gx'), may hold values from -1 to 1
- submerged_strata_tally: int32 [256, 4096], P('gy', 'gx'), may hold values from 0 to 10
- thermal_anomaly: float32 [10, 256, 4096], P(None, 'gy', 'gx'), may hold values from -6 to 6
- saltiness_anomaly: float32 [10, 256, 4096], P(None, 'gy', 'gx'), may hold values from -6 to 6
- inbound_patch_tables: int32 [16, 8, 2, 2, 2, 64], P('gy', 'gx'), may hold values from -1 to 63, as said below
- inbound_coefficient_panels: bfloat16 [16, 8, 2, 2, 64, 16, 128], P('gy', 'gx'), may hold values from -0.375 to 0.375
Outputs:
- new_temp: float32 [10, 256, 4096], P(None, 'gy', 'gx')
- new_salt: float32 [10, 256, 4096], P(None, 'gy', 'gx')
- atm_surface: float32 [4, 128, 1024], P(None, 'gy', 'gx')
The draws below stay inside these ranges and needn't reach their ends.
Inputs may be any that keep to these rules, and one draw needn't show every extreme that they name: outbound_patch_tables: row 0 lies below 64, row 1 below 64, both -1 together in unused slots, which stand at the end of each list. Entries with the same target block stand next to each other in rising order of that block; each list names each target block at most 2 times. No entry targets a latitude tile beyond the grid. inbound_patch_tables: row 0 lies below 64, row 1 below 64, both -1 together in unused slots, which stand at the end of each list. Entries with the same target block stand next to each other in rising order of that block. No entry targets a latitude tile beyond the grid.
All inputs are finite; a program needn't handle non-finite values.
Results may differ from the reference program's by a relative error of at most 0.0017.
Values sent between devices are 32-bit elements; how exact they have to be, the bound alone decides.
No kernel may reach another device: no remote copies, remote signals or barrier semaphores. Data moves between devices by JAX's collectives and lax.ppermute only.
A program may use at most 64 MiB of HBM per device.

```python
import jax
import jax.numpy as jnp
from jax import lax

OCN_ROWS = 16
OCN_COLS = 512
ATM_ROWS = 8
ATM_COLS = 128
SEA_BAND_STRATA = 10
FLUXES = 8
SRC_LEN = 16
DST_LEN = 128
COVERS = 2
DST_BLOCKS = 64
SRC_BLOCKS = 64
ENTRIES = 64
LAT_TILES = 16
LON_TILES = 8
SEA_GRID_NORTH = 256
SEA_GRID_EASTING = 4096
ATM_LAT = 128
ATM_LON = 1024


def pair_table(key):
    rows = jnp.arange(SEA_GRID_NORTH, dtype=jnp.int32)
    atm_row = jnp.minimum((rows + OCN_ROWS // 2) // 2, ATM_LAT - 1)
    per_row = SEA_GRID_EASTING // DST_LEN
    block_col = jnp.arange(per_row, dtype=jnp.int32)
    width = DST_LEN // 4
    step_len = min(SRC_LEN, width)
    row_offset = step_len * jax.random.randint(key, (SEA_GRID_NORTH,), 0, ATM_COLS // step_len).astype(jnp.int32)
    start = block_col[None, :] * width + row_offset[:, None]
    first = start // SRC_LEN
    slot_index = jnp.arange(COVERS, dtype=jnp.int32)
    src_cell = (first[:, :, None] + slot_index[None, None, :]) * SRC_LEN
    wrapped = jnp.mod(src_cell, ATM_LON)
    array_shape = (SEA_GRID_NORTH, per_row, COVERS)
    atm_lat_tile = jnp.broadcast_to((atm_row // ATM_ROWS)[:, None, None], array_shape)
    atm_lon_tile = wrapped // ATM_COLS
    src_local = (atm_row % ATM_ROWS)[:, None, None] * (ATM_COLS // SRC_LEN) + wrapped % ATM_COLS // SRC_LEN
    ocn_lat_tile = jnp.broadcast_to((rows // OCN_ROWS)[:, None, None], array_shape)
    ocn_lon_tile = jnp.broadcast_to((block_col * DST_LEN // OCN_COLS)[None, :, None], array_shape)
    dst_local = jnp.broadcast_to((rows % OCN_ROWS)[:, None, None] * (OCN_COLS // DST_LEN) + (block_col * DST_LEN % OCN_COLS // DST_LEN)[None, :, None], array_shape)
    parts = (atm_lat_tile, atm_lon_tile, src_local, ocn_lat_tile, ocn_lon_tile, dst_local)
    return [jnp.reshape(part_array, (-1,)).astype(jnp.int32) for part_array in parts]


def build_lists(key, from_lat, from_lon, to_lat, to_lon, local_from, local_to, to_count, base):
    step_lat = to_lat - from_lat + base
    step_lon = jnp.mod(to_lon - from_lon + base, LON_TILES)
    list_count = LAT_TILES * LON_TILES * 4
    list_id = (((from_lat * LON_TILES + from_lon) * 2 + step_lat) * 2 + step_lon).astype(jnp.int32)
    pair_count = list_id.shape[0]
    noise = jax.random.randint(key, (pair_count,), 0, COVERS)
    order_key = (list_id * to_count + local_to) * COVERS + noise
    order = jnp.argsort(order_key, stable=True)
    sorted_list = list_id[order]
    first_of = jnp.searchsorted(sorted_list, sorted_list, side='left')
    position = (jnp.arange(pair_count) - first_of).astype(jnp.int32)
    filled = jnp.full((list_count, 2, ENTRIES), -1, jnp.int32)
    filled = filled.at[sorted_list, 0, position].set(local_from[order].astype(jnp.int32), mode='drop')
    filled = filled.at[sorted_list, 1, position].set(local_to[order].astype(jnp.int32), mode='drop')
    return filled.reshape(LAT_TILES, LON_TILES, 2, 2, 2, ENTRIES)


def draw_outbound_patch_tables(key, part):
    atm_lat_tile, atm_lon_tile, src_local, ocn_lat_tile, ocn_lon_tile, dst_local = pair_table(key)
    key = jax.random.fold_in(key, 11)
    return build_lists(key, atm_lat_tile, atm_lon_tile, ocn_lat_tile, ocn_lon_tile, src_local, dst_local, DST_BLOCKS, 1)


def draw_inbound_patch_tables(key, part):
    atm_lat_tile, atm_lon_tile, src_local, ocn_lat_tile, ocn_lon_tile, dst_local = pair_table(key)
    key = jax.random.fold_in(key, 29)
    return build_lists(key, ocn_lat_tile, ocn_lon_tile, atm_lat_tile, atm_lon_tile, dst_local, src_local, SRC_BLOCKS, 0)


def plant(values, own_key, low, high):
    dims = values.shape
    spot = [jax.random.randint(jax.random.fold_in(own_key, axis), (), 0, dims[axis]) for axis in range(len(dims))]
    values = values.at[tuple(spot)].set(low)
    longest = dims.index(max(dims))
    spot[longest] = (spot[longest] + 1) % dims[longest]
    return values.at[tuple(spot)].set(high)


def level_of(key, extent, cuts, smallest, high):
    factor_of, own = 1.0, jax.random.fold_in(key, 6)
    for axis_at, blocks in cuts:
        steps = jnp.exp(jax.random.uniform(jax.random.fold_in(own, axis_at), (blocks,), jnp.float32, smallest / len(cuts), high / len(cuts)))
        factor_of = factor_of * jnp.repeat(steps, extent[axis_at] // blocks).reshape([-1 if axis == axis_at else 1 for axis in range(len(extent))])
    return factor_of


def scatter_about(rng, shape, scale, reach, shards=(), kind=jnp.bfloat16):
    values = scale * jax.random.normal(rng, shape, jnp.float32)
    if shards:
        values = values * level_of(rng, shape, shards, -0.22, 0.18)
    return jnp.clip(values, -reach, reach).astype(kind)


def setup_inputs(seed: int = 0) -> dict:
    keys = jax.random.split(jax.random.key(seed), 9)
    return {
        "air_surface_exchanges": scatter_about(keys[0], (FLUXES, ATM_LAT, ATM_LON), 1.0, 6.0, ((1, 16), (2, 8))),
        "outbound_patch_tables": draw_outbound_patch_tables(jax.random.fold_in(keys[8], 71), 0),
        "outbound_coefficient_panels": scatter_about(keys[2], (LAT_TILES, LON_TILES, 2, 2, ENTRIES, SRC_LEN, DST_LEN), (COVERS * SRC_LEN) ** -0.5, 1.0, ((0, 16), (1, 8))),
        "submerged_strata_tally": plant(jax.random.randint(keys[3], (SEA_GRID_NORTH, SEA_GRID_EASTING), 0, SEA_BAND_STRATA + 1), jax.random.fold_in(keys[3], 1), 0, SEA_BAND_STRATA).astype(jnp.int32),
        "thermal_anomaly": scatter_about(keys[4], (SEA_BAND_STRATA, SEA_GRID_NORTH, SEA_GRID_EASTING), 1.0, 6.0, ((1, 16), (2, 8)), jnp.float32),
        "saltiness_anomaly": scatter_about(keys[5], (SEA_BAND_STRATA, SEA_GRID_NORTH, SEA_GRID_EASTING), 1.0, 6.0, ((1, 16), (2, 8)), jnp.float32),
        "inbound_patch_tables": draw_inbound_patch_tables(jax.random.fold_in(keys[8], 71), 0),
        "inbound_coefficient_panels": scatter_about(keys[7], (LAT_TILES, LON_TILES, 2, 2, ENTRIES, SRC_LEN, DST_LEN), (2 * DST_LEN * max(1, SRC_LEN // (DST_LEN // 4))) ** -0.5, 0.375, ((0, 16), (1, 8))),
    }


HEAT_RATE = 0.1
SHORTWAVE_RATE = 0.1
FRESH_RATE = 0.05
SIDE_RATE = 0.18
MIX_BASE = 0.03
MIX_WIND = 0.09
MIX_DECAY = 0.8


def surface_terms(forcing):
    heat_flux = forcing[0] + forcing[1] + forcing[2]
    shortwave = forcing[3]
    fresh_flux = forcing[4] - forcing[5] + forcing[6]
    gust_term = forcing[7] * forcing[7] / (1.0 + forcing[7] * forcing[7])
    return jnp.stack([heat_flux, shortwave, fresh_flux, gust_term])


def advance(padded, wet_pad, planes):
    strata_total = padded.shape[1]
    height = padded.shape[2] - 2
    col_count = padded.shape[3] - 2
    centre = padded[:, :, 1:-1, 1:-1]
    wet_mid = wet_pad[:, 1:-1, 1:-1]
    side_sum = jnp.zeros_like(centre)
    for row_shift, col_shift in ((0, 1), (2, 1), (1, 0), (1, 2)):
        beside = padded[:, :, row_shift:row_shift + height, col_shift:col_shift + col_count]
        wet_beside = wet_pad[:, row_shift:row_shift + height, col_shift:col_shift + col_count]
        side_sum = side_sum + wet_beside * (beside - centre)
    depth_index = jnp.arange(strata_total - 1, dtype=jnp.float32)
    mixing = (MIX_BASE + MIX_WIND * planes[3])[None] * (MIX_DECAY ** depth_index)[:, None, None]
    across = mixing * wet_mid[:-1] * wet_mid[1:] * (centre[:, 1:] - centre[:, :-1])
    zero_face = jnp.zeros_like(across[:, :1])
    vertical = jnp.concatenate([across, zero_face], 1) - jnp.concatenate([zero_face, across], 1)
    profile = jnp.exp(-0.5 * jnp.arange(strata_total, dtype=jnp.float32))
    top_level = (jnp.arange(strata_total) == 0).astype(jnp.float32)[:, None, None]
    heat_source = SHORTWAVE_RATE * planes[1][None] * profile[:, None, None] + HEAT_RATE * top_level * planes[0][None]
    salt_source = -FRESH_RATE * top_level * planes[2][None] * centre[1, 0][None]
    source = jnp.stack([heat_source, salt_source])
    return centre + wet_mid * (SIDE_RATE * side_sum + vertical + source)


def to_tiles(fields, tile_rows, tile_cols, block_len):
    channels = fields.shape[0]
    lat_count = fields.shape[1] // tile_rows
    lon_count = fields.shape[2] // tile_cols
    arranged = fields.reshape(channels, lat_count, tile_rows, lon_count, tile_cols // block_len, block_len)
    arranged = arranged.transpose(1, 3, 2, 4, 0, 5)
    return arranged.reshape(lat_count, lon_count, tile_rows * (tile_cols // block_len), channels, block_len)


def from_tiles(blocks, tile_rows, tile_cols):
    lat_count, lon_count, block_count, channels, block_len = blocks.shape
    arranged = blocks.reshape(lat_count, lon_count, tile_rows, tile_cols // block_len, channels, block_len)
    arranged = arranged.transpose(4, 0, 2, 1, 3, 5)
    return arranged.reshape(channels, lat_count * tile_rows, lon_count * tile_cols)


def deliver(blocks, entry_lists, weight_tiles, out_count, pattern, base):
    lat_count = blocks.shape[0]
    lon_count = blocks.shape[1]

    def one_target(flat_index):
        lat_here = flat_index // lon_count
        lon_here = flat_index % lon_count
        running = None
        for lat_piece in range(2):
            for lon_piece in range(2):
                lat_from = lat_here - (lat_piece + base)
                lon_from = (lon_here - (lon_piece + base)) % lon_count
                inside = (lat_from >= 0) & (lat_from < lat_count)
                lat_safe = jnp.clip(lat_from, 0, lat_count - 1)
                sender = blocks[lat_safe, lon_from]
                entries = entry_lists[lat_safe, lon_from, lat_piece, lon_piece]
                tiles_here = weight_tiles[lat_safe, lon_from, lat_piece, lon_piece]
                picked = sender[jnp.maximum(entries[0], 0)]
                live_mask = ((entries[0] >= 0) & inside).astype(jnp.float32)
                pieces = jnp.einsum(pattern, picked.astype(jnp.float32), tiles_here.astype(jnp.float32)) * live_mask[:, None, None]
                summed = jax.ops.segment_sum(pieces, jnp.maximum(entries[1], 0), num_segments=out_count)
                running = summed if running is None else running + summed
        return running

    result = lax.map(one_target, jnp.arange(lat_count * lon_count, dtype=jnp.int32))
    return result.reshape((lat_count, lon_count) + result.shape[1:])


def pad_grid(fields):
    wrapped = jnp.concatenate([fields[..., -1:], fields, fields[..., :1]], -1)
    widths = [(0, 0)] * (fields.ndim - 2) + [(1, 1), (0, 0)]
    return jnp.pad(wrapped, widths)


def reference(air_surface_exchanges, outbound_patch_tables, outbound_coefficient_panels, submerged_strata_tally, thermal_anomaly, saltiness_anomaly, inbound_patch_tables, inbound_coefficient_panels):
    arrived = deliver(to_tiles(air_surface_exchanges, ATM_ROWS, ATM_COLS, SRC_LEN), outbound_patch_tables, outbound_coefficient_panels, DST_BLOCKS, "kcs,ksw->kcw", -1)
    forcing = from_tiles(arrived, OCN_ROWS, OCN_COLS)
    planes = surface_terms(forcing)
    wet = (jnp.arange(SEA_BAND_STRATA)[:, None, None] < submerged_strata_tally[None]).astype(jnp.float32)
    wet_pad = pad_grid(wet)
    transported_quantities = jnp.stack([thermal_anomaly, saltiness_anomaly])
    stepped = advance(pad_grid(transported_quantities), wet_pad, planes)
    final = advance(pad_grid(stepped), wet_pad, planes)
    new_temp = final[0]
    new_salt = final[1]
    wet_top = wet[0]
    surface = jnp.stack([new_temp[0] * wet_top, new_salt[0] * wet_top,
                         (new_temp[0] + new_temp[1] + new_temp[2]) / 3.0 * wet_top, wet_top]).astype(jnp.bfloat16)
    landed = deliver(to_tiles(surface, OCN_ROWS, OCN_COLS, DST_LEN), inbound_patch_tables, inbound_coefficient_panels, SRC_BLOCKS, "kcw,ksw->kcs", 0)
    atm_surface = from_tiles(landed, ATM_ROWS, ATM_COLS)
    return new_temp, new_salt, atm_surface
```

```python
import jax
import jax.numpy as jnp
from jax import lax
from jax.experimental import pallas as pl
from jax.experimental.pallas import tpu as pltpu
from jax.sharding import PartitionSpec as P

HEAT_RATE = 0.1
SHORTWAVE_RATE = 0.1
FRESH_RATE = 0.05
SIDE_RATE = 0.18
MIX_BASE = 0.03
MIX_WIND = 0.09
MIX_DECAY = 0.8

ROWS, COLS, LEVELS = 16, 512, 10
TILES = COLS // 128
F32, BF16 = jnp.float32, jnp.bfloat16
LIST_ROWS = 4 * 64
EDGE_ROWS = 24
VMEM = pl.BlockSpec(memory_space=pltpu.VMEM)
NN = (((1,), (0,)), ((), ()))
TN = (((0,), (0,)), ((), ()))
NT = (((1,), (1,)), ((), ()))


def iota(shape, axis):
    return lax.broadcasted_iota(jnp.int32, shape, axis)


def dot(x, y, dims=NN):
    return lax.dot_general(x, y, dims, preferred_element_type=F32)


def dot_split(ones, values):
    high = values.astype(BF16)
    low = (values - high.astype(F32)).astype(BF16)
    return dot(ones, high) + dot(ones, low)


def split_dot(values, ones):
    high = values.astype(BF16)
    low = (values - high.astype(F32)).astype(BF16)
    return dot(high, ones) + dot(low, ones)


def ocean_number(shape, axis):
    place = iota(shape, axis)
    return place % ROWS * TILES + place // ROWS


def atm_number(shape, axis):
    place = iota(shape, axis)
    return place % 8 * 8 + place // 8


def one_hot(number, names):
    return jnp.where(number == names, 1.0, 0.0).astype(BF16)


def group_mask():
    return iota((8, 128), 1) // 16 == iota((8, 128), 0)


def edge_columns(levels):
    lane = iota((ROWS, 128), 1)
    block = jnp.zeros((ROWS, 128), F32)
    for at, values in enumerate(levels):
        block = jnp.where(lane == at, values[:, 0:1], block)
        block = jnp.where(lane == 64 + at, values[:, COLS - 1 : COLS], block)
    return block


def outbound_kernel(air, table, panels, temp, salt, depth, own, to_gx, to_xe, to_xo, to_dg):
    odd_row = lax.axis_index("gy") % 2 == 1
    mask = group_mask()
    fold = (iota((128, 128), 0) % 16 == iota((128, 128), 1) % 16).astype(F32).astype(BF16)
    spread = []
    for c in range(8):
        for r in range(8):
            row = jnp.broadcast_to(air[c, r : r + 1, :].astype(F32), (8, 128))
            spread.append(jnp.where(mask, row, 0.0))
    tiled = dot(jnp.concatenate(spread, 0).astype(BF16), fold).astype(BF16)
    tiled = jnp.concatenate([tiled[c * 64 : (c + 1) * 64] for c in range(8)], 1)
    source = iota((64, 64), 0)
    target = ocean_number((64, 64), 0)
    for a in range(2):
        for b in range(2):
            picked = dot(one_hot(source, table[a, b, 0:1, :]), tiled, TN)
            planes = [[], [], [], []]
            for g in range(8):
                left = [
                    jnp.where(mask, picked[g * 8 : (g + 1) * 8, c * 128 : (c + 1) * 128], 0.0)
                    for c in range(8)
                ]
                piece = dot(
                    jnp.concatenate(left, 0).astype(BF16),
                    panels[2 * a + b, g * 128 : (g + 1) * 128, :],
                )
                f = [piece[c * 8 : (c + 1) * 8] for c in range(8)]
                planes[0].append(f[0] + f[1] + f[2])
                planes[1].append(f[3])
                planes[2].append(f[4] - f[5] + f[6])
                planes[3].append(f[7])
            pieces = jnp.concatenate([jnp.concatenate(p, 0) for p in planes], 1)
            summed = dot_split(one_hot(target, table[a, b, 1:2, :]), pieces)
            outs = {(1, 1): (own,), (1, 0): (to_gx,), (0, 1): (to_xe, to_xo), (0, 0): (to_dg,)}
            for out in outs[a, b]:
                for p in range(4):
                    out[p * 64 : (p + 1) * 64, :] = summed[:, p * 128 : (p + 1) * 128]
    deep = depth[...].astype(F32)
    levels = [temp[l] for l in range(LEVELS)] + [salt[l] for l in range(LEVELS)] + [deep]
    to_gx[LIST_ROWS : LIST_ROWS + ROWS, :] = edge_columns(levels)
    for out, first in ((to_xe, odd_row), (to_xo, jnp.logical_not(odd_row))):
        for base, rows in (
            (0, (temp[:, 0, :], temp[:, ROWS - 1, :])),
            (LEVELS, (salt[:, 0, :], salt[:, ROWS - 1, :])),
            (2 * LEVELS, (deep[0:1], deep[ROWS - 1 : ROWS])),
        ):
            edge = jnp.where(first, rows[0], rows[1])
            for s in range(TILES):
                at = LIST_ROWS + s * EDGE_ROWS + base
                out[at : at + edge.shape[0], :] = edge[:, s * 128 : (s + 1) * 128]


def beside(values, north, south, west, east):
    row, col = iota((ROWS, COLS), 0), iota((ROWS, COLS), 1)
    return (
        jnp.where(row == 0, north, pltpu.roll(values, 1, 0)),
        jnp.where(row == ROWS - 1, south, pltpu.roll(values, ROWS - 1, 0)),
        jnp.where(col == 0, west, pltpu.roll(values, 1, 1)),
        jnp.where(col == COLS - 1, east, pltpu.roll(values, COLS - 1, 1)),
    )


def advance(tracers, halos, depth, depths, planes, stores):
    heat, shortwave, fresh, gust = planes
    mixing = MIX_BASE + MIX_WIND * gust
    above = [None, None]
    for l in range(LEVELS):
        wet = depth > l
        wets = [d > l for d in depths]
        for t in range(2):
            centre = tracers[t][l]
            side = jnp.zeros_like(centre)
            for near, there in zip(beside(centre, *halos(t, l)), wets):
                side = side + jnp.where(there, near - centre, 0.0)
            change = SIDE_RATE * side
            if l < LEVELS - 1:
                across = mixing * (MIX_DECAY**l) * (tracers[t][l + 1] - centre)
                across = jnp.where(depth > l + 1, across, 0.0)
                change = change + across
            if l > 0:
                change = change - above[t]
            above[t] = across
            if t == 0:
                change = change + shortwave * (SHORTWAVE_RATE * 2.718281828459045 ** (-0.5 * l))
                if l == 0:
                    change = change + HEAT_RATE * heat
            elif l == 0:
                change = change - FRESH_RATE * fresh * centre
            stores(t, l, centre + jnp.where(wet, change, 0.0))


def first_kernel(
    own, core, zpair, xe, xo, dg, temp, salt, depth, new, cols, row_e, row_o, planes, depths
):
    odd_col = lax.axis_index("gx") % 2 == 1
    odd_row = lax.axis_index("gy") % 2 == 1

    def right(at, rows):
        return jnp.where(odd_col, zpair[at : at + rows, :], core[at : at + rows, :])

    def left(at, rows):
        return jnp.where(odd_col, core[at : at + rows, :], zpair[at : at + rows, :])

    def below(at, rows):
        return jnp.where(odd_row, xo[at : at + rows, :], xe[at : at + rows, :])

    def over(at, rows):
        return jnp.where(odd_row, xe[at : at + rows, :], xo[at : at + rows, :])

    forcing = []
    for p in range(4):
        parts = []
        for s in range(TILES):
            at = p * 64 + s * ROWS
            here = own[at : at + ROWS, :] + dg[at : at + ROWS, :]
            parts.append(here + right(at, ROWS) + below(at, ROWS))
        forcing.append(jnp.concatenate(parts, 1))
    squared = forcing[3] * forcing[3]
    forcing[3] = squared / (1.0 + squared)
    for p in range(4):
        planes[p] = forcing[p]
    west, east = left(LIST_ROWS, ROWS), right(LIST_ROWS, ROWS)
    norths = jnp.concatenate([over(LIST_ROWS + s * EDGE_ROWS, EDGE_ROWS) for s in range(TILES)], 1)
    souths = jnp.concatenate([below(LIST_ROWS + s * EDGE_ROWS, EDGE_ROWS) for s in range(TILES)], 1)

    def halos(t, l):
        at = t * LEVELS + l
        return (
            norths[at : at + 1],
            souths[at : at + 1],
            west[:, 64 + at : 65 + at],
            east[:, at : at + 1],
        )

    deep = depth[...].astype(F32)
    around = beside(deep, *halos(2, 0))
    for n in range(4):
        depths[n] = around[n]
    lane = iota((ROWS, 128), 1)
    block = [jnp.zeros((ROWS, 128), F32)]

    def store(t, l, value):
        new[t, l] = value
        at = t * LEVELS + l
        edge = jnp.where(lane == at, value[:, 0:1], block[0])
        block[0] = jnp.where(lane == 64 + at, value[:, COLS - 1 : COLS], edge)
        first, last = value[0:1], value[ROWS - 1 : ROWS]
        row_e[at : at + 1, :] = jnp.where(odd_row, first, last)
        row_o[at : at + 1, :] = jnp.where(odd_row, last, first)

    advance((temp, salt), halos, deep, around, forcing, store)
    cols[...] = block[0]


def second_kernel(
    old, core, zpair, xe, xo, planes, depths, depth, table, panels,
    new_temp, new_salt, own, to_gx, to_gy, to_dg,
):
    odd_col = lax.axis_index("gx") % 2 == 1
    odd_row = lax.axis_index("gy") % 2 == 1
    east = jnp.where(odd_col, zpair[...], core[...])
    west = jnp.where(odd_col, core[...], zpair[...])
    souths = jnp.where(odd_row, xo[...], xe[...])
    norths = jnp.where(odd_row, xe[...], xo[...])

    def halos(t, l):
        at = t * LEVELS + l
        return (
            norths[at : at + 1],
            souths[at : at + 1],
            west[:, 64 + at : 65 + at],
            east[:, at : at + 1],
        )

    deep = depth[...].astype(F32)
    around = [depths[n] for n in range(4)]
    top = {}

    def store(t, l, value):
        (new_temp, new_salt)[t][l] = value
        if l < 3:
            top[t, l] = value

    advance(
        (old.at[0], old.at[1]), halos, deep, around, [planes[p] for p in range(4)], store
    )
    wet_top = jnp.where(deep > 0, 1.0, 0.0)
    surface = (
        top[0, 0] * wet_top,
        top[1, 0] * wet_top,
        (top[0, 0] + top[0, 1] + top[0, 2]) / 3.0 * wet_top,
        wet_top,
    )
    blocks = jnp.concatenate(
        [
            jnp.concatenate([f[:, s * 128 : (s + 1) * 128] for s in range(TILES)], 0)
            for f in surface
        ],
        1,
    ).astype(BF16)
    mask = group_mask()
    place, lane = iota((512, 128), 0), iota((512, 128), 1)
    fold = jnp.where((place // 128 == lane // 16) & (place % 16 == lane % 16), 1.0, 0.0)
    fold = fold.astype(BF16)
    source = ocean_number((64, 64), 0)
    target = atm_number((64, 64), 0)
    outs = {(0, 0): own, (0, 1): to_gx, (1, 0): to_gy, (1, 1): to_dg}
    for a in range(2):
        for b in range(2):
            chosen = dot(one_hot(source, table[a, b, 0:1, :]), blocks, TN)
            kept = [[], [], [], []]
            for g in range(8):
                part = chosen[g * 8 : (g + 1) * 8]
                left = [part[:, c * 128 : (c + 1) * 128] for c in range(4)]
                piece = dot(
                    jnp.concatenate(left, 0).astype(BF16),
                    panels[2 * a + b, g * 128 : (g + 1) * 128, :],
                    NT,
                )
                for c in range(4):
                    kept[c].append(jnp.where(mask, piece[c * 8 : (c + 1) * 8], 0.0))
            kept = jnp.concatenate([jnp.concatenate(k, 0) for k in kept], 1)
            pieces = split_dot(kept, fold)
            outs[a, b][...] = dot_split(one_hot(target, table[a, b, 1:2, :]), pieces)


def final_kernel(own, gx, gy, dg, out):
    total = own[...] + gx[...] + gy[...] + dg[...]
    group = iota((8, 128), 1) // 16
    for c in range(4):
        field = jnp.zeros((8, 128), F32)
        for k in range(8):
            moved = pltpu.roll(total[k * 8 : (k + 1) * 8], (k - c) % 8 * 16, 1)
            field = jnp.where(group == k, moved, field)
        out[c] = field


def call(kernel, shapes, *args):
    return pl.pallas_call(
        kernel,
        out_shape=[jax.ShapeDtypeStruct(s, F32) for s in shapes],
        in_specs=[VMEM] * len(args),
        out_specs=[VMEM] * len(shapes),
        compiler_params=pltpu.CompilerParams(vmem_limit_bytes=24 * 1024 * 1024),
    )(*args)


def send(block, step):
    wide, high = lax.axis_size("gx"), lax.axis_size("gy")
    route = []
    for i in range(wide):
        for j in range(high):
            to = step(i, j)
            if 0 <= to[1] < high:
                route.append((i * high + j, to[0] % wide * high + to[1]))
    return lax.ppermute(block, ("gx", "gy"), route)


def pair(n):
    return n - 1 if n % 2 else n + 1


def other_pair(n):
    return n + 1 if n % 2 else n - 1


def per_device(air, out_tables, out_panels, depth, temp, salt, in_tables, in_panels):
    out_panels = out_panels.reshape(4, 1024, 128)
    in_panels = in_panels.reshape(4, 1024, 128)
    edged = LIST_ROWS + TILES * EDGE_ROWS
    own, to_gx, to_xe, to_xo, to_dg = call(
        outbound_kernel,
        [(LIST_ROWS, 128), (LIST_ROWS + ROWS, 128), (edged, 128), (edged, 128), (LIST_ROWS, 128)],
        air, out_tables[0, 0], out_panels, temp, salt, depth,
    )
    dg = send(to_dg, lambda i, j: (i - 1, j - 1))
    xo = send(to_xo, lambda i, j: (i, other_pair(j)))
    xe = send(to_xe, lambda i, j: (i, pair(j)))
    zpair = send(to_gx, lambda i, j: (other_pair(i), j))
    core = send(to_gx, lambda i, j: (pair(i), j))
    stepped, cols, row_e, row_o, planes, depths = call(
        first_kernel,
        [
            (2, LEVELS, ROWS, COLS), (ROWS, 128), (2 * LEVELS, COLS), (2 * LEVELS, COLS),
            (4, ROWS, COLS), (4, ROWS, COLS),
        ],
        own, core, zpair, xe, xo, dg, temp, salt, depth,
    )
    xo = send(row_o, lambda i, j: (i, other_pair(j)))
    xe = send(row_e, lambda i, j: (i, pair(j)))
    zpair = send(cols, lambda i, j: (other_pair(i), j))
    core = send(cols, lambda i, j: (pair(i), j))
    new_temp, new_salt, own, to_gx, to_gy, to_dg = call(
        second_kernel,
        [(LEVELS, ROWS, COLS)] * 2 + [(64, 128)] * 4,
        stepped, core, zpair, xe, xo, planes, depths, depth, in_tables[0, 0], in_panels,
    )
    dg = send(to_dg, lambda i, j: (i + 1, j + 1))
    gy = send(to_gy, lambda i, j: (i, j + 1))
    gx = send(to_gx, lambda i, j: (i + 1, j))
    (surface,) = call(final_kernel, [(4, 8, 128)], own, gx, gy, dg)
    return new_temp, new_salt, surface


def solution(mesh):
    in_specs = (
        P(None, "gy", "gx"),
        P("gy", "gx", None, None, None, None),
        P("gy", "gx", None, None, None, None, None),
        P("gy", "gx"),
        P(None, "gy", "gx"),
        P(None, "gy", "gx"),
        P("gy", "gx", None, None, None, None),
        P("gy", "gx", None, None, None, None, None),
    )
    out_specs = (P(None, "gy", "gx"), P(None, "gy", "gx"), P(None, "gy", "gx"))
    return jax.shard_map(
        per_device, mesh=mesh, in_specs=in_specs, out_specs=out_specs, check_vma=False
    )
```

```python
import jax
import jax.numpy as jnp
from jax import lax
from jax.experimental import pallas as pl
from jax.experimental.pallas import tpu as pltpu
from jax.sharding import PartitionSpec as P

HEAT_RATE = 0.1
SHORTWAVE_RATE = 0.1
FRESH_RATE = 0.05
SIDE_RATE = 0.18
MIX_BASE = 0.03
MIX_WIND = 0.09
MIX_DECAY = 0.8

ROWS, COLS, LEVELS = 16, 512, 10
TILES = COLS // 128
F32, BF16 = jnp.float32, jnp.bfloat16
LIST_ROWS = 4 * 64
EDGE_ROWS = 24
VMEM = pl.BlockSpec(memory_space=pltpu.VMEM)
HBM = pl.BlockSpec(memory_space=pltpu.HBM)
NN = (((1,), (0,)), ((), ()))
TN = (((0,), (0,)), ((), ()))
NT = (((1,), (1,)), ((), ()))


def iota(shape, axis):
    return lax.broadcasted_iota(jnp.int32, shape, axis)


def dot(x, y, dims=NN):
    return lax.dot_general(x, y, dims, preferred_element_type=F32)


def dot_split(ones, values):
    high = values.astype(BF16)
    low = (values - high.astype(F32)).astype(BF16)
    return dot(ones, high) + dot(ones, low)


def split_dot(values, ones):
    high = values.astype(BF16)
    low = (values - high.astype(F32)).astype(BF16)
    return dot(high, ones) + dot(low, ones)


def ocean_number(shape, axis):
    place = iota(shape, axis)
    return place % ROWS * TILES + place // ROWS


def atm_number(shape, axis):
    place = iota(shape, axis)
    return place % 8 * 8 + place // 8


def one_hot(number, names):
    return jnp.where(number == names, 1.0, 0.0).astype(BF16)


def group_mask():
    return iota((8, 128), 1) // 16 == iota((8, 128), 0)


def edge_columns(levels):
    lane = iota((ROWS, 128), 1)
    block = jnp.zeros((ROWS, 128), F32)
    for at, values in enumerate(levels):
        block = jnp.where(lane == at, values[:, 0:1], block)
        block = jnp.where(lane == 64 + at, values[:, COLS - 1 : COLS], block)
    return block


def spread_air(air, mask):
    fold = (iota((128, 128), 0) % 16 == iota((128, 128), 1) % 16).astype(F32).astype(BF16)
    spread = []
    for c in range(8):
        for r in range(8):
            row = jnp.broadcast_to(air[c, r : r + 1, :].astype(F32), (8, 128))
            spread.append(jnp.where(mask, row, 0.0))
    tiled = dot(jnp.concatenate(spread, 0).astype(BF16), fold).astype(BF16)
    return jnp.concatenate([tiled[c * 64 : (c + 1) * 64] for c in range(8)], 1)


def outbound_list(tiled, names, panel, mask, out):
    source = iota((64, 64), 0)
    target = ocean_number((64, 64), 0)
    picked = dot(one_hot(source, names[0:1, :]), tiled, TN)
    planes = [[], [], [], []]
    for g in range(8):
        left = [
            jnp.where(mask, picked[g * 8 : (g + 1) * 8, c * 128 : (c + 1) * 128], 0.0)
            for c in range(8)
        ]
        piece = dot(jnp.concatenate(left, 0).astype(BF16), panel[g * 128 : (g + 1) * 128, :])
        f = [piece[c * 8 : (c + 1) * 8] for c in range(8)]
        planes[0].append(f[0] + f[1] + f[2])
        planes[1].append(f[3])
        planes[2].append(f[4] - f[5] + f[6])
        planes[3].append(f[7])
    pieces = jnp.concatenate([jnp.concatenate(p, 0) for p in planes], 1)
    summed = dot_split(one_hot(target, names[1:2, :]), pieces)
    for p in range(4):
        out[p * 64 : (p + 1) * 64, :] = summed[:, p * 128 : (p + 1) * 128]


def fetch(sems, pairs):
    copies = [pltpu.make_async_copy(src, dst, sems.at[n]) for n, (src, dst) in enumerate(pairs)]
    for copy in copies:
        copy.start()
    return copies


def outbound_kernel(
    air_hbm, table_hbm, panels_hbm, temp_hbm, salt_hbm, depth_hbm, to_gx, to_gy, to_dg,
    air, table, panels, temp, salt, depth, sems,
):
    pairs = [(air_hbm, air), (table_hbm, table)]
    pairs += [(panels_hbm.at[n], panels.at[n]) for n in range(3)]
    pairs += [(temp_hbm, temp), (salt_hbm, salt), (depth_hbm, depth)]
    copies = fetch(sems, pairs)
    mask = group_mask()
    copies[0].wait()
    tiled = spread_air(air, mask)
    copies[1].wait()
    for n, out in ((0, to_dg), (1, to_gy), (2, to_gx)):
        copies[2 + n].wait()
        outbound_list(tiled, table[n // 2, n % 2], panels.at[n], mask, out)
    for copy in copies[5:]:
        copy.wait()
    deep = depth[...].astype(F32)
    levels = [temp[l] for l in range(LEVELS)] + [salt[l] for l in range(LEVELS)] + [deep]
    to_gx[LIST_ROWS : LIST_ROWS + ROWS, :] = edge_columns(levels)
    for base, edge in ((0, temp[:, 0, :]), (LEVELS, salt[:, 0, :]), (2 * LEVELS, deep[0:1])):
        for s in range(TILES):
            at = LIST_ROWS + s * EDGE_ROWS + base
            to_gy[at : at + edge.shape[0], :] = edge[:, s * 128 : (s + 1) * 128]


def beside(values, north, south, west, east):
    row, col = iota((ROWS, COLS), 0), iota((ROWS, COLS), 1)
    return (
        jnp.where(row == 0, north, pltpu.roll(values, 1, 0)),
        jnp.where(row == ROWS - 1, south, pltpu.roll(values, ROWS - 1, 0)),
        jnp.where(col == 0, west, pltpu.roll(values, 1, 1)),
        jnp.where(col == COLS - 1, east, pltpu.roll(values, COLS - 1, 1)),
    )


def side_sum(centre, nears, wets):
    side = jnp.zeros_like(centre)
    for near, there in zip(nears, wets):
        side = side + jnp.where(there, near - centre, 0.0)
    return SIDE_RATE * side


def inner_kernel(air, table, panels_hbm, temp, salt, depth, own, partial, panel, sem):
    copy = pltpu.make_async_copy(panels_hbm.at[3], panel, sem)
    copy.start()
    deep = depth[...].astype(F32)
    dry = jnp.zeros((1, 1), F32)
    around = beside(deep, dry, dry, dry, dry)
    for l in range(LEVELS):
        wet = deep > l
        wets = [d > l for d in around]
        for t, field in enumerate((temp, salt)):
            centre = field[l]
            side = side_sum(centre, beside(centre, dry, dry, dry, dry), wets)
            partial[t, l] = centre + jnp.where(wet, side, 0.0)
    mask = group_mask()
    tiled = spread_air(air, mask)
    copy.wait()
    outbound_list(tiled, table[1, 1], panel, mask, own)


def column_change(values, below, mixing, depth, l, across):
    change = 0.0 if l == 0 else -across
    if l < LEVELS - 1:
        across = mixing * (MIX_DECAY**l) * (below - values)
        across = jnp.where(depth > l + 1, across, 0.0)
        change = change + across
    return change, across


def source(t, l, planes, values):
    if t == 0:
        heating = planes[1] * (SHORTWAVE_RATE * 2.718281828459045 ** (-0.5 * l))
        return heating + HEAT_RATE * planes[0] if l == 0 else heating
    return -FRESH_RATE * planes[2] * values if l == 0 else 0.0


def first_kernel(
    own, core, zpair, gy, dg, partial, temp, salt, depth,
    new, cols, row_e, row_o, planes, depths, keep,
):
    odd_col = lax.axis_index("gx") % 2 == 1
    odd_row = lax.axis_index("gy") % 2 == 1

    def right(at, rows):
        return jnp.where(odd_col, zpair[at : at + rows, :], core[at : at + rows, :])

    def left(at, rows):
        return jnp.where(odd_col, core[at : at + rows, :], zpair[at : at + rows, :])

    forcing = []
    for p in range(4):
        parts = []
        for s in range(TILES):
            at = p * 64 + s * ROWS
            here = own[at : at + ROWS, :] + dg[at : at + ROWS, :]
            parts.append(here + right(at, ROWS) + gy[at : at + ROWS, :])
        forcing.append(jnp.concatenate(parts, 1))
    squared = forcing[3] * forcing[3]
    forcing[3] = squared / (1.0 + squared)
    for p in range(4):
        planes[p] = forcing[p]
    west, east = left(LIST_ROWS, ROWS), right(LIST_ROWS, ROWS)
    souths = [gy[LIST_ROWS + s * EDGE_ROWS : LIST_ROWS + (s + 1) * EDGE_ROWS, :] for s in range(TILES)]
    souths = jnp.concatenate(souths, 1)

    deep = depth[...].astype(F32)
    dry = jnp.zeros((1, 1), F32)
    last = 2 * LEVELS
    around = beside(deep, dry, souths[last : last + 1], west[:, 64 + last : 65 + last], east[:, last : last + 1])
    for n in range(4):
        depths[n] = around[n]
    lane = iota((ROWS, 128), 1)
    row = iota((8, COLS), 0)
    mixing = MIX_BASE + MIX_WIND * forcing[3]
    sides = ((0, west, 64, around[2], 0), (COLS - 128, east, 0, around[3], 127))
    block = jnp.zeros((ROWS, 128), F32)
    for t, field in enumerate((temp, salt)):
        across = None
        for l in range(LEVELS):
            at = t * LEVELS + l
            centre = field[l]
            change, across = column_change(
                centre, field[min(l + 1, LEVELS - 1)], mixing, deep, l, across
            )
            change = change + source(t, l, forcing, centre)
            new[t, l] = partial[t, l] + jnp.where(deep > l, change, 0.0)
            low = centre[8:16]
            here = (row == 7) & (around[1][8:16] > l) & (deep[8:16] > l)
            low = jnp.where(here, SIDE_RATE * (souths[at : at + 1] - low), 0.0)
            new[t, l, 8:16, :] += low
            for first, halo, offset, far, spot in sides:
                here = (lane == spot) & (far[:, first : first + 128] > l)
                here = here & (deep[:, first : first + 128] > l)
                near = halo[:, offset + at : offset + at + 1] - centre[:, first : first + 128]
                new[t, l, :, first : first + 128] += jnp.where(here, SIDE_RATE * near, 0.0)
            block = jnp.where(lane == at, new[t, l, :, 0:1], block)
            block = jnp.where(lane == 64 + at, new[t, l, :, COLS - 1 : COLS], block)
    cols[...] = block
    olds = (temp[:, 0, :], salt[:, 0, :])
    lows = (temp[:, ROWS - 1, :], salt[:, ROWS - 1, :])
    for t in range(2):
        span = slice(t * LEVELS, (t + 1) * LEVELS)
        first, final = new[t, :, 0, :], new[t, :, ROWS - 1, :]
        row_e[span, :] = jnp.where(odd_row, first, final)
        row_o[span, :] = jnp.where(odd_row, final, first)
        level = iota((LEVELS, COLS), 0)
        here = (souths[last : last + 1] > level) & (deep[ROWS - 1 : ROWS] > level)
        fix = jnp.where(here, SIDE_RATE * (lows[t] - souths[span]), 0.0)
        keep[span, :] = olds[t]
        keep[20 + t * LEVELS : 20 + (t + 1) * LEVELS, :] = fix
        for out in (row_e, row_o):
            out[20 + t * LEVELS : 20 + (t + 1) * LEVELS, :] = lows[t]
    keep[40:41, 0:128] = west[0:1]
    keep[41:42, 0:128] = east[0:1]
    for out in (row_e, row_o):
        out[40:41, :] = deep[ROWS - 1 : ROWS]
        out[41:42, 0:128] = west[ROWS - 1 : ROWS]
        out[42:43, 0:128] = east[ROWS - 1 : ROWS]


def inbound_list(blocks, names, panel, fold, mask, out):
    source_block = ocean_number((64, 64), 0)
    target = atm_number((64, 64), 0)
    chosen = dot(one_hot(source_block, names[0:1, :]), blocks, TN)
    kept = [[], [], [], []]
    for g in range(8):
        part = chosen[g * 8 : (g + 1) * 8]
        left = [part[:, c * 128 : (c + 1) * 128] for c in range(4)]
        piece = dot(
            jnp.concatenate(left, 0).astype(BF16), panel[g * 128 : (g + 1) * 128, :], NT
        )
        for c in range(4):
            kept[c].append(jnp.where(mask, piece[c * 8 : (c + 1) * 8], 0.0))
    kept = jnp.concatenate([jnp.concatenate(k, 0) for k in kept], 1)
    pieces = split_dot(kept, fold)
    out[...] = dot_split(one_hot(target, names[1:2, :]), pieces)


def inbound_fold():
    place, lane = iota((512, 128), 0), iota((512, 128), 1)
    fold = jnp.where((place // 128 == lane // 16) & (place % 16 == lane % 16), 1.0, 0.0)
    return fold.astype(BF16)


def second_kernel(
    old, core, zpair, xe, xo, planes, depths, keep, depth, table_hbm, panels,
    final, surface_blocks, to_gx, to_gy, to_dg, table, sem,
):
    copy = pltpu.make_async_copy(table_hbm, table, sem)
    copy.start()
    odd_col = lax.axis_index("gx") % 2 == 1
    odd_row = lax.axis_index("gy") % 2 == 1
    deep = depth[...].astype(F32)
    souths = jnp.where(odd_row, xo[...], xe[...])
    norths = jnp.where(odd_row, xe[...], xo[...])
    level = iota((2 * LEVELS, COLS), 0) % LEVELS
    here = (deep[0:1] > level) & (norths[40:41] > level)
    fix = jnp.where(here, SIDE_RATE * (norths[20:40] - keep[0:20, :]), 0.0)
    souths = souths[0:20] + keep[20:40, :]
    lane = iota((1, 128), 1)
    ends = []
    for halo, at, deepest in (
        (jnp.where(odd_col, core[...], zpair[...]), 0, 84),
        (jnp.where(odd_col, zpair[...], core[...]), 1, 20),
    ):
        mine, over = keep[40 + at : 41 + at, 0:128], norths[41 + at : 42 + at, 0:128]
        level = lane % 64 % LEVELS
        here = (mine[:, deepest : deepest + 1] > level) & (over[:, deepest : deepest + 1] > level)
        end_fix = jnp.where(here, SIDE_RATE * (over - mine), 0.0)
        ends.append(halo + jnp.where(iota((ROWS, 128), 0) == 0, end_fix, 0.0))
    west, east = ends
    row8, row = iota((8, COLS), 0), iota((ROWS, COLS), 0)
    around = [jnp.where(row == 0, norths[40:41], depths[0])] + [depths[n] for n in (1, 2, 3)]
    forcing = [planes[p] for p in range(4)]
    mixing = MIX_BASE + MIX_WIND * forcing[3]
    top = {}

    def whole(t, l):
        at = t * LEVELS + l
        high = old[t, l, 0:8, :] + jnp.where(row8 == 0, fix[at : at + 1], 0.0)
        return jnp.concatenate([high, old[t, l, 8:16, :]], 0)

    for t in range(2):
        across, centre = None, whole(t, 0)
        for l in range(LEVELS):
            at = t * LEVELS + l
            below = whole(t, l + 1) if l < LEVELS - 1 else None
            change, across = column_change(centre, below, mixing, deep, l, across)
            change = change + source(t, l, forcing, centre)
            nears = beside(
                centre,
                norths[at : at + 1],
                souths[at : at + 1],
                west[:, 64 + at : 65 + at],
                east[:, at : at + 1],
            )
            change = change + side_sum(centre, nears, [d > l for d in around])
            value = centre + jnp.where(deep > l, change, 0.0)
            final[t, l] = value
            if l < 3:
                top[t, l] = value
            centre = below
    wet_top = jnp.where(deep > 0, 1.0, 0.0)
    surface = (
        top[0, 0] * wet_top,
        top[1, 0] * wet_top,
        (top[0, 0] + top[0, 1] + top[0, 2]) / 3.0 * wet_top,
        wet_top,
    )
    parts = []
    for f in surface:
        parts.append(jnp.concatenate([f[:, s * 128 : (s + 1) * 128] for s in range(TILES)], 0))
    blocks = jnp.concatenate(parts, 1).astype(BF16)
    surface_blocks[...] = blocks
    mask, fold = group_mask(), inbound_fold()
    copy.wait()
    for n, out in ((3, to_dg), (2, to_gy), (1, to_gx)):
        inbound_list(blocks, table[n // 2, n % 2], panels.at[n], fold, mask, out)


def outer_kernel(final, blocks, table, panels, new_temp, new_salt, own, sems):
    copies = fetch(sems, [(final.at[0], new_temp), (final.at[1], new_salt)])
    inbound_list(blocks[...], table[0, 0], panels.at[0], inbound_fold(), group_mask(), own)
    for copy in copies:
        copy.wait()


def final_kernel(dg, gy, gx, own, out):
    total = own[...] + gx[...] + gy[...] + dg[...]
    group = iota((8, 128), 1) // 16
    for c in range(4):
        field = jnp.zeros((8, 128), F32)
        for k in range(8):
            moved = pltpu.roll(total[k * 8 : (k + 1) * 8], (k - c) % 8 * 16, 1)
            field = jnp.where(group == k, moved, field)
        out[c] = field


def call(kernel, shapes, args, scratch=(), hbm_in=(), hbm_out=(), mib=12):
    shapes = [s if isinstance(s, jax.ShapeDtypeStruct) else jax.ShapeDtypeStruct(s, F32) for s in shapes]
    return pl.pallas_call(
        kernel,
        out_shape=shapes,
        in_specs=[HBM if n in hbm_in else VMEM for n in range(len(args))],
        out_specs=[HBM if n in hbm_out else VMEM for n in range(len(shapes))],
        scratch_shapes=list(scratch),
        compiler_params=pltpu.CompilerParams(vmem_limit_bytes=mib * 1024 * 1024),
    )(*args)


def send(block, step):
    wide, high = lax.axis_size("gx"), lax.axis_size("gy")
    route = []
    for i in range(wide):
        for j in range(high):
            to = step(i, j)
            if 0 <= to[1] < high:
                route.append((i * high + j, to[0] % wide * high + to[1]))
    return lax.ppermute(block, ("gx", "gy"), route)


def pair(n):
    return n - 1 if n % 2 else n + 1


def other_pair(n):
    return n + 1 if n % 2 else n - 1


def per_device(air, out_tables, out_panels, depth, temp, salt, in_tables, in_panels):
    out_panels = out_panels.reshape(4, 1024, 128)
    in_panels = in_panels.reshape(4, 1024, 128)
    out_tables, in_tables = out_tables[0, 0], in_tables[0, 0]
    field = (2, LEVELS, ROWS, COLS)
    to_gx, to_gy, to_dg = call(
        outbound_kernel,
        [(LIST_ROWS + ROWS, 128), (LIST_ROWS + TILES * EDGE_ROWS, 128), (LIST_ROWS, 128)],
        [air, out_tables, out_panels, temp, salt, depth],
        [
            pltpu.VMEM(air.shape, BF16), pltpu.VMEM(out_tables.shape, jnp.int32),
            pltpu.VMEM((3, 1024, 128), BF16), pltpu.VMEM(temp.shape, F32),
            pltpu.VMEM(temp.shape, F32), pltpu.VMEM(depth.shape, jnp.int32),
            pltpu.SemaphoreType.DMA((8,)),
        ],
        hbm_in=range(6),
    )
    dg = send(to_dg, lambda i, j: (i - 1, j - 1))
    gy = send(to_gy, lambda i, j: (i, j - 1))
    zpair = send(to_gx, lambda i, j: (other_pair(i), j))
    core = send(to_gx, lambda i, j: (pair(i), j))
    own, partial = call(
        inner_kernel,
        [(LIST_ROWS, 128), field],
        [air, out_tables, out_panels, temp, salt, depth],
        [pltpu.VMEM((1024, 128), BF16), pltpu.SemaphoreType.DMA],
        hbm_in=(2,),
    )
    stepped, cols, row_e, row_o, planes, depths, keep = call(
        first_kernel,
        [field, (ROWS, 128), (48, COLS), (48, COLS), (4, ROWS, COLS), (4, ROWS, COLS), (48, COLS)],
        [own, core, zpair, gy, dg, partial, temp, salt, depth],
    )
    xo = send(row_o, lambda i, j: (i, other_pair(j)))
    xe = send(row_e, lambda i, j: (i, pair(j)))
    zpair = send(cols, lambda i, j: (other_pair(i), j))
    core = send(cols, lambda i, j: (pair(i), j))
    final, blocks, to_gx, to_gy, to_dg = call(
        second_kernel,
        [field, jax.ShapeDtypeStruct((64, COLS), BF16)] + [(64, 128)] * 3,
        [stepped, core, zpair, xe, xo, planes, depths, keep, depth, in_tables, in_panels],
        [pltpu.VMEM(in_tables.shape, jnp.int32), pltpu.SemaphoreType.DMA],
        hbm_in=(9,),
    )
    dg = send(to_dg, lambda i, j: (i + 1, j + 1))
    gy = send(to_gy, lambda i, j: (i, j + 1))
    gx = send(to_gx, lambda i, j: (i + 1, j))
    new_temp, new_salt, own = call(
        outer_kernel,
        [temp.shape, salt.shape, (64, 128)],
        [final, blocks, in_tables, in_panels],
        [pltpu.SemaphoreType.DMA((2,))],
        hbm_out=(0, 1),
    )
    (surface,) = call(final_kernel, [(4, 8, 128)], [dg, gy, gx, own])
    return new_temp, new_salt, surface


def solution(mesh):
    in_specs = (
        P(None, "gy", "gx"),
        P("gy", "gx", None, None, None, None),
        P("gy", "gx", None, None, None, None, None),
        P("gy", "gx"),
        P(None, "gy", "gx"),
        P(None, "gy", "gx"),
        P("gy", "gx", None, None, None, None),
        P("gy", "gx", None, None, None, None, None),
    )
    out_specs = (P(None, "gy", "gx"), P(None, "gy", "gx"), P(None, "gy", "gx"))
    return jax.shard_map(
        per_device, mesh=mesh, in_specs=in_specs, out_specs=out_specs, check_vma=False
    )
```

```python
import jax
import jax.numpy as jnp
from jax import lax
from jax.experimental import pallas as pl
from jax.experimental.pallas import tpu as pltpu
from jax.sharding import PartitionSpec as P

HEAT_RATE = 0.1
SHORTWAVE_RATE = 0.1
FRESH_RATE = 0.05
SIDE_RATE = 0.18
MIX_BASE = 0.03
MIX_WIND = 0.09
MIX_DECAY = 0.8

ROWS, COLS, LEVELS = 16, 512, 10
TILES = COLS // 128
F32, BF16 = jnp.float32, jnp.bfloat16
LIST_ROWS = 4 * 64
EDGE_ROWS = 24
VMEM = pl.BlockSpec(memory_space=pltpu.VMEM)
HBM = pl.BlockSpec(memory_space=pltpu.HBM)
NN = (((1,), (0,)), ((), ()))
TN = (((0,), (0,)), ((), ()))
NT = (((1,), (1,)), ((), ()))


def iota(shape, axis):
    return lax.broadcasted_iota(jnp.int32, shape, axis)


def dot(x, y, dims=NN):
    return lax.dot_general(x, y, dims, preferred_element_type=F32)


def dot_split(ones, values):
    high = values.astype(BF16)
    low = (values - high.astype(F32)).astype(BF16)
    return dot(ones, high) + dot(ones, low)


def split_dot(values, ones):
    high = values.astype(BF16)
    low = (values - high.astype(F32)).astype(BF16)
    return dot(high, ones) + dot(low, ones)


def ocean_number(shape, axis):
    place = iota(shape, axis)
    return place % ROWS * TILES + place // ROWS


def atm_number(shape, axis):
    place = iota(shape, axis)
    return place % 8 * 8 + place // 8


def one_hot(number, names):
    return jnp.where(number == names, 1.0, 0.0).astype(BF16)


def group_mask():
    return iota((8, 128), 1) // 16 == iota((8, 128), 0)


def edge_columns(levels):
    lane = iota((ROWS, 128), 1)
    block = jnp.zeros((ROWS, 128), F32)
    for at, values in enumerate(levels):
        block = jnp.where(lane == at, values[:, 0:1], block)
        block = jnp.where(lane == 64 + at, values[:, COLS - 1 : COLS], block)
    return block


def spread_air(air, mask):
    fold = (iota((128, 128), 0) % 16 == iota((128, 128), 1) % 16).astype(F32).astype(BF16)
    spread = []
    for c in range(8):
        for r in range(8):
            row = jnp.broadcast_to(air[c, r : r + 1, :].astype(F32), (8, 128))
            spread.append(jnp.where(mask, row, 0.0))
    tiled = dot(jnp.concatenate(spread, 0).astype(BF16), fold).astype(BF16)
    return jnp.concatenate([tiled[c * 64 : (c + 1) * 64] for c in range(8)], 1)


def outbound_list(tiled, names, panel, mask, out):
    source = iota((64, 64), 0)
    target = ocean_number((64, 64), 0)
    picked = dot(one_hot(source, names[0:1, :]), tiled, TN)
    planes = [[], [], [], []]
    for g in range(8):
        left = [
            jnp.where(mask, picked[g * 8 : (g + 1) * 8, c * 128 : (c + 1) * 128], 0.0)
            for c in range(8)
        ]
        piece = dot(jnp.concatenate(left, 0).astype(BF16), panel[g * 128 : (g + 1) * 128, :])
        f = [piece[c * 8 : (c + 1) * 8] for c in range(8)]
        planes[0].append(f[0] + f[1] + f[2])
        planes[1].append(f[3])
        planes[2].append(f[4] - f[5] + f[6])
        planes[3].append(f[7])
    pieces = jnp.concatenate([jnp.concatenate(p, 0) for p in planes], 1)
    summed = dot_split(one_hot(target, names[1:2, :]), pieces)
    for p in range(4):
        out[p * 64 : (p + 1) * 64, :] = summed[:, p * 128 : (p + 1) * 128]


def fetch(sems, pairs):
    copies = [pltpu.make_async_copy(src, dst, sems.at[n]) for n, (src, dst) in enumerate(pairs)]
    for copy in copies:
        copy.start()
    return copies


def outbound_kernel(
    air_hbm, table_hbm, panels_hbm, temp_hbm, salt_hbm, depth_hbm, to_gx,
    air, table, panels, temp, salt, depth, sems,
):
    pairs = [(air_hbm, air), (table_hbm, table)]
    pairs += [(panels_hbm.at[2 * n], panels.at[n]) for n in range(2)]
    pairs += [(temp_hbm, temp), (salt_hbm, salt), (depth_hbm, depth)]
    copies = fetch(sems, pairs)
    mask = group_mask()
    copies[0].wait()
    tiled = spread_air(air, mask)
    copies[1].wait()
    for n in range(2):
        copies[2 + n].wait()
        out = to_gx.at[n * LIST_ROWS : (n + 1) * LIST_ROWS]
        outbound_list(tiled, table[n, 0], panels.at[n], mask, out)
    for copy in copies[4:]:
        copy.wait()
    deep = depth[...].astype(F32)
    levels = [temp[l] for l in range(LEVELS)] + [salt[l] for l in range(LEVELS)] + [deep]
    to_gx[2 * LIST_ROWS :, :] = edge_columns(levels)


def beside(values, north, south, west, east):
    row, col = iota((ROWS, COLS), 0), iota((ROWS, COLS), 1)
    return (
        jnp.where(row == 0, north, pltpu.roll(values, 1, 0)),
        jnp.where(row == ROWS - 1, south, pltpu.roll(values, ROWS - 1, 0)),
        jnp.where(col == 0, west, pltpu.roll(values, 1, 1)),
        jnp.where(col == COLS - 1, east, pltpu.roll(values, COLS - 1, 1)),
    )


def side_sum(centre, nears, wets):
    side = jnp.zeros_like(centre)
    for near, there in zip(nears, wets):
        side = side + jnp.where(there, near - centre, 0.0)
    return SIDE_RATE * side


def inner_kernel(
    air, table, panels_hbm, temp, salt, depth, own, north, partial, panels, sems
):
    copies = fetch(sems, [(panels_hbm.at[2 * n + 1], panels.at[n]) for n in range(2)])
    deep = depth[...].astype(F32)
    dry = jnp.zeros((1, 1), F32)
    around = beside(deep, dry, dry, dry, dry)
    for l in range(LEVELS):
        wet = deep > l
        wets = [d > l for d in around]
        for t, field in enumerate((temp, salt)):
            centre = field[l]
            side = side_sum(centre, beside(centre, dry, dry, dry, dry), wets)
            partial[t, l] = centre + jnp.where(wet, side, 0.0)
    for base, edge in ((0, temp[:, 0, :]), (LEVELS, salt[:, 0, :]), (2 * LEVELS, deep[0:1])):
        for s in range(TILES):
            at = LIST_ROWS + s * EDGE_ROWS + base
            north[at : at + edge.shape[0], :] = edge[:, s * 128 : (s + 1) * 128]
    mask = group_mask()
    tiled = spread_air(air, mask)
    for n, out in ((0, north), (1, own)):
        copies[n].wait()
        outbound_list(tiled, table[n, 1], panels.at[n], mask, out)


def north_kernel(part, core, zpair, out):
    odd_col = lax.axis_index("gx") % 2 == 1
    out[0:LIST_ROWS, :] = part[0:LIST_ROWS, :] + jnp.where(
        odd_col, zpair[0:LIST_ROWS, :], core[0:LIST_ROWS, :]
    )
    out[LIST_ROWS:, :] = part[LIST_ROWS:, :]


def edge_kernel(own, core, zpair, partial, temp, salt, depth, base, west, east, depths, whole):
    odd_col = lax.axis_index("gx") % 2 == 1
    base[...] = own[...] + jnp.where(
        odd_col, zpair[LIST_ROWS : 2 * LIST_ROWS, :], core[LIST_ROWS : 2 * LIST_ROWS, :]
    )
    left = jnp.where(odd_col, core[2 * LIST_ROWS :, :], zpair[2 * LIST_ROWS :, :])
    right = jnp.where(odd_col, zpair[2 * LIST_ROWS :, :], core[2 * LIST_ROWS :, :])
    west[...] = left
    east[...] = right
    deep = depth[...].astype(F32)
    dry = jnp.zeros((1, 1), F32)
    last = 2 * LEVELS
    around = beside(deep, dry, dry, left[:, 64 + last : 65 + last], right[:, last : last + 1])
    for n in range(4):
        depths[n] = around[n]
    lane = iota((ROWS, 128), 1)
    sides = ((0, left, 64, around[2], 0), (COLS - 128, right, 0, around[3], 127))
    for t, field in enumerate((temp, salt)):
        for l in range(LEVELS):
            at = t * LEVELS + l
            whole[t, l] = partial[t, l]
            for first, halo, offset, far, spot in sides:
                here = (lane == spot) & (far[:, first : first + 128] > l)
                here = here & (deep[:, first : first + 128] > l)
                near = halo[:, offset + at : offset + at + 1] - field[l, :, first : first + 128]
                whole[t, l, :, first : first + 128] += jnp.where(here, SIDE_RATE * near, 0.0)


def column_change(values, below, mixing, depth, l, across):
    change = 0.0 if l == 0 else -across
    if l < LEVELS - 1:
        across = mixing * (MIX_DECAY**l) * (below - values)
        across = jnp.where(depth > l + 1, across, 0.0)
        change = change + across
    return change, across


def source(t, l, planes, values):
    if t == 0:
        heating = planes[1] * (SHORTWAVE_RATE * 2.718281828459045 ** (-0.5 * l))
        return heating + HEAT_RATE * planes[0] if l == 0 else heating
    return -FRESH_RATE * planes[2] * values if l == 0 else 0.0


def first_kernel(
    gy, base, west, east, side_depths, partial, temp, salt, depth,
    new, cols, row_e, row_o, planes, depths, keep,
):
    odd_row = lax.axis_index("gy") % 2 == 1
    forcing = []
    for p in range(4):
        parts = []
        for s in range(TILES):
            at = p * 64 + s * ROWS
            parts.append(base[at : at + ROWS, :] + gy[at : at + ROWS, :])
        forcing.append(jnp.concatenate(parts, 1))
    squared = forcing[3] * forcing[3]
    forcing[3] = squared / (1.0 + squared)
    for p in range(4):
        planes[p] = forcing[p]
    souths = [gy[LIST_ROWS + s * EDGE_ROWS : LIST_ROWS + (s + 1) * EDGE_ROWS, :] for s in range(TILES)]
    souths = jnp.concatenate(souths, 1)
    deep = depth[...].astype(F32)
    last = 2 * LEVELS
    south = jnp.where(
        iota((ROWS, COLS), 0) == ROWS - 1, souths[last : last + 1], side_depths[1]
    )
    for n in (0, 2, 3):
        depths[n] = side_depths[n]
    depths[1] = south
    lane = iota((ROWS, 128), 1)
    row = iota((8, COLS), 0)
    mixing = MIX_BASE + MIX_WIND * forcing[3]
    block = jnp.zeros((ROWS, 128), F32)
    for t, field in enumerate((temp, salt)):
        across = None
        for l in range(LEVELS):
            at = t * LEVELS + l
            centre = field[l]
            change, across = column_change(
                centre, field[min(l + 1, LEVELS - 1)], mixing, deep, l, across
            )
            change = change + source(t, l, forcing, centre)
            low = centre[8:16]
            here = (row == 7) & (south[8:16] > l)
            low = jnp.where(here, SIDE_RATE * (souths[at : at + 1] - low), 0.0)
            change = jnp.concatenate([change[0:8], change[8:16] + low], 0)
            value = partial[t, l] + jnp.where(deep > l, change, 0.0)
            new[t, l] = value
            block = jnp.where(lane == at, value[:, 0:1], block)
            block = jnp.where(lane == 64 + at, value[:, COLS - 1 : COLS], block)
    cols[...] = block
    olds = (temp[:, 0, :], salt[:, 0, :])
    lows = (temp[:, ROWS - 1, :], salt[:, ROWS - 1, :])
    for t in range(2):
        span = slice(t * LEVELS, (t + 1) * LEVELS)
        first, final = new[t, :, 0, :], new[t, :, ROWS - 1, :]
        row_e[span, :] = jnp.where(odd_row, first, final)
        row_o[span, :] = jnp.where(odd_row, final, first)
        level = iota((LEVELS, COLS), 0)
        here = (souths[last : last + 1] > level) & (deep[ROWS - 1 : ROWS] > level)
        fix = jnp.where(here, SIDE_RATE * (lows[t] - souths[span]), 0.0)
        keep[span, :] = olds[t]
        keep[20 + t * LEVELS : 20 + (t + 1) * LEVELS, :] = fix
        for out in (row_e, row_o):
            out[20 + t * LEVELS : 20 + (t + 1) * LEVELS, :] = lows[t]
    keep[40:41, 0:128] = west[0:1, :]
    keep[41:42, 0:128] = east[0:1, :]
    for out in (row_e, row_o):
        out[40:41, :] = deep[ROWS - 1 : ROWS]
        out[41:42, 0:128] = west[ROWS - 1 : ROWS, :]
        out[42:43, 0:128] = east[ROWS - 1 : ROWS, :]


def inbound_list(blocks, names, panel, fold, mask, out):
    source_block = ocean_number((64, 64), 0)
    target = atm_number((64, 64), 0)
    chosen = dot(one_hot(source_block, names[0:1, :]), blocks, TN)
    kept = [[], [], [], []]
    for g in range(8):
        part = chosen[g * 8 : (g + 1) * 8]
        left = [part[:, c * 128 : (c + 1) * 128] for c in range(4)]
        piece = dot(
            jnp.concatenate(left, 0).astype(BF16), panel[g * 128 : (g + 1) * 128, :], NT
        )
        for c in range(4):
            kept[c].append(jnp.where(mask, piece[c * 8 : (c + 1) * 8], 0.0))
    kept = jnp.concatenate([jnp.concatenate(k, 0) for k in kept], 1)
    pieces = split_dot(kept, fold)
    out[...] = dot_split(one_hot(target, names[1:2, :]), pieces)


def inbound_fold():
    place, lane = iota((512, 128), 0), iota((512, 128), 1)
    fold = jnp.where((place // 128 == lane // 16) & (place % 16 == lane % 16), 1.0, 0.0)
    return fold.astype(BF16)


def second_kernel(
    old, core, zpair, xe, xo, planes, depths, keep, depth, table_hbm, panels,
    final, surface_blocks, to_gx, table, sem,
):
    copy = pltpu.make_async_copy(table_hbm, table, sem)
    copy.start()
    odd_col = lax.axis_index("gx") % 2 == 1
    odd_row = lax.axis_index("gy") % 2 == 1
    deep = depth[...].astype(F32)
    souths = jnp.where(odd_row, xo[...], xe[...])
    norths = jnp.where(odd_row, xe[...], xo[...])
    level = iota((2 * LEVELS, COLS), 0) % LEVELS
    here = (deep[0:1] > level) & (norths[40:41] > level)
    fix = jnp.where(here, SIDE_RATE * (norths[20:40] - keep[0:20, :]), 0.0)
    souths = souths[0:20] + keep[20:40, :]
    lane = iota((1, 128), 1)
    ends = []
    for halo, at, deepest in (
        (jnp.where(odd_col, core[...], zpair[...]), 0, 84),
        (jnp.where(odd_col, zpair[...], core[...]), 1, 20),
    ):
        mine, over = keep[40 + at : 41 + at, 0:128], norths[41 + at : 42 + at, 0:128]
        level = lane % 64 % LEVELS
        here = (mine[:, deepest : deepest + 1] > level) & (over[:, deepest : deepest + 1] > level)
        end_fix = jnp.where(here, SIDE_RATE * (over - mine), 0.0)
        ends.append(halo + jnp.where(iota((ROWS, 128), 0) == 0, end_fix, 0.0))
    west, east = ends
    row8, row = iota((8, COLS), 0), iota((ROWS, COLS), 0)
    around = [jnp.where(row == 0, norths[40:41], depths[0])] + [depths[n] for n in (1, 2, 3)]
    forcing = [planes[p] for p in range(4)]
    mixing = MIX_BASE + MIX_WIND * forcing[3]
    top = {}

    def whole(t, l):
        at = t * LEVELS + l
        high = old[t, l, 0:8, :] + jnp.where(row8 == 0, fix[at : at + 1], 0.0)
        return jnp.concatenate([high, old[t, l, 8:16, :]], 0)

    for t in range(2):
        across, centre = None, whole(t, 0)
        for l in range(LEVELS):
            at = t * LEVELS + l
            below = whole(t, l + 1) if l < LEVELS - 1 else None
            change, across = column_change(centre, below, mixing, deep, l, across)
            change = change + source(t, l, forcing, centre)
            nears = beside(
                centre,
                norths[at : at + 1],
                souths[at : at + 1],
                west[:, 64 + at : 65 + at],
                east[:, at : at + 1],
            )
            change = change + side_sum(centre, nears, [d > l for d in around])
            value = centre + jnp.where(deep > l, change, 0.0)
            final[t, l] = value
            if l < 3:
                top[t, l] = value
            centre = below
    wet_top = jnp.where(deep > 0, 1.0, 0.0)
    surface = (
        top[0, 0] * wet_top,
        top[1, 0] * wet_top,
        (top[0, 0] + top[0, 1] + top[0, 2]) / 3.0 * wet_top,
        wet_top,
    )
    parts = []
    for f in surface:
        parts.append(jnp.concatenate([f[:, s * 128 : (s + 1) * 128] for s in range(TILES)], 0))
    blocks = jnp.concatenate(parts, 1).astype(BF16)
    surface_blocks[...] = blocks
    mask, fold = group_mask(), inbound_fold()
    copy.wait()
    for a in range(2):
        out = to_gx.at[a * 64 : (a + 1) * 64]
        inbound_list(blocks, table[a, 1], panels.at[2 * a + 1], fold, mask, out)


def outer_kernel(
    final, blocks, table_hbm, panels, new_temp, new_salt, own, south, table, sems
):
    pairs = [(table_hbm, table), (final.at[0], new_temp), (final.at[1], new_salt)]
    copies = fetch(sems, pairs)
    copies[0].wait()
    fold, mask = inbound_fold(), group_mask()
    for a, out in ((1, south), (0, own)):
        inbound_list(blocks[...], table[a, 0], panels.at[2 * a], fold, mask, out)
    for copy in copies[1:]:
        copy.wait()


def final_kernel(gy, gx, own, out):
    total = own[...] + gx[0:64, :] + gy[...]
    group = iota((8, 128), 1) // 16
    for c in range(4):
        field = jnp.zeros((8, 128), F32)
        for k in range(8):
            moved = pltpu.roll(total[k * 8 : (k + 1) * 8], (k - c) % 8 * 16, 1)
            field = jnp.where(group == k, moved, field)
        out[c] = field


def call(kernel, shapes, args, scratch=(), hbm_in=(), hbm_out=(), mib=12):
    args = [
        pltpu.with_memory_space_constraint(x, pltpu.HBM) if n in hbm_in else x
        for n, x in enumerate(args)
    ]
    shapes = [s if isinstance(s, jax.ShapeDtypeStruct) else jax.ShapeDtypeStruct(s, F32) for s in shapes]
    return pl.pallas_call(
        kernel,
        out_shape=shapes,
        in_specs=[HBM if n in hbm_in else VMEM for n in range(len(args))],
        out_specs=[HBM if n in hbm_out else VMEM for n in range(len(shapes))],
        scratch_shapes=list(scratch),
        compiler_params=pltpu.CompilerParams(vmem_limit_bytes=mib * 1024 * 1024),
    )(*args)


def send(block, step):
    wide, high = lax.axis_size("gx"), lax.axis_size("gy")
    route = []
    for i in range(wide):
        for j in range(high):
            to = step(i, j)
            if 0 <= to[1] < high:
                route.append((i * high + j, to[0] % wide * high + to[1]))
    return lax.ppermute(block, ("gx", "gy"), route)


def pair(n):
    return n - 1 if n % 2 else n + 1


def other_pair(n):
    return n + 1 if n % 2 else n - 1


def per_device(air, out_tables, out_panels, depth, temp, salt, in_tables, in_panels):
    out_panels = out_panels.reshape(4, 1024, 128)
    in_panels = in_panels.reshape(4, 1024, 128)
    out_tables, in_tables = out_tables[0, 0], in_tables[0, 0]
    field = (2, LEVELS, ROWS, COLS)
    (to_gx,) = call(
        outbound_kernel,
        [(2 * LIST_ROWS + ROWS, 128)],
        [air, out_tables, out_panels, temp, salt, depth],
        [
            pltpu.VMEM(air.shape, BF16), pltpu.VMEM(out_tables.shape, jnp.int32),
            pltpu.VMEM((2, 1024, 128), BF16), pltpu.VMEM(temp.shape, F32),
            pltpu.VMEM(temp.shape, F32), pltpu.VMEM(depth.shape, jnp.int32),
            pltpu.SemaphoreType.DMA((7,)),
        ],
        hbm_in=range(6),
    )
    zpair = send(to_gx, lambda i, j: (other_pair(i), j))
    core = send(to_gx, lambda i, j: (pair(i), j))
    own, north, partial = call(
        inner_kernel,
        [(LIST_ROWS, 128), (LIST_ROWS + TILES * EDGE_ROWS, 128), field],
        [air, out_tables, out_panels, temp, salt, depth],
        [pltpu.VMEM((2, 1024, 128), BF16), pltpu.SemaphoreType.DMA((2,))],
        hbm_in=(2,),
    )
    (to_gy,) = call(north_kernel, [north.shape], [north, core, zpair])
    gy = send(to_gy, lambda i, j: (i, j - 1))
    base, west, east, depths, partial = call(
        edge_kernel,
        [(LIST_ROWS, 128), (ROWS, 128), (ROWS, 128), (4, ROWS, COLS), field],
        [own, core, zpair, partial, temp, salt, depth],
    )
    stepped, cols, row_e, row_o, planes, depths, keep = call(
        first_kernel,
        [field, (ROWS, 128), (48, COLS), (48, COLS), (4, ROWS, COLS), (4, ROWS, COLS), (48, COLS)],
        [gy, base, west, east, depths, partial, temp, salt, depth],
    )
    xo = send(row_o, lambda i, j: (i, other_pair(j)))
    xe = send(row_e, lambda i, j: (i, pair(j)))
    zpair = send(cols, lambda i, j: (other_pair(i), j))
    core = send(cols, lambda i, j: (pair(i), j))
    final, blocks, to_gx = call(
        second_kernel,
        [field, jax.ShapeDtypeStruct((64, COLS), BF16), (128, 128)],
        [stepped, core, zpair, xe, xo, planes, depths, keep, depth, in_tables, in_panels],
        [pltpu.VMEM(in_tables.shape, jnp.int32), pltpu.SemaphoreType.DMA],
        hbm_in=(9,),
    )
    gx = send(to_gx, lambda i, j: (i + 1, j))
    new_temp, new_salt, own, south = call(
        outer_kernel,
        [temp.shape, salt.shape, (64, 128), (64, 128)],
        [final, blocks, in_tables, in_panels],
        [pltpu.VMEM(in_tables.shape, jnp.int32), pltpu.SemaphoreType.DMA((3,))],
        hbm_in=(2,),
        hbm_out=(0, 1),
    )
    gy = send(south + gx[64:128], lambda i, j: (i, j + 1))
    (surface,) = call(final_kernel, [(4, 8, 128)], [gy, gx, own])
    return new_temp, new_salt, surface


def solution(mesh):
    in_specs = (
        P(None, "gy", "gx"),
        P("gy", "gx", None, None, None, None),
        P("gy", "gx", None, None, None, None, None),
        P("gy", "gx"),
        P(None, "gy", "gx"),
        P(None, "gy", "gx"),
        P("gy", "gx", None, None, None, None),
        P("gy", "gx", None, None, None, None, None),
    )
    out_specs = (P(None, "gy", "gx"), P(None, "gy", "gx"), P(None, "gy", "gx"))
    return jax.shard_map(
        per_device, mesh=mesh, in_specs=in_specs, out_specs=out_specs, check_vma=False
    )
```

```python
import jax
import jax.numpy as jnp
from jax import lax
from jax.experimental import pallas as pl
from jax.experimental.pallas import tpu as pltpu
from jax.sharding import PartitionSpec as P

HEAT_RATE = 0.1
SHORTWAVE_RATE = 0.1
FRESH_RATE = 0.05
SIDE_RATE = 0.18
MIX_BASE = 0.03
MIX_WIND = 0.09
MIX_DECAY = 0.8

ROWS, COLS, LEVELS = 16, 512, 10
TILES = COLS // 128
F32, BF16 = jnp.float32, jnp.bfloat16
LIST_ROWS = 4 * 64
VMEM = pl.BlockSpec(memory_space=pltpu.VMEM)
HBM = pl.BlockSpec(memory_space=pltpu.HBM)
NN = (((1,), (0,)), ((), ()))
TN = (((0,), (0,)), ((), ()))
NT = (((1,), (1,)), ((), ()))


def iota(shape, axis):
    return lax.broadcasted_iota(jnp.int32, shape, axis)


def dot(x, y, dims=NN):
    return lax.dot_general(x, y, dims, preferred_element_type=F32)


def dot_split(ones, values):
    high = values.astype(BF16)
    low = (values - high.astype(F32)).astype(BF16)
    return dot(ones, high) + dot(ones, low)


def split_dot(values, ones):
    high = values.astype(BF16)
    low = (values - high.astype(F32)).astype(BF16)
    return dot(high, ones) + dot(low, ones)


def ocean_number(shape, axis):
    place = iota(shape, axis)
    return place % ROWS * TILES + place // ROWS


def atm_number(shape, axis):
    place = iota(shape, axis)
    return place % 8 * 8 + place // 8


def one_hot(number, names):
    return jnp.where(number == names, 1.0, 0.0).astype(BF16)


def group_mask():
    return iota((8, 128), 1) // 16 == iota((8, 128), 0)


def edge_columns(levels):
    lane = iota((ROWS, 128), 1)
    block = jnp.zeros((ROWS, 128), F32)
    for at, values in enumerate(levels):
        block = jnp.where(lane == at, values[:, 0:1], block)
        block = jnp.where(lane == 64 + at, values[:, COLS - 1 : COLS], block)
    return block


def spread_air(air, mask):
    fold = (iota((128, 128), 0) % 16 == iota((128, 128), 1) % 16).astype(F32).astype(BF16)
    spread = []
    for c in range(8):
        for r in range(8):
            row = jnp.broadcast_to(air[c, r : r + 1, :].astype(F32), (8, 128))
            spread.append(jnp.where(mask, row, 0.0))
    tiled = dot(jnp.concatenate(spread, 0).astype(BF16), fold).astype(BF16)
    return jnp.concatenate([tiled[c * 64 : (c + 1) * 64] for c in range(8)], 1)


def outbound_list(tiled, names, panel, mask, out):
    source = iota((64, 64), 0)
    target = ocean_number((64, 64), 0)
    picked = dot(one_hot(source, names[0:1, :]), tiled, TN)
    planes = [[], [], [], []]
    for g in range(8):
        left = [
            jnp.where(mask, picked[g * 8 : (g + 1) * 8, c * 128 : (c + 1) * 128], 0.0)
            for c in range(8)
        ]
        piece = dot(jnp.concatenate(left, 0).astype(BF16), panel[g * 128 : (g + 1) * 128, :])
        f = [piece[c * 8 : (c + 1) * 8] for c in range(8)]
        planes[0].append(f[0] + f[1] + f[2])
        planes[1].append(f[3])
        planes[2].append(f[4] - f[5] + f[6])
        planes[3].append(f[7])
    pieces = jnp.concatenate([jnp.concatenate(p, 0) for p in planes], 1)
    summed = dot_split(one_hot(target, names[1:2, :]), pieces)
    for p in range(4):
        out[p * 64 : (p + 1) * 64, :] = summed[:, p * 128 : (p + 1) * 128]


def fetch(sems, pairs):
    copies = [pltpu.make_async_copy(src, dst, sems.at[n]) for n, (src, dst) in enumerate(pairs)]
    for copy in copies:
        copy.start()
    return copies


def outbound_kernel(
    air_hbm, table_hbm, panels_hbm, temp_hbm, salt_hbm, depth_hbm,
    to_gx, tiled, table, panels, temp, salt, depth, air, panel, sems,
):
    pairs = [(air_hbm, air), (table_hbm, table), (panels_hbm.at[0], panel)]
    pairs += [(temp_hbm, temp), (salt_hbm, salt), (depth_hbm, depth)]
    copies = fetch(sems, pairs + [(panels_hbm.at[1:4], panels)])
    mask = group_mask()
    copies[0].wait()
    tiled[...] = spread_air(air, mask)
    copies[1].wait()
    copies[2].wait()
    outbound_list(tiled[...], table[0, 0], panel, mask, to_gx)
    for copy in copies[3:]:
        copy.wait()


def side_kernel(tiled, table, panels, temp, salt, depth, to_gx, north):
    mask = group_mask()
    deep = depth[...].astype(F32)
    levels = [temp[l] for l in range(LEVELS)] + [salt[l] for l in range(LEVELS)] + [deep]
    to_gx[LIST_ROWS:, :] = edge_columns(levels)
    outbound_list(tiled[...], table[1, 0], panels.at[1], mask, to_gx.at[0:LIST_ROWS])
    outbound_list(tiled[...], table[0, 1], panels.at[0], mask, north)


def beside(values, north, south, west, east):
    row, col = iota((ROWS, COLS), 0), iota((ROWS, COLS), 1)
    return (
        jnp.where(row == 0, north, pltpu.roll(values, 1, 0)),
        jnp.where(row == ROWS - 1, south, pltpu.roll(values, ROWS - 1, 0)),
        jnp.where(col == 0, west, pltpu.roll(values, 1, 1)),
        jnp.where(col == COLS - 1, east, pltpu.roll(values, COLS - 1, 1)),
    )


def side_sum(centre, nears, wets):
    side = jnp.zeros_like(centre)
    for near, there in zip(nears, wets):
        side = side + jnp.where(there, near - centre, 0.0)
    return SIDE_RATE * side


def inner_kernel(tiled, table, panels, temp, salt, depth, own, partial):
    deep = depth[...].astype(F32)
    dry = jnp.zeros((1, 1), F32)
    around = beside(deep, dry, dry, dry, dry)
    for l in range(LEVELS):
        wet = deep > l
        wets = [d > l for d in around]
        for t, field in enumerate((temp, salt)):
            centre = field[l]
            side = side_sum(centre, beside(centre, dry, dry, dry, dry), wets)
            partial[t, l] = centre + jnp.where(wet, side, 0.0)
    outbound_list(tiled[...], table[1, 1], panels.at[2], group_mask(), own)


def north_kernel(part, core, zpair, out):
    odd_col = lax.axis_index("gx") % 2 == 1
    out[...] = part[...] + jnp.where(odd_col, zpair[...], core[...])


def edge_kernel(own, core, zpair, partial, temp, salt, depth, base, west, east, depths, whole):
    odd_col = lax.axis_index("gx") % 2 == 1
    base[...] = own[...] + jnp.where(
        odd_col, zpair[0:LIST_ROWS, :], core[0:LIST_ROWS, :]
    )
    left = jnp.where(odd_col, core[LIST_ROWS:, :], zpair[LIST_ROWS:, :])
    right = jnp.where(odd_col, zpair[LIST_ROWS:, :], core[LIST_ROWS:, :])
    west[...] = left
    east[...] = right
    deep = depth[...].astype(F32)
    dry = jnp.zeros((1, 1), F32)
    last = 2 * LEVELS
    around = beside(deep, dry, dry, left[:, 64 + last : 65 + last], right[:, last : last + 1])
    for n in range(4):
        depths[n] = around[n]
    lane = iota((ROWS, 128), 1)
    sides = ((0, left, 64, around[2], 0), (COLS - 128, right, 0, around[3], 127))
    for t, field in enumerate((temp, salt)):
        for l in range(LEVELS):
            at = t * LEVELS + l
            whole[t, l] = partial[t, l]
            for first, halo, offset, far, spot in sides:
                here = (lane == spot) & (far[:, first : first + 128] > l)
                here = here & (deep[:, first : first + 128] > l)
                near = halo[:, offset + at : offset + at + 1] - field[l, :, first : first + 128]
                whole[t, l, :, first : first + 128] += jnp.where(here, SIDE_RATE * near, 0.0)


def column_change(values, below, mixing, depth, l, across):
    change = 0.0 if l == 0 else -across
    if l < LEVELS - 1:
        across = mixing * (MIX_DECAY**l) * (below - values)
        across = jnp.where(depth > l + 1, across, 0.0)
        change = change + across
    return change, across


def source(t, l, planes, values):
    if t == 0:
        heating = planes[1] * (SHORTWAVE_RATE * 2.718281828459045 ** (-0.5 * l))
        return heating + HEAT_RATE * planes[0] if l == 0 else heating
    return -FRESH_RATE * planes[2] * values if l == 0 else 0.0


def first_kernel(
    gy, base, west, east, partial, temp, salt, depth, new, cols, row_e, row_o, planes, keep
):
    odd_row = lax.axis_index("gy") % 2 == 1
    forcing = []
    for p in range(4):
        parts = []
        for s in range(TILES):
            at = p * 64 + s * ROWS
            parts.append(base[at : at + ROWS, :] + gy[at : at + ROWS, :])
        forcing.append(jnp.concatenate(parts, 1))
    squared = forcing[3] * forcing[3]
    forcing[3] = squared / (1.0 + squared)
    for p in range(4):
        planes[p] = forcing[p]
    deep = depth[...].astype(F32)
    lane = iota((ROWS, 128), 1)
    mixing = MIX_BASE + MIX_WIND * forcing[3]
    block = jnp.zeros((ROWS, 128), F32)
    for t, field in enumerate((temp, salt)):
        across = None
        for l in range(LEVELS):
            at = t * LEVELS + l
            centre = field[l]
            change, across = column_change(
                centre, field[min(l + 1, LEVELS - 1)], mixing, deep, l, across
            )
            change = change + source(t, l, forcing, centre)
            value = partial[t, l] + jnp.where(deep > l, change, 0.0)
            new[t, l] = value
            block = jnp.where(lane == at, value[:, 0:1], block)
            block = jnp.where(lane == 64 + at, value[:, COLS - 1 : COLS], block)
    cols[...] = block
    edges = []
    for r in (0, ROWS - 1):
        rows = [new[0, :, r, :], new[1, :, r, :], temp[:, r, :], salt[:, r, :], deep[r : r + 1]]
        edges.append(rows + [west[r : r + 1, :], east[r : r + 1, :]])
    for out, first in ((row_e, odd_row), (row_o, jnp.logical_not(odd_row))):
        at = 0
        for a, b in zip(*edges):
            out[at : at + a.shape[0], 0 : a.shape[1]] = jnp.where(first, a, b)
            at += a.shape[0]
    for n in range(2):
        keep[20 * n : 20 * n + 10, :] = edges[n][2]
        keep[20 * n + 10 : 20 * n + 20, :] = edges[n][3]
        keep[40 + 2 * n : 41 + 2 * n, 0:128] = edges[n][5]
        keep[41 + 2 * n : 42 + 2 * n, 0:128] = edges[n][6]


def inbound_list(blocks, names, panel, fold, mask, out):
    source_block = ocean_number((64, 64), 0)
    target = atm_number((64, 64), 0)
    chosen = dot(one_hot(source_block, names[0:1, :]), blocks, TN)
    kept = [[], [], [], []]
    for g in range(8):
        part = chosen[g * 8 : (g + 1) * 8]
        left = [part[:, c * 128 : (c + 1) * 128] for c in range(4)]
        piece = dot(
            jnp.concatenate(left, 0).astype(BF16), panel[g * 128 : (g + 1) * 128, :], NT
        )
        for c in range(4):
            kept[c].append(jnp.where(mask, piece[c * 8 : (c + 1) * 8], 0.0))
    kept = jnp.concatenate([jnp.concatenate(k, 0) for k in kept], 1)
    pieces = split_dot(kept, fold)
    out[...] = dot_split(one_hot(target, names[1:2, :]), pieces)


def inbound_fold():
    place, lane = iota((512, 128), 0), iota((512, 128), 1)
    fold = jnp.where((place // 128 == lane // 16) & (place % 16 == lane % 16), 1.0, 0.0)
    return fold.astype(BF16)


def second_kernel(
    old, core, zpair, xe, xo, planes, depths, keep, depth, table_hbm, panels,
    final, surface_blocks, to_gx, table, sem,
):
    copy = pltpu.make_async_copy(table_hbm, table, sem)
    copy.start()
    odd_col = lax.axis_index("gx") % 2 == 1
    odd_row = lax.axis_index("gy") % 2 == 1
    deep = depth[...].astype(F32)
    beyond = (jnp.where(odd_row, xe[...], xo[...]), jnp.where(odd_row, xo[...], xe[...]))
    level = iota((2 * LEVELS, COLS), 0) % LEVELS
    fixes, halo_rows = [], []
    for n, other in enumerate(beyond):
        r = n * (ROWS - 1)
        here = (deep[r : r + 1] > level) & (other[40:41] > level)
        fix = jnp.where(here, SIDE_RATE * (other[20:40] - keep[20 * n : 20 * n + 20, :]), 0.0)
        fixes.append(fix)
        halo_rows.append(other[0:20] - fix)
    norths, souths = halo_rows
    level = iota((1, 128), 1) % 64 % LEVELS
    row = iota((ROWS, 128), 0)
    ends = []
    for halo, at, deepest in (
        (jnp.where(odd_col, core[...], zpair[...]), 0, 84),
        (jnp.where(odd_col, zpair[...], core[...]), 1, 20),
    ):
        for n, other in enumerate(beyond):
            mine = keep[40 + 2 * n + at : 41 + 2 * n + at, 0:128]
            far = other[41 + at : 42 + at, 0:128]
            here = mine[:, deepest : deepest + 1] > level
            here = here & (far[:, deepest : deepest + 1] > level)
            fix = jnp.where(here, SIDE_RATE * (far - mine), 0.0)
            halo = halo + jnp.where(row == n * (ROWS - 1), fix, 0.0)
        ends.append(halo)
    west, east = ends
    row8, row = iota((8, COLS), 0), iota((ROWS, COLS), 0)
    around = [depths[n] for n in range(4)]
    around[0] = jnp.where(row == 0, beyond[0][40:41], around[0])
    around[1] = jnp.where(row == ROWS - 1, beyond[1][40:41], around[1])
    forcing = [planes[p] for p in range(4)]
    mixing = MIX_BASE + MIX_WIND * forcing[3]
    top = {}

    def whole(t, l):
        at = t * LEVELS + l
        high = old[t, l, 0:8, :] + jnp.where(row8 == 0, fixes[0][at : at + 1], 0.0)
        low = old[t, l, 8:16, :] + jnp.where(row8 == 7, fixes[1][at : at + 1], 0.0)
        return jnp.concatenate([high, low], 0)

    for t in range(2):
        across, centre = None, whole(t, 0)
        for l in range(LEVELS):
            at = t * LEVELS + l
            below = whole(t, l + 1) if l < LEVELS - 1 else None
            change, across = column_change(centre, below, mixing, deep, l, across)
            change = change + source(t, l, forcing, centre)
            nears = beside(
                centre,
                norths[at : at + 1],
                souths[at : at + 1],
                west[:, 64 + at : 65 + at],
                east[:, at : at + 1],
            )
            change = change + side_sum(centre, nears, [d > l for d in around])
            value = centre + jnp.where(deep > l, change, 0.0)
            final[t, l] = value
            if l < 3:
                top[t, l] = value
            centre = below
    wet_top = jnp.where(deep > 0, 1.0, 0.0)
    surface = (
        top[0, 0] * wet_top,
        top[1, 0] * wet_top,
        (top[0, 0] + top[0, 1] + top[0, 2]) / 3.0 * wet_top,
        wet_top,
    )
    parts = []
    for f in surface:
        parts.append(jnp.concatenate([f[:, s * 128 : (s + 1) * 128] for s in range(TILES)], 0))
    blocks = jnp.concatenate(parts, 1).astype(BF16)
    surface_blocks[...] = blocks
    mask, fold = group_mask(), inbound_fold()
    copy.wait()
    for a in range(2):
        out = to_gx.at[a * 64 : (a + 1) * 64]
        inbound_list(blocks, table[a, 1], panels.at[2 * a + 1], fold, mask, out)


def outer_kernel(
    final, blocks, table_hbm, panels, new_temp, new_salt, own, south, table, sems
):
    pairs = [(table_hbm, table), (final.at[0], new_temp), (final.at[1], new_salt)]
    copies = fetch(sems, pairs)
    copies[0].wait()
    fold, mask = inbound_fold(), group_mask()
    for a, out in ((1, south), (0, own)):
        inbound_list(blocks[...], table[a, 0], panels.at[2 * a], fold, mask, out)
    for copy in copies[1:]:
        copy.wait()


def final_kernel(gy, gx, own, out):
    total = own[...] + gx[0:64, :] + gy[...]
    group = iota((8, 128), 1) // 16
    for c in range(4):
        field = jnp.zeros((8, 128), F32)
        for k in range(8):
            moved = pltpu.roll(total[k * 8 : (k + 1) * 8], (k - c) % 8 * 16, 1)
            field = jnp.where(group == k, moved, field)
        out[c] = field


def call(kernel, shapes, args, scratch=(), hbm_in=(), hbm_out=(), mib=12):
    args = [
        pltpu.with_memory_space_constraint(x, pltpu.HBM) if n in hbm_in else x
        for n, x in enumerate(args)
    ]
    shapes = [s if isinstance(s, jax.ShapeDtypeStruct) else jax.ShapeDtypeStruct(s, F32) for s in shapes]
    return pl.pallas_call(
        kernel,
        out_shape=shapes,
        in_specs=[HBM if n in hbm_in else VMEM for n in range(len(args))],
        out_specs=[HBM if n in hbm_out else VMEM for n in range(len(shapes))],
        scratch_shapes=list(scratch),
        compiler_params=pltpu.CompilerParams(vmem_limit_bytes=mib * 1024 * 1024),
    )(*args)


def send(block, step):
    wide, high = lax.axis_size("gx"), lax.axis_size("gy")
    route = []
    for i in range(wide):
        for j in range(high):
            to = step(i, j)
            if 0 <= to[1] < high:
                route.append((i * high + j, to[0] % wide * high + to[1]))
    return lax.ppermute(block, ("gx", "gy"), route)


def pair(n):
    return n - 1 if n % 2 else n + 1


def other_pair(n):
    return n + 1 if n % 2 else n - 1


def per_device(air, out_tables, out_panels, depth, temp, salt, in_tables, in_panels):
    out_panels = out_panels.reshape(4, 1024, 128)
    in_panels = in_panels.reshape(4, 1024, 128)
    out_tables, in_tables = out_tables[0, 0], in_tables[0, 0]
    field = (2, LEVELS, ROWS, COLS)
    to_gx, tiled, out_tables, out_panels, temp, salt, depth = call(
        outbound_kernel,
        [
            (LIST_ROWS, 128),
            jax.ShapeDtypeStruct((64, 1024), BF16),
            jax.ShapeDtypeStruct(out_tables.shape, jnp.int32),
            jax.ShapeDtypeStruct((3, 1024, 128), BF16),
            temp.shape,
            salt.shape,
            jax.ShapeDtypeStruct(depth.shape, jnp.int32),
        ],
        [air, out_tables, out_panels, temp, salt, depth],
        [
            pltpu.VMEM(air.shape, BF16),
            pltpu.VMEM((1024, 128), BF16),
            pltpu.SemaphoreType.DMA((7,)),
        ],
        hbm_in=range(6),
    )
    zpair = send(to_gx, lambda i, j: (other_pair(i), j))
    core = send(to_gx, lambda i, j: (pair(i), j))
    to_side, north = call(
        side_kernel,
        [(LIST_ROWS + ROWS, 128), (LIST_ROWS, 128)],
        [tiled, out_tables, out_panels, temp, salt, depth],
    )
    side_z = send(to_side, lambda i, j: (other_pair(i), j))
    side_core = send(to_side, lambda i, j: (pair(i), j))
    (to_gy,) = call(north_kernel, [north.shape], [north, core, zpair])
    gy = send(to_gy, lambda i, j: (i, j - 1))
    own, partial = call(
        inner_kernel,
        [(LIST_ROWS, 128), field],
        [tiled, out_tables, out_panels, temp, salt, depth],
    )
    base, west, east, depths, partial = call(
        edge_kernel,
        [(LIST_ROWS, 128), (ROWS, 128), (ROWS, 128), (4, ROWS, COLS), field],
        [own, side_core, side_z, partial, temp, salt, depth],
    )
    stepped, cols, row_e, row_o, planes, keep = call(
        first_kernel,
        [field, (ROWS, 128), (43, COLS), (43, COLS), (4, ROWS, COLS), (44, COLS)],
        [gy, base, west, east, partial, temp, salt, depth],
    )
    xo = send(row_o, lambda i, j: (i, other_pair(j)))
    xe = send(row_e, lambda i, j: (i, pair(j)))
    zpair = send(cols, lambda i, j: (other_pair(i), j))
    core = send(cols, lambda i, j: (pair(i), j))
    final, blocks, to_gx = call(
        second_kernel,
        [field, jax.ShapeDtypeStruct((64, COLS), BF16), (128, 128)],
        [stepped, core, zpair, xe, xo, planes, depths, keep, depth, in_tables, in_panels],
        [pltpu.VMEM(in_tables.shape, jnp.int32), pltpu.SemaphoreType.DMA],
        hbm_in=(9,),
    )
    gx = send(to_gx, lambda i, j: (i + 1, j))
    new_temp, new_salt, own, south = call(
        outer_kernel,
        [temp.shape, salt.shape, (64, 128), (64, 128)],
        [final, blocks, in_tables, in_panels],
        [pltpu.VMEM(in_tables.shape, jnp.int32), pltpu.SemaphoreType.DMA((3,))],
        hbm_in=(2,),
        hbm_out=(0, 1),
    )
    gy = send(south + gx[64:128], lambda i, j: (i, j + 1))
    (surface,) = call(final_kernel, [(4, 8, 128)], [gy, gx, own])
    return new_temp, new_salt, surface


def solution(mesh):
    in_specs = (
        P(None, "gy", "gx"),
        P("gy", "gx", None, None, None, None),
        P("gy", "gx", None, None, None, None, None),
        P("gy", "gx"),
        P(None, "gy", "gx"),
        P(None, "gy", "gx"),
        P("gy", "gx", None, None, None, None),
        P("gy", "gx", None, None, None, None, None),
    )
    out_specs = (P(None, "gy", "gx"), P(None, "gy", "gx"), P(None, "gy", "gx"))
    return jax.shard_map(
        per_device, mesh=mesh, in_specs=in_specs, out_specs=out_specs, check_vma=False
    )
```

```python
import jax
import jax.numpy as jnp
from jax import lax
from jax.experimental import pallas as pl
from jax.experimental.pallas import tpu as pltpu
from jax.sharding import PartitionSpec as P

HEAT_RATE = 0.1
SHORTWAVE_RATE = 0.1
FRESH_RATE = 0.05
SIDE_RATE = 0.18
MIX_BASE = 0.03
MIX_WIND = 0.09
MIX_DECAY = 0.8

ROWS, COLS, LEVELS = 16, 512, 10
TILES = COLS // 128
F32, BF16 = jnp.float32, jnp.bfloat16
LIST_ROWS = 4 * 64
VMEM = pl.BlockSpec(memory_space=pltpu.VMEM)
HBM = pl.BlockSpec(memory_space=pltpu.HBM)
NN = (((1,), (0,)), ((), ()))
TN = (((0,), (0,)), ((), ()))
NT = (((1,), (1,)), ((), ()))


def iota(shape, axis):
    return lax.broadcasted_iota(jnp.int32, shape, axis)


def dot(x, y, dims=NN):
    return lax.dot_general(x, y, dims, preferred_element_type=F32)


def dot_split(ones, values):
    high = values.astype(BF16)
    low = (values - high.astype(F32)).astype(BF16)
    return dot(ones, high) + dot(ones, low)


def split_dot(values, ones):
    high = values.astype(BF16)
    low = (values - high.astype(F32)).astype(BF16)
    return dot(high, ones) + dot(low, ones)


def ocean_number(shape, axis):
    place = iota(shape, axis)
    return place % ROWS * TILES + place // ROWS


def atm_number(shape, axis):
    place = iota(shape, axis)
    return place % 8 * 8 + place // 8


def one_hot(number, names):
    return jnp.where(number == names, 1.0, 0.0).astype(BF16)


def group_mask():
    return iota((8, 128), 1) // 16 == iota((8, 128), 0)


def edge_columns(levels):
    lane = iota((ROWS, 128), 1)
    block = jnp.zeros((ROWS, 128), F32)
    for at, values in enumerate(levels):
        block = jnp.where(lane == at, values[:, 0:1], block)
        block = jnp.where(lane == 64 + at, values[:, COLS - 1 : COLS], block)
    return block


def spread_air(air, mask):
    fold = (iota((128, 128), 0) % 16 == iota((128, 128), 1) % 16).astype(F32).astype(BF16)
    spread = []
    for c in range(8):
        for r in range(8):
            row = jnp.broadcast_to(air[c, r : r + 1, :].astype(F32), (8, 128))
            spread.append(jnp.where(mask, row, 0.0))
    tiled = dot(jnp.concatenate(spread, 0).astype(BF16), fold).astype(BF16)
    return jnp.concatenate([tiled[c * 64 : (c + 1) * 64] for c in range(8)], 1)


def outbound_list(tiled, names, panel, mask, out):
    source = iota((64, 64), 0)
    target = ocean_number((64, 64), 0)
    picked = dot(one_hot(source, names[0:1, :]), tiled, TN)
    planes = [[], [], [], []]
    for g in range(8):
        left = [
            jnp.where(mask, picked[g * 8 : (g + 1) * 8, c * 128 : (c + 1) * 128], 0.0)
            for c in range(8)
        ]
        piece = dot(jnp.concatenate(left, 0).astype(BF16), panel[g * 128 : (g + 1) * 128, :])
        f = [piece[c * 8 : (c + 1) * 8] for c in range(8)]
        planes[0].append(f[0] + f[1] + f[2])
        planes[1].append(f[3])
        planes[2].append(f[4] - f[5] + f[6])
        planes[3].append(f[7])
    pieces = jnp.concatenate([jnp.concatenate(p, 0) for p in planes], 1)
    summed = dot_split(one_hot(target, names[1:2, :]), pieces)
    for p in range(4):
        out[p * 64 : (p + 1) * 64, :] = summed[:, p * 128 : (p + 1) * 128]


def fetch(sems, pairs):
    copies = [pltpu.make_async_copy(src, dst, sems.at[n]) for n, (src, dst) in enumerate(pairs)]
    for copy in copies:
        copy.start()
    return copies


def outbound_kernel(
    air_hbm, table_hbm, panels_hbm, temp_hbm, salt_hbm, depth_hbm,
    to_gx, tiled, table, panels, temp, salt, depth, air, panel, sems,
):
    pairs = [(air_hbm, air), (table_hbm, table), (panels_hbm.at[0], panel)]
    pairs += [(temp_hbm, temp), (salt_hbm, salt), (depth_hbm, depth)]
    copies = fetch(sems, pairs + [(panels_hbm.at[1:4], panels)])
    mask = group_mask()
    copies[0].wait()
    tiled[...] = spread_air(air, mask)
    copies[1].wait()
    copies[2].wait()
    outbound_list(tiled[...], table[0, 0], panel, mask, to_gx)
    for copy in copies[3:]:
        copy.wait()


def side_kernel(tiled, table, panels, temp, salt, depth, to_gx, north):
    mask = group_mask()
    deep = depth[...].astype(F32)
    levels = [temp[l] for l in range(LEVELS)] + [salt[l] for l in range(LEVELS)] + [deep]
    to_gx[LIST_ROWS:, :] = edge_columns(levels)
    outbound_list(tiled[...], table[1, 0], panels.at[1], mask, to_gx.at[0:LIST_ROWS])
    outbound_list(tiled[...], table[0, 1], panels.at[0], mask, north)


def beside(values, north, south, west, east):
    row, col = iota((ROWS, COLS), 0), iota((ROWS, COLS), 1)
    return (
        jnp.where(row == 0, north, pltpu.roll(values, 1, 0)),
        jnp.where(row == ROWS - 1, south, pltpu.roll(values, ROWS - 1, 0)),
        jnp.where(col == 0, west, pltpu.roll(values, 1, 1)),
        jnp.where(col == COLS - 1, east, pltpu.roll(values, COLS - 1, 1)),
    )


def side_sum(centre, nears, wets):
    side = jnp.zeros_like(centre)
    for near, there in zip(nears, wets):
        side = side + jnp.where(there, near - centre, 0.0)
    return SIDE_RATE * side


def inner_kernel(tiled, table, panels, temp, salt, depth, own, partial):
    deep = depth[...].astype(F32)
    dry = jnp.zeros((1, 1), F32)
    around = beside(deep, dry, dry, dry, dry)
    for l in range(LEVELS):
        wet = deep > l
        wets = [d > l for d in around]
        for t, field in enumerate((temp, salt)):
            centre = field[l]
            side = side_sum(centre, beside(centre, dry, dry, dry, dry), wets)
            partial[t, l] = centre + jnp.where(wet, side, 0.0)
    outbound_list(tiled[...], table[1, 1], panels.at[2], group_mask(), own)


def north_kernel(part, core, zpair, out):
    odd_col = lax.axis_index("gx") % 2 == 1
    out[...] = part[...] + jnp.where(odd_col, zpair[...], core[...])


def edge_kernel(own, core, zpair, partial, temp, salt, depth, base, west, east, depths, whole):
    odd_col = lax.axis_index("gx") % 2 == 1
    base[...] = own[...] + jnp.where(
        odd_col, zpair[0:LIST_ROWS, :], core[0:LIST_ROWS, :]
    )
    left = jnp.where(odd_col, core[LIST_ROWS:, :], zpair[LIST_ROWS:, :])
    right = jnp.where(odd_col, zpair[LIST_ROWS:, :], core[LIST_ROWS:, :])
    west[...] = left
    east[...] = right
    deep = depth[...].astype(F32)
    dry = jnp.zeros((1, 1), F32)
    last = 2 * LEVELS
    around = beside(deep, dry, dry, left[:, 64 + last : 65 + last], right[:, last : last + 1])
    for n in range(4):
        depths[n] = around[n]
    lane = iota((ROWS, 128), 1)
    sides = ((0, left, 64, around[2], 0), (COLS - 128, right, 0, around[3], 127))
    for t, field in enumerate((temp, salt)):
        for l in range(LEVELS):
            at = t * LEVELS + l
            whole[t, l] = partial[t, l]
            for first, halo, offset, far, spot in sides:
                here = (lane == spot) & (far[:, first : first + 128] > l)
                here = here & (deep[:, first : first + 128] > l)
                near = halo[:, offset + at : offset + at + 1] - field[l, :, first : first + 128]
                whole[t, l, :, first : first + 128] += jnp.where(here, SIDE_RATE * near, 0.0)


def column_change(values, below, mixing, depth, l, across):
    change = 0.0 if l == 0 else -across
    if l < LEVELS - 1:
        across = mixing * (MIX_DECAY**l) * (below - values)
        across = jnp.where(depth > l + 1, across, 0.0)
        change = change + across
    return change, across


def source(t, l, planes, values):
    if t == 0:
        heating = planes[1] * (SHORTWAVE_RATE * 2.718281828459045 ** (-0.5 * l))
        return heating + HEAT_RATE * planes[0] if l == 0 else heating
    return -FRESH_RATE * planes[2] * values if l == 0 else 0.0


def first_kernel(
    gy, base, west, east, partial, temp, salt, depth, new, cols, row_e, row_o, planes, keep
):
    odd_row = lax.axis_index("gy") % 2 == 1
    forcing = []
    for p in range(4):
        parts = []
        for s in range(TILES):
            at = p * 64 + s * ROWS
            parts.append(base[at : at + ROWS, :] + gy[at : at + ROWS, :])
        forcing.append(jnp.concatenate(parts, 1))
    squared = forcing[3] * forcing[3]
    forcing[3] = squared / (1.0 + squared)
    for p in range(4):
        planes[p] = forcing[p]
    deep = depth[...].astype(F32)
    lane = iota((ROWS, 128), 1)
    mixing = MIX_BASE + MIX_WIND * forcing[3]
    block = jnp.zeros((ROWS, 128), F32)
    for t, field in enumerate((temp, salt)):
        across = None
        for l in range(LEVELS):
            at = t * LEVELS + l
            centre = field[l]
            change, across = column_change(
                centre, field[min(l + 1, LEVELS - 1)], mixing, deep, l, across
            )
            change = change + source(t, l, forcing, centre)
            value = partial[t, l] + jnp.where(deep > l, change, 0.0)
            new[t, l] = value
            block = jnp.where(lane == at, value[:, 0:1], block)
            block = jnp.where(lane == 64 + at, value[:, COLS - 1 : COLS], block)
    cols[...] = block
    edges = []
    for r in (0, ROWS - 1):
        rows = [new[0, :, r, :], new[1, :, r, :], temp[:, r, :], salt[:, r, :], deep[r : r + 1]]
        edges.append(rows + [west[r : r + 1, :], east[r : r + 1, :]])
    for out, first in ((row_e, odd_row), (row_o, jnp.logical_not(odd_row))):
        at = 0
        for a, b in zip(*edges):
            out[at : at + a.shape[0], 0 : a.shape[1]] = jnp.where(first, a, b)
            at += a.shape[0]
    for n in range(2):
        keep[20 * n : 20 * n + 10, :] = edges[n][2]
        keep[20 * n + 10 : 20 * n + 20, :] = edges[n][3]
        keep[40 + 2 * n : 41 + 2 * n, 0:128] = edges[n][5]
        keep[41 + 2 * n : 42 + 2 * n, 0:128] = edges[n][6]


def inbound_list(blocks, names, panel, fold, mask, out):
    source_block = ocean_number((64, 64), 0)
    target = atm_number((64, 64), 0)
    chosen = dot(one_hot(source_block, names[0:1, :]), blocks, TN)
    kept = [[], [], [], []]
    for g in range(8):
        part = chosen[g * 8 : (g + 1) * 8]
        left = [part[:, c * 128 : (c + 1) * 128] for c in range(4)]
        piece = dot(
            jnp.concatenate(left, 0).astype(BF16), panel[g * 128 : (g + 1) * 128, :], NT
        )
        for c in range(4):
            kept[c].append(jnp.where(mask, piece[c * 8 : (c + 1) * 8], 0.0))
    kept = jnp.concatenate([jnp.concatenate(k, 0) for k in kept], 1)
    pieces = split_dot(kept, fold)
    out[...] = dot_split(one_hot(target, names[1:2, :]), pieces)


def inbound_fold():
    place, lane = iota((512, 128), 0), iota((512, 128), 1)
    fold = jnp.where((place // 128 == lane // 16) & (place % 16 == lane % 16), 1.0, 0.0)
    return fold.astype(BF16)


def second_kernel(
    old, core, zpair, xe, xo, planes, depths, keep, depth, table_hbm, panels,
    final, surface_blocks, to_gx, table, sem,
):
    copy = pltpu.make_async_copy(table_hbm, table, sem)
    copy.start()
    odd_col = lax.axis_index("gx") % 2 == 1
    odd_row = lax.axis_index("gy") % 2 == 1
    deep = depth[...].astype(F32)
    beyond = (jnp.where(odd_row, xe[...], xo[...]), jnp.where(odd_row, xo[...], xe[...]))
    level = iota((2 * LEVELS, COLS), 0) % LEVELS
    at_end = (lax.axis_index("gy") == 0, lax.axis_index("gy") == lax.axis_size("gy") - 1)
    beyond_deep = [jnp.where(end, 0.0, other[40:41]) for end, other in zip(at_end, beyond)]
    fixes, halo_rows = [], []
    for n, other in enumerate(beyond):
        r = n * (ROWS - 1)
        here = (deep[r : r + 1] > level) & (beyond_deep[n] > level)
        fix = jnp.where(here, SIDE_RATE * (other[20:40] - keep[20 * n : 20 * n + 20, :]), 0.0)
        fixes.append(fix)
        halo_rows.append(other[0:20] - fix)
    norths, souths = halo_rows
    level = iota((1, 128), 1) % 64 % LEVELS
    row = iota((ROWS, 128), 0)
    ends = []
    for halo, at, deepest in (
        (jnp.where(odd_col, core[...], zpair[...]), 0, 84),
        (jnp.where(odd_col, zpair[...], core[...]), 1, 20),
    ):
        for n, other in enumerate(beyond):
            mine = keep[40 + 2 * n + at : 41 + 2 * n + at, 0:128]
            far = other[41 + at : 42 + at, 0:128]
            here = mine[:, deepest : deepest + 1] > level
            here = here & (jnp.where(at_end[n], 0.0, far[:, deepest : deepest + 1]) > level)
            fix = jnp.where(here, SIDE_RATE * (far - mine), 0.0)
            halo = halo + jnp.where(row == n * (ROWS - 1), fix, 0.0)
        ends.append(halo)
    west, east = ends
    row8, row = iota((8, COLS), 0), iota((ROWS, COLS), 0)
    around = [depths[n] for n in range(4)]
    around[0] = jnp.where(row == 0, beyond_deep[0], around[0])
    around[1] = jnp.where(row == ROWS - 1, beyond_deep[1], around[1])
    forcing = [planes[p] for p in range(4)]
    mixing = MIX_BASE + MIX_WIND * forcing[3]
    top = {}

    def whole(t, l):
        at = t * LEVELS + l
        high = old[t, l, 0:8, :] + jnp.where(row8 == 0, fixes[0][at : at + 1], 0.0)
        low = old[t, l, 8:16, :] + jnp.where(row8 == 7, fixes[1][at : at + 1], 0.0)
        return jnp.concatenate([high, low], 0)

    for t in range(2):
        across, centre = None, whole(t, 0)
        for l in range(LEVELS):
            at = t * LEVELS + l
            below = whole(t, l + 1) if l < LEVELS - 1 else None
            change, across = column_change(centre, below, mixing, deep, l, across)
            change = change + source(t, l, forcing, centre)
            nears = beside(
                centre,
                norths[at : at + 1],
                souths[at : at + 1],
                west[:, 64 + at : 65 + at],
                east[:, at : at + 1],
            )
            change = change + side_sum(centre, nears, [d > l for d in around])
            value = centre + jnp.where(deep > l, change, 0.0)
            final[t, l] = value
            if l < 3:
                top[t, l] = value
            centre = below
    wet_top = jnp.where(deep > 0, 1.0, 0.0)
    surface = (
        top[0, 0] * wet_top,
        top[1, 0] * wet_top,
        (top[0, 0] + top[0, 1] + top[0, 2]) / 3.0 * wet_top,
        wet_top,
    )
    parts = []
    for f in surface:
        parts.append(jnp.concatenate([f[:, s * 128 : (s + 1) * 128] for s in range(TILES)], 0))
    blocks = jnp.concatenate(parts, 1).astype(BF16)
    surface_blocks[...] = blocks
    mask, fold = group_mask(), inbound_fold()
    copy.wait()
    for a in range(2):
        out = to_gx.at[a * 64 : (a + 1) * 64]
        inbound_list(blocks, table[a, 1], panels.at[2 * a + 1], fold, mask, out)


def outer_kernel(
    final, blocks, table_hbm, panels, new_temp, new_salt, own, south, table, sems
):
    pairs = [(table_hbm, table), (final.at[0], new_temp), (final.at[1], new_salt)]
    copies = fetch(sems, pairs)
    copies[0].wait()
    fold, mask = inbound_fold(), group_mask()
    for a, out in ((1, south), (0, own)):
        inbound_list(blocks[...], table[a, 0], panels.at[2 * a], fold, mask, out)
    for copy in copies[1:]:
        copy.wait()


def final_kernel(gy, gx, own, out):
    total = own[...] + gx[0:64, :] + gy[...]
    group = iota((8, 128), 1) // 16
    for c in range(4):
        field = jnp.zeros((8, 128), F32)
        for k in range(8):
            moved = pltpu.roll(total[k * 8 : (k + 1) * 8], (k - c) % 8 * 16, 1)
            field = jnp.where(group == k, moved, field)
        out[c] = field


def call(kernel, shapes, args, scratch=(), hbm_in=(), hbm_out=(), mib=12):
    args = [
        pltpu.with_memory_space_constraint(x, pltpu.HBM) if n in hbm_in else x
        for n, x in enumerate(args)
    ]
    shapes = [s if isinstance(s, jax.ShapeDtypeStruct) else jax.ShapeDtypeStruct(s, F32) for s in shapes]
    return pl.pallas_call(
        kernel,
        out_shape=shapes,
        in_specs=[HBM if n in hbm_in else VMEM for n in range(len(args))],
        out_specs=[HBM if n in hbm_out else VMEM for n in range(len(shapes))],
        scratch_shapes=list(scratch),
        compiler_params=pltpu.CompilerParams(vmem_limit_bytes=mib * 1024 * 1024),
    )(*args)


def send(block, step):
    wide, high = lax.axis_size("gx"), lax.axis_size("gy")
    route = []
    for i in range(wide):
        for j in range(high):
            to = step(i, j)
            route.append((i * high + j, to[0] % wide * high + to[1] % high))
    return lax.ppermute(block, ("gx", "gy"), route)


def pair(n):
    return n - 1 if n % 2 else n + 1


def other_pair(n):
    return n + 1 if n % 2 else n - 1


def row_pair(i, j):
    return (i, other_pair(j)) if 0 <= other_pair(j) < lax.axis_size("gy") else (pair(i), j)


def per_device(air, out_tables, out_panels, depth, temp, salt, in_tables, in_panels):
    out_panels = out_panels.reshape(4, 1024, 128)
    in_panels = in_panels.reshape(4, 1024, 128)
    out_tables, in_tables = out_tables[0, 0], in_tables[0, 0]
    field = (2, LEVELS, ROWS, COLS)
    to_gx, tiled, out_tables, out_panels, temp, salt, depth = call(
        outbound_kernel,
        [
            (LIST_ROWS, 128),
            jax.ShapeDtypeStruct((64, 1024), BF16),
            jax.ShapeDtypeStruct(out_tables.shape, jnp.int32),
            jax.ShapeDtypeStruct((3, 1024, 128), BF16),
            temp.shape,
            salt.shape,
            jax.ShapeDtypeStruct(depth.shape, jnp.int32),
        ],
        [air, out_tables, out_panels, temp, salt, depth],
        [
            pltpu.VMEM(air.shape, BF16),
            pltpu.VMEM((1024, 128), BF16),
            pltpu.SemaphoreType.DMA((7,)),
        ],
        hbm_in=range(6),
    )
    zpair = send(to_gx, lambda i, j: (other_pair(i), j))
    core = send(to_gx, lambda i, j: (pair(i), j))
    to_side, north = call(
        side_kernel,
        [(LIST_ROWS + ROWS, 128), (LIST_ROWS, 128)],
        [tiled, out_tables, out_panels, temp, salt, depth],
    )
    side_z = send(to_side, lambda i, j: (other_pair(i), j))
    side_core = send(to_side, lambda i, j: (pair(i), j))
    (to_gy,) = call(north_kernel, [north.shape], [north, core, zpair])
    gy = send(to_gy, lambda i, j: (i, j - 1))
    own, partial = call(
        inner_kernel,
        [(LIST_ROWS, 128), field],
        [tiled, out_tables, out_panels, temp, salt, depth],
    )
    base, west, east, depths, partial = call(
        edge_kernel,
        [(LIST_ROWS, 128), (ROWS, 128), (ROWS, 128), (4, ROWS, COLS), field],
        [own, side_core, side_z, partial, temp, salt, depth],
    )
    stepped, cols, row_e, row_o, planes, keep = call(
        first_kernel,
        [field, (ROWS, 128), (43, COLS), (43, COLS), (4, ROWS, COLS), (44, COLS)],
        [gy, base, west, east, partial, temp, salt, depth],
    )
    xo = send(row_o, row_pair)
    xe = send(row_e, lambda i, j: (i, pair(j)))
    zpair = send(cols, lambda i, j: (other_pair(i), j))
    core = send(cols, lambda i, j: (pair(i), j))
    final, blocks, to_gx = call(
        second_kernel,
        [field, jax.ShapeDtypeStruct((64, COLS), BF16), (128, 128)],
        [stepped, core, zpair, xe, xo, planes, depths, keep, depth, in_tables, in_panels],
        [pltpu.VMEM(in_tables.shape, jnp.int32), pltpu.SemaphoreType.DMA],
        hbm_in=(9,),
    )
    gx = send(to_gx, lambda i, j: (i + 1, j))
    new_temp, new_salt, own, south = call(
        outer_kernel,
        [temp.shape, salt.shape, (64, 128), (64, 128)],
        [final, blocks, in_tables, in_panels],
        [pltpu.VMEM(in_tables.shape, jnp.int32), pltpu.SemaphoreType.DMA((3,))],
        hbm_in=(2,),
        hbm_out=(0, 1),
    )
    gy = send(south + gx[64:128], lambda i, j: (i, j + 1))
    (surface,) = call(final_kernel, [(4, 8, 128)], [gy, gx, own])
    return new_temp, new_salt, surface


def solution(mesh):
    in_specs = (
        P(None, "gy", "gx"),
        P("gy", "gx", None, None, None, None),
        P("gy", "gx", None, None, None, None, None),
        P("gy", "gx"),
        P(None, "gy", "gx"),
        P(None, "gy", "gx"),
        P("gy", "gx", None, None, None, None),
        P("gy", "gx", None, None, None, None, None),
    )
    out_specs = (P(None, "gy", "gx"), P(None, "gy", "gx"), P(None, "gy", "gx"))
    return jax.shard_map(
        per_device, mesh=mesh, in_specs=in_specs, out_specs=out_specs, check_vma=False
    )
```

```python
import functools

import jax
import jax.numpy as jnp
from jax import lax
from jax.experimental import pallas as pl
from jax.experimental.pallas import tpu as pltpu
from jax.sharding import PartitionSpec as P

HEAT_RATE = 0.1
SHORTWAVE_RATE = 0.1
FRESH_RATE = 0.05
SIDE_RATE = 0.18
MIX_BASE = 0.03
MIX_WIND = 0.09
MIX_DECAY = 0.8

ROWS, COLS, LEVELS = 16, 512, 10
TILES = COLS // 128
F32, BF16 = jnp.float32, jnp.bfloat16
LIST_ROWS = 4 * 64
VMEM = pl.BlockSpec(memory_space=pltpu.VMEM)
HBM = pl.BlockSpec(memory_space=pltpu.HBM)
NN = (((1,), (0,)), ((), ()))
TN = (((0,), (0,)), ((), ()))
NT = (((1,), (1,)), ((), ()))


def iota(shape, axis):
    return lax.broadcasted_iota(jnp.int32, shape, axis)


def dot(x, y, dims=NN):
    return lax.dot_general(x, y, dims, preferred_element_type=F32)


def dot_split(ones, values):
    high = values.astype(BF16)
    low = (values - high.astype(F32)).astype(BF16)
    return dot(ones, high) + dot(ones, low)


def split_dot(values, ones):
    high = values.astype(BF16)
    low = (values - high.astype(F32)).astype(BF16)
    return dot(high, ones) + dot(low, ones)


def ocean_number(shape, axis):
    place = iota(shape, axis)
    return place % ROWS * TILES + place // ROWS


def atm_number(shape, axis):
    place = iota(shape, axis)
    return place % 8 * 8 + place // 8


def one_hot(number, names):
    return jnp.where(number == names, 1.0, 0.0).astype(BF16)


def group_mask():
    return iota((8, 128), 1) // 16 == iota((8, 128), 0)


def edge_columns(levels):
    lane = iota((ROWS, 128), 1)
    block = jnp.zeros((ROWS, 128), F32)
    for at, values in enumerate(levels):
        block = jnp.where(lane == at, values[:, 0:1], block)
        block = jnp.where(lane == 64 + at, values[:, COLS - 1 : COLS], block)
    return block


def spread_air(air, mask):
    fold = (iota((128, 128), 0) % 16 == iota((128, 128), 1) % 16).astype(F32).astype(BF16)
    spread = []
    for c in range(8):
        for r in range(8):
            row = jnp.broadcast_to(air[c, r : r + 1, :].astype(F32), (8, 128))
            spread.append(jnp.where(mask, row, 0.0))
    tiled = dot(jnp.concatenate(spread, 0).astype(BF16), fold).astype(BF16)
    return jnp.concatenate([tiled[c * 64 : (c + 1) * 64] for c in range(8)], 1)


def outbound_list(tiled, names, panel, mask, out):
    source = iota((64, 64), 0)
    target = ocean_number((64, 64), 0)
    picked = dot(one_hot(source, names[0:1, :]), tiled, TN)
    planes = [[], [], [], []]
    for g in range(8):
        left = [
            jnp.where(mask, picked[g * 8 : (g + 1) * 8, c * 128 : (c + 1) * 128], 0.0)
            for c in range(8)
        ]
        piece = dot(jnp.concatenate(left, 0).astype(BF16), panel[g * 128 : (g + 1) * 128, :])
        f = [piece[c * 8 : (c + 1) * 8] for c in range(8)]
        planes[0].append(f[0] + f[1] + f[2])
        planes[1].append(f[3])
        planes[2].append(f[4] - f[5] + f[6])
        planes[3].append(f[7])
    pieces = jnp.concatenate([jnp.concatenate(p, 0) for p in planes], 1)
    summed = dot_split(one_hot(target, names[1:2, :]), pieces)
    for p in range(4):
        out[p * 64 : (p + 1) * 64, :] = summed[:, p * 128 : (p + 1) * 128]


def fetch(sems, pairs):
    copies = [pltpu.make_async_copy(src, dst, sems.at[n]) for n, (src, dst) in enumerate(pairs)]
    for copy in copies:
        copy.start()
    return copies


def outbound_kernel(
    air_hbm, table_hbm, panels_hbm, temp_hbm, salt_hbm, depth_hbm,
    to_gx, tiled, table, panels, temp, salt, depth, air, panel, sems,
):
    pairs = [(air_hbm, air), (table_hbm, table), (panels_hbm.at[0], panel)]
    pairs += [(temp_hbm, temp), (salt_hbm, salt), (depth_hbm, depth)]
    copies = fetch(sems, pairs + [(panels_hbm.at[1:4], panels)])
    mask = group_mask()
    copies[0].wait()
    tiled[...] = spread_air(air, mask)
    copies[1].wait()
    copies[2].wait()
    outbound_list(tiled[...], table[0, 0], panel, mask, to_gx)
    for copy in copies[3:]:
        copy.wait()


def side_kernel(tiled, table, panels, temp, salt, depth, to_gx, north):
    mask = group_mask()
    deep = depth[...].astype(F32)
    levels = [temp[l] for l in range(LEVELS)] + [salt[l] for l in range(LEVELS)] + [deep]
    to_gx[LIST_ROWS:, :] = edge_columns(levels)
    outbound_list(tiled[...], table[1, 0], panels.at[1], mask, to_gx.at[0:LIST_ROWS])
    outbound_list(tiled[...], table[0, 1], panels.at[0], mask, north)


def beside(values, north, south, west, east):
    row, col = iota((ROWS, COLS), 0), iota((ROWS, COLS), 1)
    return (
        jnp.where(row == 0, north, pltpu.roll(values, 1, 0)),
        jnp.where(row == ROWS - 1, south, pltpu.roll(values, ROWS - 1, 0)),
        jnp.where(col == 0, west, pltpu.roll(values, 1, 1)),
        jnp.where(col == COLS - 1, east, pltpu.roll(values, COLS - 1, 1)),
    )


def side_sum(centre, nears, wets):
    side = jnp.zeros_like(centre)
    for near, there in zip(nears, wets):
        side = side + jnp.where(there, near - centre, 0.0)
    return SIDE_RATE * side


def inner_kernel(tiled, table, panels, temp, salt, depth, own, partial):
    deep = depth[...].astype(F32)
    dry = jnp.zeros((1, 1), F32)
    around = beside(deep, dry, dry, dry, dry)
    for l in range(LEVELS):
        wet = deep > l
        wets = [d > l for d in around]
        for t, field in enumerate((temp, salt)):
            centre = field[l]
            side = side_sum(centre, beside(centre, dry, dry, dry, dry), wets)
            partial[t, l] = centre + jnp.where(wet, side, 0.0)
    outbound_list(tiled[...], table[1, 1], panels.at[2], group_mask(), own)


def north_kernel(part, core, zpair, out):
    odd_col = lax.axis_index("gx") % 2 == 1
    out[...] = part[...] + jnp.where(odd_col, zpair[...], core[...])


def edge_kernel(own, core, zpair, partial, temp, salt, depth, base, west, east, depths, whole):
    odd_col = lax.axis_index("gx") % 2 == 1
    base[...] = own[...] + jnp.where(
        odd_col, zpair[0:LIST_ROWS, :], core[0:LIST_ROWS, :]
    )
    left = jnp.where(odd_col, core[LIST_ROWS:, :], zpair[LIST_ROWS:, :])
    right = jnp.where(odd_col, zpair[LIST_ROWS:, :], core[LIST_ROWS:, :])
    west[...] = left
    east[...] = right
    deep = depth[...].astype(F32)
    dry = jnp.zeros((1, 1), F32)
    last = 2 * LEVELS
    around = beside(deep, dry, dry, left[:, 64 + last : 65 + last], right[:, last : last + 1])
    for n in range(4):
        depths[n] = around[n]
    lane = iota((ROWS, 128), 1)
    sides = ((0, left, 64, around[2], 0), (COLS - 128, right, 0, around[3], 127))
    for t, field in enumerate((temp, salt)):
        for l in range(LEVELS):
            at = t * LEVELS + l
            whole[t, l] = partial[t, l]
            for first, halo, offset, far, spot in sides:
                here = (lane == spot) & (far[:, first : first + 128] > l)
                here = here & (deep[:, first : first + 128] > l)
                near = halo[:, offset + at : offset + at + 1] - field[l, :, first : first + 128]
                whole[t, l, :, first : first + 128] += jnp.where(here, SIDE_RATE * near, 0.0)


def column_change(values, below, mixing, depth, l, across):
    change = 0.0 if l == 0 else -across
    if l < LEVELS - 1:
        across = mixing * (MIX_DECAY**l) * (below - values)
        across = jnp.where(depth > l + 1, across, 0.0)
        change = change + across
    return change, across


def source(t, l, planes, values):
    if t == 0:
        heating = planes[1] * (SHORTWAVE_RATE * 2.718281828459045 ** (-0.5 * l))
        return heating + HEAT_RATE * planes[0] if l == 0 else heating
    return -FRESH_RATE * planes[2] * values if l == 0 else 0.0


def first_kernel(
    gy, base, west, east, partial, temp, salt, depth, new, cols, row_e, row_o, planes, keep
):
    odd_row = lax.axis_index("gy") % 2 == 1
    forcing = []
    for p in range(4):
        parts = []
        for s in range(TILES):
            at = p * 64 + s * ROWS
            parts.append(base[at : at + ROWS, :] + gy[at : at + ROWS, :])
        forcing.append(jnp.concatenate(parts, 1))
    squared = forcing[3] * forcing[3]
    forcing[3] = squared / (1.0 + squared)
    for p in range(4):
        planes[p] = forcing[p]
    deep = depth[...].astype(F32)
    lane = iota((ROWS, 128), 1)
    mixing = MIX_BASE + MIX_WIND * forcing[3]
    block = jnp.zeros((ROWS, 128), F32)
    for t, field in enumerate((temp, salt)):
        across = None
        for l in range(LEVELS):
            at = t * LEVELS + l
            centre = field[l]
            change, across = column_change(
                centre, field[min(l + 1, LEVELS - 1)], mixing, deep, l, across
            )
            change = change + source(t, l, forcing, centre)
            value = partial[t, l] + jnp.where(deep > l, change, 0.0)
            new[t, l] = value
            block = jnp.where(lane == at, value[:, 0:1], block)
            block = jnp.where(lane == 64 + at, value[:, COLS - 1 : COLS], block)
    cols[...] = block
    edges = []
    for r in (0, ROWS - 1):
        rows = [new[0, :, r, :], new[1, :, r, :], temp[:, r, :], salt[:, r, :], deep[r : r + 1]]
        edges.append(rows + [west[r : r + 1, :], east[r : r + 1, :]])
    for out, first in ((row_e, odd_row), (row_o, jnp.logical_not(odd_row))):
        at = 0
        for a, b in zip(*edges):
            out[at : at + a.shape[0], 0 : a.shape[1]] = jnp.where(first, a, b)
            at += a.shape[0]
    row_o[43:48, :] = jnp.zeros((5, COLS), F32)
    for n in range(2):
        keep[20 * n : 20 * n + 10, :] = edges[n][2]
        keep[20 * n + 10 : 20 * n + 20, :] = edges[n][3]
        keep[40 + 2 * n : 41 + 2 * n, 0:128] = edges[n][5]
        keep[41 + 2 * n : 42 + 2 * n, 0:128] = edges[n][6]


def inbound_list(blocks, names, panel, fold, mask, out):
    source_block = ocean_number((64, 64), 0)
    target = atm_number((64, 64), 0)
    chosen = dot(one_hot(source_block, names[0:1, :]), blocks, TN)
    kept = [[], [], [], []]
    for g in range(8):
        part = chosen[g * 8 : (g + 1) * 8]
        left = [part[:, c * 128 : (c + 1) * 128] for c in range(4)]
        piece = dot(
            jnp.concatenate(left, 0).astype(BF16), panel[g * 128 : (g + 1) * 128, :], NT
        )
        for c in range(4):
            kept[c].append(jnp.where(mask, piece[c * 8 : (c + 1) * 8], 0.0))
    kept = jnp.concatenate([jnp.concatenate(k, 0) for k in kept], 1)
    pieces = split_dot(kept, fold)
    out[0:64, :] = dot_split(one_hot(target, names[1:2, :]), pieces)


def inbound_fold():
    place, lane = iota((512, 128), 0), iota((512, 128), 1)
    fold = jnp.where((place // 128 == lane // 16) & (place % 16 == lane % 16), 1.0, 0.0)
    return fold.astype(BF16)


def second_kernel(
    old, core, zpair, xe, xo, planes, depths, keep, depth, table_hbm, panels,
    final, surface_blocks, to_dg, table, sem,
):
    copy = pltpu.make_async_copy(table_hbm, table, sem)
    copy.start()
    odd_col = lax.axis_index("gx") % 2 == 1
    odd_row = lax.axis_index("gy") % 2 == 1
    deep = depth[...].astype(F32)
    row_e, row_o = xe[...], xo[0:43, :]
    beyond = (jnp.where(odd_row, row_e, row_o), jnp.where(odd_row, row_o, row_e))
    level = iota((2 * LEVELS, COLS), 0) % LEVELS
    at_end = (lax.axis_index("gy") == 0, lax.axis_index("gy") == lax.axis_size("gy") - 1)
    beyond_deep = [jnp.where(end, 0.0, other[40:41]) for end, other in zip(at_end, beyond)]
    fixes, halo_rows = [], []
    for n, other in enumerate(beyond):
        r = n * (ROWS - 1)
        here = (deep[r : r + 1] > level) & (beyond_deep[n] > level)
        fix = jnp.where(here, SIDE_RATE * (other[20:40] - keep[20 * n : 20 * n + 20, :]), 0.0)
        fixes.append(fix)
        halo_rows.append(other[0:20] - fix)
    norths, souths = halo_rows
    level = iota((1, 128), 1) % 64 % LEVELS
    row = iota((ROWS, 128), 0)
    ends = []
    for halo, at, deepest in (
        (jnp.where(odd_col, core[...], zpair[...]), 0, 84),
        (jnp.where(odd_col, zpair[...], core[...]), 1, 20),
    ):
        for n, other in enumerate(beyond):
            mine = keep[40 + 2 * n + at : 41 + 2 * n + at, 0:128]
            far = other[41 + at : 42 + at, 0:128]
            here = mine[:, deepest : deepest + 1] > level
            here = here & (jnp.where(at_end[n], 0.0, far[:, deepest : deepest + 1]) > level)
            fix = jnp.where(here, SIDE_RATE * (far - mine), 0.0)
            halo = halo + jnp.where(row == n * (ROWS - 1), fix, 0.0)
        ends.append(halo)
    west, east = ends
    row8, row = iota((8, COLS), 0), iota((ROWS, COLS), 0)
    around = [depths[n] for n in range(4)]
    around[0] = jnp.where(row == 0, beyond_deep[0], around[0])
    around[1] = jnp.where(row == ROWS - 1, beyond_deep[1], around[1])
    forcing = [planes[p] for p in range(4)]
    mixing = MIX_BASE + MIX_WIND * forcing[3]
    top = {}

    def whole(t, l):
        at = t * LEVELS + l
        high = old[t, l, 0:8, :] + jnp.where(row8 == 0, fixes[0][at : at + 1], 0.0)
        low = old[t, l, 8:16, :] + jnp.where(row8 == 7, fixes[1][at : at + 1], 0.0)
        return jnp.concatenate([high, low], 0)

    for t in range(2):
        across, centre = None, whole(t, 0)
        for l in range(LEVELS):
            at = t * LEVELS + l
            below = whole(t, l + 1) if l < LEVELS - 1 else None
            change, across = column_change(centre, below, mixing, deep, l, across)
            change = change + source(t, l, forcing, centre)
            nears = beside(
                centre,
                norths[at : at + 1],
                souths[at : at + 1],
                west[:, 64 + at : 65 + at],
                east[:, at : at + 1],
            )
            change = change + side_sum(centre, nears, [d > l for d in around])
            value = centre + jnp.where(deep > l, change, 0.0)
            final[t, l] = value
            if l < 3:
                top[t, l] = value
            centre = below
    wet_top = jnp.where(deep > 0, 1.0, 0.0)
    surface = (
        top[0, 0] * wet_top,
        top[1, 0] * wet_top,
        (top[0, 0] + top[0, 1] + top[0, 2]) / 3.0 * wet_top,
        wet_top,
    )
    parts = []
    for f in surface:
        parts.append(jnp.concatenate([f[:, s * 128 : (s + 1) * 128] for s in range(TILES)], 0))
    blocks = jnp.concatenate(parts, 1).astype(BF16)
    surface_blocks[...] = blocks
    copy.wait()
    inbound_list(blocks, table[1, 1], panels.at[3], inbound_fold(), group_mask(), to_dg)
    to_dg[64:, :] = jnp.zeros((16, 128), F32)


def inbound_kernel(a, b, blocks, table, panels, out):
    fold, mask = inbound_fold(), group_mask()
    inbound_list(blocks[...], table[a, b], panels.at[2 * a + b], fold, mask, out)
    if out.shape[0] > 64:
        out[64:, :] = jnp.zeros((out.shape[0] - 64, 128), F32)


def outer_kernel(final, blocks, table, panels, new_temp, new_salt, own, sems):
    copies = fetch(sems, [(final.at[0], new_temp), (final.at[1], new_salt)])
    inbound_kernel(0, 0, blocks, table, panels, own)
    for copy in copies:
        copy.wait()


def final_kernel(dg, gy, gx, own, out):
    total = own[...] + gx[0:64, :] + gy[0:64, :] + dg[0:64, :]
    group = iota((8, 128), 1) // 16
    for c in range(4):
        field = jnp.zeros((8, 128), F32)
        for k in range(8):
            moved = pltpu.roll(total[k * 8 : (k + 1) * 8], (k - c) % 8 * 16, 1)
            field = jnp.where(group == k, moved, field)
        out[c] = field


def call(kernel, shapes, args, scratch=(), hbm_in=(), hbm_out=(), mib=12):
    args = [
        pltpu.with_memory_space_constraint(x, pltpu.HBM) if n in hbm_in else x
        for n, x in enumerate(args)
    ]
    shapes = [s if isinstance(s, jax.ShapeDtypeStruct) else jax.ShapeDtypeStruct(s, F32) for s in shapes]
    return pl.pallas_call(
        kernel,
        out_shape=shapes,
        in_specs=[HBM if n in hbm_in else VMEM for n in range(len(args))],
        out_specs=[HBM if n in hbm_out else VMEM for n in range(len(shapes))],
        scratch_shapes=list(scratch),
        compiler_params=pltpu.CompilerParams(vmem_limit_bytes=mib * 1024 * 1024),
    )(*args)


def send(block, step):
    wide, high = lax.axis_size("gx"), lax.axis_size("gy")
    route = []
    for i in range(wide):
        for j in range(high):
            to = step(i, j)
            route.append((i * high + j, to[0] % wide * high + to[1] % high))
    return lax.ppermute(block, ("gx", "gy"), route)


def pair(n):
    return n - 1 if n % 2 else n + 1


def other_pair(n):
    return n + 1 if n % 2 else n - 1


def row_pair(i, j):
    return (i, other_pair(j)) if 0 <= other_pair(j) < lax.axis_size("gy") else (pair(i), j)


def per_device(air, out_tables, out_panels, depth, temp, salt, in_tables, in_panels):
    out_panels = out_panels.reshape(4, 1024, 128)
    in_panels = in_panels.reshape(4, 1024, 128)
    out_tables, in_tables = out_tables[0, 0], in_tables[0, 0]
    field = (2, LEVELS, ROWS, COLS)
    to_gx, tiled, out_tables, out_panels, temp, salt, depth = call(
        outbound_kernel,
        [
            (LIST_ROWS, 128),
            jax.ShapeDtypeStruct((64, 1024), BF16),
            jax.ShapeDtypeStruct(out_tables.shape, jnp.int32),
            jax.ShapeDtypeStruct((3, 1024, 128), BF16),
            temp.shape,
            salt.shape,
            jax.ShapeDtypeStruct(depth.shape, jnp.int32),
        ],
        [air, out_tables, out_panels, temp, salt, depth],
        [
            pltpu.VMEM(air.shape, BF16),
            pltpu.VMEM((1024, 128), BF16),
            pltpu.SemaphoreType.DMA((7,)),
        ],
        hbm_in=range(6),
    )
    zpair = send(to_gx, lambda i, j: (other_pair(i), j))
    core = send(to_gx, lambda i, j: (pair(i), j))
    to_side, north = call(
        side_kernel,
        [(LIST_ROWS + ROWS, 128), (LIST_ROWS, 128)],
        [tiled, out_tables, out_panels, temp, salt, depth],
    )
    side_z = send(to_side, lambda i, j: (other_pair(i), j))
    side_core = send(to_side, lambda i, j: (pair(i), j))
    (to_gy,) = call(north_kernel, [north.shape], [north, core, zpair])
    gy = send(to_gy, lambda i, j: (i, j - 1))
    own, partial = call(
        inner_kernel,
        [(LIST_ROWS, 128), field],
        [tiled, out_tables, out_panels, temp, salt, depth],
    )
    base, west, east, depths, partial = call(
        edge_kernel,
        [(LIST_ROWS, 128), (ROWS, 128), (ROWS, 128), (4, ROWS, COLS), field],
        [own, side_core, side_z, partial, temp, salt, depth],
    )
    stepped, cols, row_e, row_o, planes, keep = call(
        first_kernel,
        [field, (ROWS, 128), (43, COLS), (48, COLS), (4, ROWS, COLS), (44, COLS)],
        [gy, base, west, east, partial, temp, salt, depth],
    )
    xo = send(row_o, row_pair)
    xe = send(row_e, lambda i, j: (i, pair(j)))
    zpair = send(cols, lambda i, j: (other_pair(i), j))
    core = send(cols, lambda i, j: (pair(i), j))
    final, blocks, to_dg, in_tables = call(
        second_kernel,
        [
            field,
            jax.ShapeDtypeStruct((64, COLS), BF16),
            (80, 128),
            jax.ShapeDtypeStruct(in_tables.shape, jnp.int32),
        ],
        [stepped, core, zpair, xe, xo, planes, depths, keep, depth, in_tables, in_panels],
        [pltpu.SemaphoreType.DMA],
        hbm_in=(9,),
    )
    dg = send(to_dg, lambda i, j: (i + 1, j + 1) if j + 1 < lax.axis_size("gy") else (i, j + 1))
    (to_gy,) = call(
        functools.partial(inbound_kernel, 1, 0), [(72, 128)], [blocks, in_tables, in_panels]
    )
    gy = send(to_gy, lambda i, j: (i, j + 1))
    (to_gx,) = call(
        functools.partial(inbound_kernel, 0, 1), [(64, 128)], [blocks, in_tables, in_panels]
    )
    gx = send(to_gx, lambda i, j: (i + 1, j))
    new_temp, new_salt, own = call(
        outer_kernel,
        [temp.shape, salt.shape, (64, 128)],
        [final, blocks, in_tables, in_panels],
        [pltpu.SemaphoreType.DMA((2,))],
        hbm_out=(0, 1),
    )
    (surface,) = call(final_kernel, [(4, 8, 128)], [dg, gy, gx, own])
    return new_temp, new_salt, surface


def solution(mesh):
    in_specs = (
        P(None, "gy", "gx"),
        P("gy", "gx", None, None, None, None),
        P("gy", "gx", None, None, None, None, None),
        P("gy", "gx"),
        P(None, "gy", "gx"),
        P(None, "gy", "gx"),
        P("gy", "gx", None, None, None, None),
        P("gy", "gx", None, None, None, None, None),
    )
    out_specs = (P(None, "gy", "gx"), P(None, "gy", "gx"), P(None, "gy", "gx"))
    return jax.shard_map(
        per_device, mesh=mesh, in_specs=in_specs, out_specs=out_specs, check_vma=False
    )
```

```python
import functools

import jax
import jax.numpy as jnp
from jax import lax
from jax.experimental import pallas as pl
from jax.experimental.pallas import tpu as pltpu
from jax.sharding import PartitionSpec as P

HEAT_RATE = 0.1
SHORTWAVE_RATE = 0.1
FRESH_RATE = 0.05
SIDE_RATE = 0.18
MIX_BASE = 0.03
MIX_WIND = 0.09
MIX_DECAY = 0.8

ROWS, COLS, LEVELS = 16, 512, 10
TILES = COLS // 128
F32, BF16 = jnp.float32, jnp.bfloat16
LIST_ROWS = 4 * 64
FORCING_ORDER = ((0, 0), (1, 0), (0, 1))
TOP_LEVELS = ((0, 3), (0, 1))
SURFACE_ORDER = ((1, 1), (1, 0), (0, 1))
VMEM = pl.BlockSpec(memory_space=pltpu.VMEM)
HBM = pl.BlockSpec(memory_space=pltpu.HBM)
NN = (((1,), (0,)), ((), ()))
TN = (((0,), (0,)), ((), ()))
NT = (((1,), (1,)), ((), ()))


def iota(shape, axis):
    return lax.broadcasted_iota(jnp.int32, shape, axis)


def dot(x, y, dims=NN):
    return lax.dot_general(x, y, dims, preferred_element_type=F32)


def dot_split(ones, values):
    high = values.astype(BF16)
    low = (values - high.astype(F32)).astype(BF16)
    return dot(jnp.concatenate([ones, ones], 1), jnp.concatenate([high, low], 0))


def split_dot(values, ones):
    high = values.astype(BF16)
    low = (values - high.astype(F32)).astype(BF16)
    return dot(high, ones) + dot(low, ones)


def ocean_number(shape, axis):
    place = iota(shape, axis)
    return place % ROWS * TILES + place // ROWS


def atm_number(shape, axis):
    place = iota(shape, axis)
    return place % 8 * 8 + place // 8


def one_hot(number, names):
    return jnp.where(number == names, 1.0, 0.0).astype(BF16)


def group_mask():
    return iota((8, 128), 1) // 16 == iota((8, 128), 0)


def edge_columns(levels):
    lane = iota((ROWS, 128), 1)
    block = jnp.zeros((ROWS, 128), F32)
    for at, values in enumerate(levels):
        block = jnp.where(lane == at, values[:, 0:1], block)
        block = jnp.where(lane == 64 + at, values[:, COLS - 1 : COLS], block)
    return block


def spread_air(air, mask):
    fold = (iota((128, 128), 0) % 16 == iota((128, 128), 1) % 16).astype(F32).astype(BF16)
    spread = []
    for c in range(8):
        for r in range(8):
            row = jnp.broadcast_to(air[c, r : r + 1, :].astype(F32), (8, 128))
            spread.append(jnp.where(mask, row, 0.0))
    tiled = dot(jnp.concatenate(spread, 0).astype(BF16), fold).astype(BF16)
    return jnp.concatenate([tiled[c * 64 : (c + 1) * 64] for c in range(8)], 1)


def outbound_list(tiled, names, panel, mask, outs):
    source = iota((64, 64), 0)
    target = ocean_number((64, 64), 0)
    picked = dot(one_hot(source, names[0:1, :]), tiled, TN)
    planes = [[], [], [], []]
    for g in range(8):
        left = [
            jnp.where(mask, picked[g * 8 : (g + 1) * 8, c * 128 : (c + 1) * 128], 0.0)
            for c in range(8)
        ]
        piece = dot(jnp.concatenate(left, 0).astype(BF16), panel[g * 128 : (g + 1) * 128, :])
        f = [piece[c * 8 : (c + 1) * 8] for c in range(8)]
        planes[0].append(f[0] + f[1] + f[2])
        planes[1].append(f[3])
        planes[2].append(f[4] - f[5] + f[6])
        planes[3].append(f[7])
    pieces = jnp.concatenate([jnp.concatenate(p, 0) for p in planes], 1)
    summed = dot_split(one_hot(target, names[1:2, :]), pieces)
    for out in outs:
        for p in range(4):
            out[p * 64 : (p + 1) * 64, :] = summed[:, p * 128 : (p + 1) * 128]


def fetch(sems, pairs):
    copies = [pltpu.make_async_copy(src, dst, sems.at[n]) for n, (src, dst) in enumerate(pairs)]
    for copy in copies:
        copy.start()
    return copies


def outbound_list_out(kind, tiled, table, panels, temp, salt, depth, outs):
    a, b = kind
    for out in outs:
        if out.shape[0] > LIST_ROWS:
            out[LIST_ROWS:, :] = jnp.zeros((out.shape[0] - LIST_ROWS, 128), F32)
    if kind == (1, 0):
        deep = depth[...].astype(F32)
        levels = [temp[l] for l in range(LEVELS)] + [salt[l] for l in range(LEVELS)] + [deep]
        block = edge_columns(levels)
        for out in outs:
            out[LIST_ROWS : LIST_ROWS + ROWS, :] = block
    outbound_list(tiled, table[a, b], panels.at[2 * a + b], group_mask(), outs)


def outbound_kernel(
    kind, air_hbm, table_hbm, panels_hbm, temp_hbm, salt_hbm, depth_hbm,
    tiled, table, panels, temp, salt, depth, *rest,
):
    outs, (air, sems) = rest[:-2], rest[-2:]
    order = [2 * kind[0] + kind[1]]
    order += [n for n in range(4) if n not in order]
    pairs = [(air_hbm, air), (table_hbm, table), (panels_hbm.at[order[0]], panels.at[order[0]])]
    pairs += [(temp_hbm, temp), (salt_hbm, salt), (depth_hbm, depth)]
    copies = fetch(sems, pairs + [(panels_hbm.at[n], panels.at[n]) for n in order[1:]])
    copies[0].wait()
    tiled[...] = spread_air(air, group_mask())
    for copy in copies[1:6]:
        copy.wait()
    outbound_list_out(kind, tiled[...], table, panels, temp, salt, depth, outs)
    for copy in copies[6:]:
        copy.wait()


def next_kernel(kind, tiled, table, panels, temp, salt, depth, *outs):
    outbound_list_out(kind, tiled[...], table, panels, temp, salt, depth, outs)


def beside(values, north, south, west, east):
    row, col = iota((ROWS, COLS), 0), iota((ROWS, COLS), 1)
    return (
        jnp.where(row == 0, north, pltpu.roll(values, 1, 0)),
        jnp.where(row == ROWS - 1, south, pltpu.roll(values, ROWS - 1, 0)),
        jnp.where(col == 0, west, pltpu.roll(values, 1, 1)),
        jnp.where(col == COLS - 1, east, pltpu.roll(values, COLS - 1, 1)),
    )


def side_sum(centre, nears, wets):
    side = jnp.zeros_like(centre)
    for near, there in zip(nears, wets):
        side = side + jnp.where(there, near - centre, 0.0)
    return SIDE_RATE * side


def inner_kernel(
    tiled, table, panels, temp, salt, depth, in_table_hbm, own, partial, sources, targets, fold,
    in_table, sem,
):
    copy = pltpu.make_async_copy(in_table_hbm, in_table, sem)
    copy.start()
    deep = depth[...].astype(F32)
    dry = jnp.zeros((1, 1), F32)
    around = beside(deep, dry, dry, dry, dry)
    for l in range(LEVELS):
        wet = deep > l
        wets = [d > l for d in around]
        for t, field in enumerate((temp, salt)):
            centre = field[l]
            side = side_sum(centre, beside(centre, dry, dry, dry, dry), wets)
            partial[t, l] = centre + jnp.where(wet, side, 0.0)
    outbound_list(tiled[...], table[1, 1], panels.at[3], group_mask(), (own,))
    copy.wait()
    fold[...] = inbound_fold()
    source_block, target = ocean_number((64, 64), 0), atm_number((64, 64), 0)
    for n in range(4):
        sources[n] = one_hot(source_block, in_table[n // 2, n % 2, 0:1, :])
        targets[n] = one_hot(target, in_table[n // 2, n % 2, 1:2, :])


def edge_kernel(own, core, zpair, partial, temp, salt, depth, base, west, east, depths, whole):
    odd_col = lax.axis_index("gx") % 2 == 1
    base[...] = own[...] + jnp.where(
        odd_col, zpair[0:LIST_ROWS, :], core[0:LIST_ROWS, :]
    )
    at = slice(LIST_ROWS, LIST_ROWS + ROWS)
    left = jnp.where(odd_col, core[at, :], zpair[at, :])
    right = jnp.where(odd_col, zpair[at, :], core[at, :])
    west[...] = left
    east[...] = right
    deep = depth[...].astype(F32)
    dry = jnp.zeros((1, 1), F32)
    last = 2 * LEVELS
    around = beside(deep, dry, dry, left[:, 64 + last : 65 + last], right[:, last : last + 1])
    for n in range(4):
        depths[n] = around[n]
    lane = iota((ROWS, 128), 1)
    sides = ((0, left, 64, around[2], 0), (COLS - 128, right, 0, around[3], 127))
    for t, field in enumerate((temp, salt)):
        for l in range(LEVELS):
            at = t * LEVELS + l
            whole[t, l] = partial[t, l]
            for first, halo, offset, far, spot in sides:
                here = (lane == spot) & (far[:, first : first + 128] > l)
                here = here & (deep[:, first : first + 128] > l)
                near = halo[:, offset + at : offset + at + 1] - field[l, :, first : first + 128]
                whole[t, l, :, first : first + 128] += jnp.where(here, SIDE_RATE * near, 0.0)


def column_change(values, below, mixing, depth, l, across):
    change = 0.0 if l == 0 else -across
    if l < LEVELS - 1:
        across = mixing * (MIX_DECAY**l) * (below - values)
        across = jnp.where(depth > l + 1, across, 0.0)
        change = change + across
    return change, across


def source(t, l, planes, values):
    if t == 0:
        heating = planes[1] * (SHORTWAVE_RATE * 2.718281828459045 ** (-0.5 * l))
        return heating + HEAT_RATE * planes[0] if l == 0 else heating
    return -FRESH_RATE * planes[2] * values if l == 0 else 0.0


def first_kernel(
    dg, gy, base, partial, temp, salt, depth, new, cols, planes
):
    forcing = []
    for p in range(4):
        parts = []
        for s in range(TILES):
            at = p * 64 + s * ROWS
            parts.append(base[at : at + ROWS, :] + gy[at : at + ROWS, :] + dg[at : at + ROWS, :])
        forcing.append(jnp.concatenate(parts, 1))
    squared = forcing[3] * forcing[3]
    forcing[3] = squared / (1.0 + squared)
    for p in range(4):
        planes[p] = forcing[p]
    deep = depth[...].astype(F32)
    lane = iota((ROWS, 128), 1)
    mixing = MIX_BASE + MIX_WIND * forcing[3]
    block = jnp.zeros((ROWS, 128), F32)
    for t, field in enumerate((temp, salt)):
        across = None
        for l in range(LEVELS):
            at = t * LEVELS + l
            centre = field[l]
            change, across = column_change(
                centre, field[min(l + 1, LEVELS - 1)], mixing, deep, l, across
            )
            change = change + source(t, l, forcing, centre)
            value = partial[t, l] + jnp.where(deep > l, change, 0.0)
            new[t, l] = value
            block = jnp.where(lane == at, value[:, 0:1], block)
            block = jnp.where(lane == 64 + at, value[:, COLS - 1 : COLS], block)
    cols[...] = block


def rows_kernel(new, temp, salt, depth, west, east, row_e, row_o, keep):
    odd_row = lax.axis_index("gy") % 2 == 1
    deep = depth[...].astype(F32)
    edges = []
    for r in (0, ROWS - 1):
        rows = [new[0, :, r, :], new[1, :, r, :], temp[:, r, :], salt[:, r, :], deep[r : r + 1]]
        edges.append(rows + [west[r : r + 1, :], east[r : r + 1, :]])
    for out, first in ((row_e, odd_row), (row_o, jnp.logical_not(odd_row))):
        at = 0
        for a, b in zip(*edges):
            out[at : at + a.shape[0], 0 : a.shape[1]] = jnp.where(first, a, b)
            at += a.shape[0]
    row_o[43:48, :] = jnp.zeros((5, COLS), F32)
    for n in range(2):
        keep[20 * n : 20 * n + 10, :] = edges[n][2]
        keep[20 * n + 10 : 20 * n + 20, :] = edges[n][3]
        keep[40 + 2 * n : 41 + 2 * n, 0:128] = edges[n][5]
        keep[41 + 2 * n : 42 + 2 * n, 0:128] = edges[n][6]


def inbound_list(blocks, source, target, panel, fold, out):
    mask = group_mask()
    chosen = dot(source, blocks, TN)
    kept = [[], [], [], []]
    for g in range(8):
        part = chosen[g * 8 : (g + 1) * 8]
        left = [part[:, c * 128 : (c + 1) * 128] for c in range(4)]
        piece = dot(
            jnp.concatenate(left, 0).astype(BF16), panel[g * 128 : (g + 1) * 128, :], NT
        )
        for c in range(4):
            kept[c].append(jnp.where(mask, piece[c * 8 : (c + 1) * 8], 0.0))
    kept = jnp.concatenate([jnp.concatenate(k, 0) for k in kept], 1)
    pieces = split_dot(kept, fold)
    out[0:64, :] = dot_split(target, pieces)


def inbound_fold():
    place, lane = iota((512, 128), 0), iota((512, 128), 1)
    fold = jnp.where((place // 128 == lane // 16) & (place % 16 == lane % 16), 1.0, 0.0)
    return fold.astype(BF16)


def second_step(levels, old, core, zpair, xe, xo, planes, depths, keep, depth, store):
    odd_col = lax.axis_index("gx") % 2 == 1
    odd_row = lax.axis_index("gy") % 2 == 1
    deep = depth[...].astype(F32)
    row_e, row_o = xe[...], xo[0:43, :]
    beyond = (jnp.where(odd_row, row_e, row_o), jnp.where(odd_row, row_o, row_e))
    level = iota((2 * LEVELS, COLS), 0) % LEVELS
    at_end = (lax.axis_index("gy") == 0, lax.axis_index("gy") == lax.axis_size("gy") - 1)
    beyond_deep = [jnp.where(end, 0.0, other[40:41]) for end, other in zip(at_end, beyond)]
    fixes, halo_rows = [], []
    for n, other in enumerate(beyond):
        r = n * (ROWS - 1)
        here = (deep[r : r + 1] > level) & (beyond_deep[n] > level)
        fix = jnp.where(here, SIDE_RATE * (other[20:40] - keep[20 * n : 20 * n + 20, :]), 0.0)
        fixes.append(fix)
        halo_rows.append(other[0:20] - fix)
    norths, souths = halo_rows
    level = iota((1, 128), 1) % 64 % LEVELS
    row = iota((ROWS, 128), 0)
    ends = []
    for halo, at, deepest in (
        (jnp.where(odd_col, core[...], zpair[...]), 0, 84),
        (jnp.where(odd_col, zpair[...], core[...]), 1, 20),
    ):
        for n, other in enumerate(beyond):
            mine = keep[40 + 2 * n + at : 41 + 2 * n + at, 0:128]
            far = other[41 + at : 42 + at, 0:128]
            here = mine[:, deepest : deepest + 1] > level
            here = here & (jnp.where(at_end[n], 0.0, far[:, deepest : deepest + 1]) > level)
            fix = jnp.where(here, SIDE_RATE * (far - mine), 0.0)
            halo = halo + jnp.where(row == n * (ROWS - 1), fix, 0.0)
        ends.append(halo)
    west, east = ends
    row8, row = iota((8, COLS), 0), iota((ROWS, COLS), 0)
    around = [depths[n] for n in range(4)]
    around[0] = jnp.where(row == 0, beyond_deep[0], around[0])
    around[1] = jnp.where(row == ROWS - 1, beyond_deep[1], around[1])
    forcing = [planes[p] for p in range(4)]
    mixing = MIX_BASE + MIX_WIND * forcing[3]
    def whole(t, l):
        at = t * LEVELS + l
        high = old[t, l, 0:8, :] + jnp.where(row8 == 0, fixes[0][at : at + 1], 0.0)
        low = old[t, l, 8:16, :] + jnp.where(row8 == 7, fixes[1][at : at + 1], 0.0)
        return jnp.concatenate([high, low], 0)

    for t, (start, stop) in enumerate(levels):
        across, centre = None, whole(t, start)
        if start:
            across = mixing * (MIX_DECAY ** (start - 1)) * (centre - whole(t, start - 1))
            across = jnp.where(deep > start, across, 0.0)
        for l in range(start, stop):
            at = t * LEVELS + l
            below = whole(t, l + 1) if l < LEVELS - 1 else None
            change, across = column_change(centre, below, mixing, deep, l, across)
            change = change + source(t, l, forcing, centre)
            nears = beside(
                centre,
                norths[at : at + 1],
                souths[at : at + 1],
                west[:, 64 + at : 65 + at],
                east[:, at : at + 1],
            )
            change = change + side_sum(centre, nears, [d > l for d in around])
            store(t, l, centre + jnp.where(deep > l, change, 0.0))
            centre = below


def second_kernel(
    old, core, zpair, xe, xo, planes, depths, keep, depth, sources, targets, fold, panels,
    top_temp, top_salt, surface_blocks, out,
):
    top = {}

    def store(t, l, value):
        (top_temp, top_salt)[t][l] = value
        top[t, l] = value

    second_step(TOP_LEVELS, old, core, zpair, xe, xo, planes, depths, keep, depth, store)
    deep = depth[...].astype(F32)
    wet_top = jnp.where(deep > 0, 1.0, 0.0)
    surface = (
        top[0, 0] * wet_top,
        top[1, 0] * wet_top,
        (top[0, 0] + top[0, 1] + top[0, 2]) / 3.0 * wet_top,
        wet_top,
    )
    parts = []
    for f in surface:
        parts.append(jnp.concatenate([f[:, s * 128 : (s + 1) * 128] for s in range(TILES)], 0))
    blocks = jnp.concatenate(parts, 1).astype(BF16)
    surface_blocks[...] = blocks
    inbound_kernel(*SURFACE_ORDER[0], surface_blocks, sources, targets, fold, panels, out)


def inbound_kernel(a, b, blocks, sources, targets, fold, panels, out):
    n = 2 * a + b
    inbound_list(blocks[...], sources[n], targets[n], panels.at[n], fold[...], out)
    if out.shape[0] > 64:
        out[64:, :] = jnp.zeros((out.shape[0] - 64, 128), F32)


def outer_kernel(
    old, core, zpair, xe, xo, planes, depths, keep, depth, top_temp, top_salt,
    blocks, sources, targets, fold, panels, new_temp, new_salt, own, rest, sems,
):
    pairs = []
    for t, (top, new) in enumerate(((top_temp, new_temp), (top_salt, new_salt))):
        count = TOP_LEVELS[t][1]
        pairs.append((top, new.at[0:count]))
    copies = fetch(sems.at[0:2], pairs)

    def store(t, l, value):
        rest[t, l] = value

    levels = [(stop, LEVELS) for _, stop in TOP_LEVELS]
    second_step(levels, old, core, zpair, xe, xo, planes, depths, keep, depth, store)
    pairs = []
    for t, new in enumerate((new_temp, new_salt)):
        span = slice(TOP_LEVELS[t][1], LEVELS)
        pairs.append((rest.at[t, span], new.at[span]))
    copies += fetch(sems.at[2:4], pairs)
    inbound_kernel(0, 0, blocks, sources, targets, fold, panels, own)
    for copy in copies:
        copy.wait()


def final_kernel(dg, gy, gx, own, out):
    total = own[...] + gx[0:64, :] + gy[0:64, :] + dg[0:64, :]
    group = iota((8, 128), 1) // 16
    for c in range(4):
        field = jnp.zeros((8, 128), F32)
        for k in range(8):
            moved = pltpu.roll(total[k * 8 : (k + 1) * 8], (k - c) % 8 * 16, 1)
            field = jnp.where(group == k, moved, field)
        out[c] = field


def call(kernel, shapes, args, scratch=(), hbm_in=(), hbm_out=(), mib=12):
    args = [
        pltpu.with_memory_space_constraint(x, pltpu.HBM) if n in hbm_in else x
        for n, x in enumerate(args)
    ]
    shapes = [s if isinstance(s, jax.ShapeDtypeStruct) else jax.ShapeDtypeStruct(s, F32) for s in shapes]
    return pl.pallas_call(
        kernel,
        out_shape=shapes,
        in_specs=[HBM if n in hbm_in else VMEM for n in range(len(args))],
        out_specs=[HBM if n in hbm_out else VMEM for n in range(len(shapes))],
        scratch_shapes=list(scratch),
        compiler_params=pltpu.CompilerParams(vmem_limit_bytes=mib * 1024 * 1024),
    )(*args)


def send(block, step):
    wide, high = lax.axis_size("gx"), lax.axis_size("gy")
    route = []
    for i in range(wide):
        for j in range(high):
            to = step(i, j)
            route.append((i * high + j, to[0] % wide * high + to[1] % high))
    return lax.ppermute(block, ("gx", "gy"), route)


def pair(n):
    return n - 1 if n % 2 else n + 1


def other_pair(n):
    return n + 1 if n % 2 else n - 1


def row_pair(i, j):
    return (i, other_pair(j)) if 0 <= other_pair(j) < lax.axis_size("gy") else (pair(i), j)


def outbound_shapes(n):
    rows = LIST_ROWS + ROWS
    shapes = [(rows + 8 * (3 - n), 128)]
    return shapes + [(rows, 128)] if FORCING_ORDER[n] == (1, 0) else shapes


def per_device(air, out_tables, out_panels, depth, temp, salt, in_tables, in_panels):
    out_panels = out_panels.reshape(4, 1024, 128)
    in_panels = in_panels.reshape(4, 1024, 128)
    out_tables, in_tables = out_tables[0, 0], in_tables[0, 0]
    field = (2, LEVELS, ROWS, COLS)
    tiled, out_tables, out_panels, temp, salt, depth, *first = call(
        functools.partial(outbound_kernel, FORCING_ORDER[0]),
        [
            jax.ShapeDtypeStruct((64, 1024), BF16),
            jax.ShapeDtypeStruct(out_tables.shape, jnp.int32),
            jax.ShapeDtypeStruct((4, 1024, 128), BF16),
            temp.shape,
            salt.shape,
            jax.ShapeDtypeStruct(depth.shape, jnp.int32),
        ] + outbound_shapes(0),
        [air, out_tables, out_panels, temp, salt, depth],
        [pltpu.VMEM(air.shape, BF16), pltpu.SemaphoreType.DMA((9,))],
        hbm_in=range(6),
    )
    got = {}
    for n, kind in enumerate(FORCING_ORDER):
        blocks = first
        if n:
            blocks = call(
                functools.partial(next_kernel, kind),
                outbound_shapes(n),
                [tiled, out_tables, out_panels, temp, salt, depth],
            )
        if kind == (0, 0):
            got["dg"] = send(blocks[0], lambda i, j: (i - 1, j - 1) if j else (i, j - 1))
        if kind == (0, 1):
            got["gy"] = send(blocks[0], lambda i, j: (i, j - 1))
        if kind == (1, 0):
            got["z"] = send(blocks[0], lambda i, j: (other_pair(i), j))
            got["core"] = send(blocks[1], lambda i, j: (pair(i), j))
    dg, gy, zpair, core = got["dg"], got["gy"], got["z"], got["core"]
    ones = jax.ShapeDtypeStruct((4, 64, 64), BF16)
    own, partial, *maps = call(
        inner_kernel,
        [(LIST_ROWS, 128), field, ones, ones, jax.ShapeDtypeStruct((512, 128), BF16)],
        [tiled, out_tables, out_panels, temp, salt, depth, in_tables],
        [pltpu.VMEM(in_tables.shape, jnp.int32), pltpu.SemaphoreType.DMA],
        hbm_in=(6,),
    )
    base, west, east, depths, partial = call(
        edge_kernel,
        [(LIST_ROWS, 128), (ROWS, 128), (ROWS, 128), (4, ROWS, COLS), field],
        [own, core, zpair, partial, temp, salt, depth],
    )
    stepped, cols, planes = call(
        first_kernel,
        [field, (ROWS, 128), (4, ROWS, COLS)],
        [dg, gy, base, partial, temp, salt, depth],
    )
    row_e, row_o, keep = call(
        rows_kernel,
        [(43, COLS), (48, COLS), (44, COLS)],
        [stepped, temp, salt, depth, west, east],
    )
    xo = send(row_o, row_pair)
    xe = send(row_e, lambda i, j: (i, pair(j)))
    zpair = send(cols, lambda i, j: (other_pair(i), j))
    core = send(cols, lambda i, j: (pair(i), j))
    state = [stepped, core, zpair, xe, xo, planes, depths, keep, depth]
    top_temp, top_salt, blocks, *first = call(
        second_kernel,
        [
            (TOP_LEVELS[0][1], ROWS, COLS),
            (TOP_LEVELS[1][1], ROWS, COLS),
            jax.ShapeDtypeStruct((64, COLS), BF16),
            (80, 128),
        ],
        state + maps + [in_panels],
    )
    got = {}
    for n, kind in enumerate(SURFACE_ORDER):
        block = first
        if n:
            kernel = functools.partial(inbound_kernel, *kind)
            block = call(kernel, [(80 - 8 * n, 128)], [blocks, *maps, in_panels])
        steps = {
            (1, 1): lambda i, j: (i + 1, j + 1) if j + 1 < lax.axis_size("gy") else (i, j + 1),
            (1, 0): lambda i, j: (i, j + 1),
            (0, 1): lambda i, j: (i + 1, j),
        }
        got[kind] = send(block[0], steps[kind])
    dg, gy, gx = got[1, 1], got[1, 0], got[0, 1]
    new_temp, new_salt, own = call(
        outer_kernel,
        [temp.shape, salt.shape, (64, 128)],
        state + [top_temp, top_salt, blocks, *maps, in_panels],
        [pltpu.VMEM(field, F32), pltpu.SemaphoreType.DMA((4,))],
        hbm_out=(0, 1),
    )
    (surface,) = call(final_kernel, [(4, 8, 128)], [dg, gy, gx, own])
    return new_temp, new_salt, surface


def solution(mesh):
    in_specs = (
        P(None, "gy", "gx"),
        P("gy", "gx", None, None, None, None),
        P("gy", "gx", None, None, None, None, None),
        P("gy", "gx"),
        P(None, "gy", "gx"),
        P(None, "gy", "gx"),
        P("gy", "gx", None, None, None, None),
        P("gy", "gx", None, None, None, None, None),
    )
    out_specs = (P(None, "gy", "gx"), P(None, "gy", "gx"), P(None, "gy", "gx"))
    return jax.shard_map(
        per_device, mesh=mesh, in_specs=in_specs, out_specs=out_specs, check_vma=False
    )
```

```python
import jax
import jax.numpy as jnp
from jax import lax
from jax.experimental import pallas as pl
from jax.experimental.pallas import tpu as pltpu
from jax.sharding import PartitionSpec as P

HEAT_RATE = 0.1
SHORTWAVE_RATE = 0.1
FRESH_RATE = 0.05
SIDE_RATE = 0.18
MIX_BASE = 0.03
MIX_WIND = 0.09
MIX_DECAY = 0.8

ROWS, COLS, LEVELS = 16, 512, 10
TILES = COLS // 128
F32, BF16 = jnp.float32, jnp.bfloat16
LIST_ROWS = 4 * 64
TOP_LEVELS = ((0, 3), (0, 1))
VMEM = pl.BlockSpec(memory_space=pltpu.VMEM)
HBM = pl.BlockSpec(memory_space=pltpu.HBM)
NN = (((1,), (0,)), ((), ()))
TN = (((0,), (0,)), ((), ()))
NT = (((1,), (1,)), ((), ()))


def iota(shape, axis):
    return lax.broadcasted_iota(jnp.int32, shape, axis)


def dot(x, y, dims=NN):
    return lax.dot_general(x, y, dims, preferred_element_type=F32)


def dot_split(ones, values):
    high = values.astype(BF16)
    low = (values - high.astype(F32)).astype(BF16)
    return dot(jnp.concatenate([ones, ones], 1), jnp.concatenate([high, low], 0))


def split_dot(values, ones):
    high = values.astype(BF16)
    low = (values - high.astype(F32)).astype(BF16)
    return dot(high, ones) + dot(low, ones)


def ocean_number(shape, axis):
    place = iota(shape, axis)
    return place % ROWS * TILES + place // ROWS


def atm_number(shape, axis):
    place = iota(shape, axis)
    return place % 8 * 8 + place // 8


def one_hot(number, names):
    return jnp.where(number == names, 1.0, 0.0).astype(BF16)


def group_mask():
    return iota((8, 128), 1) // 16 == iota((8, 128), 0)


def edge_columns(levels):
    lane = iota((ROWS, 128), 1)
    block = jnp.zeros((ROWS, 128), F32)
    for at, values in enumerate(levels):
        block = jnp.where(lane == at, values[:, 0:1], block)
        block = jnp.where(lane == 64 + at, values[:, COLS - 1 : COLS], block)
    return block


def spread_air(air, mask):
    fold = (iota((128, 128), 0) % 16 == iota((128, 128), 1) % 16).astype(F32).astype(BF16)
    spread = []
    for c in range(8):
        for r in range(8):
            row = jnp.broadcast_to(air[c, r : r + 1, :].astype(F32), (8, 128))
            spread.append(jnp.where(mask, row, 0.0))
    tiled = dot(jnp.concatenate(spread, 0).astype(BF16), fold).astype(BF16)
    return jnp.concatenate([tiled[c * 64 : (c + 1) * 64] for c in range(8)], 1)


def outbound_lists(kinds, tiled, table, panels, outs):
    mask = group_mask()
    source = iota((64, 64), 0)
    target = ocean_number((64, 64), 0)
    ones = jnp.concatenate([one_hot(source, table[a, b, 0:1, :]) for a, b in kinds], 1)
    picked = dot(ones, tiled, TN)
    pieces = []
    for n, (a, b) in enumerate(kinds):
        planes = [[], [], [], []]
        for g in range(8):
            part = picked[n * 64 + g * 8 : n * 64 + (g + 1) * 8]
            left = [jnp.where(mask, part[:, c * 128 : (c + 1) * 128], 0.0) for c in range(8)]
            piece = dot(
                jnp.concatenate(left, 0).astype(BF16),
                panels[2 * a + b, g * 128 : (g + 1) * 128, :],
            )
            f = [piece[c * 8 : (c + 1) * 8] for c in range(8)]
            planes[0].append(f[0] + f[1] + f[2])
            planes[1].append(f[3])
            planes[2].append(f[4] - f[5] + f[6])
            planes[3].append(f[7])
        pieces.append(jnp.concatenate([jnp.concatenate(p, 0) for p in planes], 1))
    for (a, b), values, places in zip(kinds, pieces, outs):
        summed = dot_split(one_hot(target, table[a, b, 1:2, :]), values)
        for out in places:
            for p in range(4):
                out[p * 64 : (p + 1) * 64, :] = summed[:, p * 128 : (p + 1) * 128]


def fetch(sems, pairs):
    copies = [pltpu.make_async_copy(src, dst, sems.at[n]) for n, (src, dst) in enumerate(pairs)]
    for copy in copies:
        copy.start()
    return copies


def outbound_kernel(
    air_hbm, table_hbm, panels_hbm, temp_hbm, salt_hbm, depth_hbm,
    tiled, table, panels, temp, salt, depth, to_dg, to_z, to_core, to_gy, air, sems,
):
    pairs = [(air_hbm, air), (table_hbm, table)]
    pairs += [(panels_hbm.at[n], panels.at[n]) for n in range(3)]
    pairs += [(temp_hbm, temp), (salt_hbm, salt), (depth_hbm, depth)]
    copies = fetch(sems, pairs + [(panels_hbm.at[3], panels.at[3])])
    for out in (to_dg, to_z, to_gy):
        out[LIST_ROWS:, :] = jnp.zeros((out.shape[0] - LIST_ROWS, 128), F32)
    copies[0].wait()
    tiled[...] = spread_air(air, group_mask())
    for copy in copies[1:8]:
        copy.wait()
    outbound_lists(
        ((0, 0), (1, 0), (0, 1)), tiled[...], table, panels, ((to_dg,), (to_z, to_core), (to_gy,))
    )
    deep = depth[...].astype(F32)
    levels = [temp[l] for l in range(LEVELS)] + [salt[l] for l in range(LEVELS)] + [deep]
    block = edge_columns(levels)
    for out in (to_z, to_core):
        out[LIST_ROWS : LIST_ROWS + ROWS, :] = block
    copies[8].wait()


def beside(values, north, south, west, east):
    row, col = iota((ROWS, COLS), 0), iota((ROWS, COLS), 1)
    return (
        jnp.where(row == 0, north, pltpu.roll(values, 1, 0)),
        jnp.where(row == ROWS - 1, south, pltpu.roll(values, ROWS - 1, 0)),
        jnp.where(col == 0, west, pltpu.roll(values, 1, 1)),
        jnp.where(col == COLS - 1, east, pltpu.roll(values, COLS - 1, 1)),
    )


def side_sum(centre, nears, wets):
    side = jnp.zeros_like(centre)
    for near, there in zip(nears, wets):
        side = side + jnp.where(there, near - centre, 0.0)
    return SIDE_RATE * side


def inner_kernel(
    tiled, table, panels, temp, salt, depth, in_table_hbm, own, partial, sources, targets, fold,
    in_table, sem,
):
    copy = pltpu.make_async_copy(in_table_hbm, in_table, sem)
    copy.start()
    deep = depth[...].astype(F32)
    dry = jnp.zeros((1, 1), F32)
    around = beside(deep, dry, dry, dry, dry)
    for l in range(LEVELS):
        wet = deep > l
        wets = [d > l for d in around]
        for t, field in enumerate((temp, salt)):
            centre = field[l]
            side = side_sum(centre, beside(centre, dry, dry, dry, dry), wets)
            partial[t, l] = centre + jnp.where(wet, side, 0.0)
    outbound_lists(((1, 1),), tiled[...], table, panels, ((own,),))
    copy.wait()
    fold[...] = inbound_fold()
    eye = one_hot(iota((64, 64), 0), iota((64, 64), 1))
    source_block, target = ocean_number((64, 64), 0), atm_number((64, 64), 0)
    for n in range(4):
        ones = one_hot(source_block, in_table[n // 2, n % 2, 0:1, :])
        sources[n] = dot(ones, eye, TN).astype(BF16)
        targets[n] = one_hot(target, in_table[n // 2, n % 2, 1:2, :])


def edge_kernel(own, core, zpair, partial, temp, salt, depth, base, west, east, depths, whole):
    odd_col = lax.axis_index("gx") % 2 == 1
    base[...] = own[...] + jnp.where(
        odd_col, zpair[0:LIST_ROWS, :], core[0:LIST_ROWS, :]
    )
    at = slice(LIST_ROWS, LIST_ROWS + ROWS)
    left = jnp.where(odd_col, core[at, :], zpair[at, :])
    right = jnp.where(odd_col, zpair[at, :], core[at, :])
    west[...] = left
    east[...] = right
    deep = depth[...].astype(F32)
    dry = jnp.zeros((1, 1), F32)
    last = 2 * LEVELS
    around = beside(deep, dry, dry, left[:, 64 + last : 65 + last], right[:, last : last + 1])
    for n in range(4):
        depths[n] = around[n]
    lane = iota((ROWS, 128), 1)
    sides = ((0, left, 64, around[2], 0), (COLS - 128, right, 0, around[3], 127))
    for t, field in enumerate((temp, salt)):
        for l in range(LEVELS):
            at = t * LEVELS + l
            whole[t, l] = partial[t, l]
            for first, halo, offset, far, spot in sides:
                here = (lane == spot) & (far[:, first : first + 128] > l)
                here = here & (deep[:, first : first + 128] > l)
                near = halo[:, offset + at : offset + at + 1] - field[l, :, first : first + 128]
                whole[t, l, :, first : first + 128] += jnp.where(here, SIDE_RATE * near, 0.0)


def column_change(values, below, mixing, depth, l, across):
    change = 0.0 if l == 0 else -across
    if l < LEVELS - 1:
        across = mixing * (MIX_DECAY**l) * (below - values)
        across = jnp.where(depth > l + 1, across, 0.0)
        change = change + across
    return change, across


def source(t, l, planes, values):
    if t == 0:
        heating = planes[1] * (SHORTWAVE_RATE * 2.718281828459045 ** (-0.5 * l))
        return heating + HEAT_RATE * planes[0] if l == 0 else heating
    return -FRESH_RATE * planes[2] * values if l == 0 else 0.0


def first_kernel(
    dg, gy, base, partial, temp, salt, depth, new, cols, planes
):
    forcing = []
    for p in range(4):
        parts = []
        for s in range(TILES):
            at = p * 64 + s * ROWS
            parts.append(base[at : at + ROWS, :] + gy[at : at + ROWS, :] + dg[at : at + ROWS, :])
        forcing.append(jnp.concatenate(parts, 1))
    squared = forcing[3] * forcing[3]
    forcing[3] = squared / (1.0 + squared)
    for p in range(4):
        planes[p] = forcing[p]
    deep = depth[...].astype(F32)
    lane = iota((ROWS, 128), 1)
    mixing = MIX_BASE + MIX_WIND * forcing[3]
    block = jnp.zeros((ROWS, 128), F32)
    for t, field in enumerate((temp, salt)):
        across = None
        for l in range(LEVELS):
            at = t * LEVELS + l
            centre = field[l]
            change, across = column_change(
                centre, field[min(l + 1, LEVELS - 1)], mixing, deep, l, across
            )
            change = change + source(t, l, forcing, centre)
            value = partial[t, l] + jnp.where(deep > l, change, 0.0)
            new[t, l] = value
            block = jnp.where(lane == at, value[:, 0:1], block)
            block = jnp.where(lane == 64 + at, value[:, COLS - 1 : COLS], block)
    cols[...] = block


def rows_kernel(new, temp, salt, depth, west, east, row_e, row_o, keep):
    odd_row = lax.axis_index("gy") % 2 == 1
    deep = depth[...].astype(F32)
    edges = []
    for r in (0, ROWS - 1):
        rows = [new[0, :, r, :], new[1, :, r, :], temp[:, r, :], salt[:, r, :], deep[r : r + 1]]
        edges.append(rows + [west[r : r + 1, :], east[r : r + 1, :]])
    for out, first in ((row_e, odd_row), (row_o, jnp.logical_not(odd_row))):
        at = 0
        for a, b in zip(*edges):
            out[at : at + a.shape[0], 0 : a.shape[1]] = jnp.where(first, a, b)
            at += a.shape[0]
    row_o[43:48, :] = jnp.zeros((5, COLS), F32)
    for n in range(2):
        keep[20 * n : 20 * n + 10, :] = edges[n][2]
        keep[20 * n + 10 : 20 * n + 20, :] = edges[n][3]
        keep[40 + 2 * n : 41 + 2 * n, 0:128] = edges[n][5]
        keep[41 + 2 * n : 42 + 2 * n, 0:128] = edges[n][6]


def inbound_lists(kinds, blocks, sources, targets, fold, panels, outs):
    mask = group_mask()
    numbers = [2 * a + b for a, b in kinds]
    chosen = dot(jnp.concatenate([sources[n] for n in numbers], 0), blocks)
    lists = []
    for m, n in enumerate(numbers):
        kept = [[], [], [], []]
        for g in range(8):
            part = chosen[m * 64 + g * 8 : m * 64 + (g + 1) * 8]
            left = [part[:, c * 128 : (c + 1) * 128] for c in range(4)]
            piece = dot(
                jnp.concatenate(left, 0).astype(BF16), panels[n, g * 128 : (g + 1) * 128, :], NT
            )
            for c in range(4):
                kept[c].append(jnp.where(mask, piece[c * 8 : (c + 1) * 8], 0.0))
        lists.append(jnp.concatenate([jnp.concatenate(k, 0) for k in kept], 1))
    pieces = split_dot(jnp.concatenate(lists, 0), fold)
    for m, (n, out) in enumerate(zip(numbers, outs)):
        out[0:64, :] = dot_split(targets[n], pieces[m * 64 : (m + 1) * 64])
        if out.shape[0] > 64:
            out[64:, :] = jnp.zeros((out.shape[0] - 64, 128), F32)


def inbound_fold():
    place, lane = iota((512, 128), 0), iota((512, 128), 1)
    fold = jnp.where((place // 128 == lane // 16) & (place % 16 == lane % 16), 1.0, 0.0)
    return fold.astype(BF16)


def second_step(levels, old, core, zpair, xe, xo, planes, depths, keep, depth, store):
    odd_col = lax.axis_index("gx") % 2 == 1
    odd_row = lax.axis_index("gy") % 2 == 1
    deep = depth[...].astype(F32)
    row_e, row_o = xe[...], xo[0:43, :]
    beyond = (jnp.where(odd_row, row_e, row_o), jnp.where(odd_row, row_o, row_e))
    level = iota((2 * LEVELS, COLS), 0) % LEVELS
    at_end = (lax.axis_index("gy") == 0, lax.axis_index("gy") == lax.axis_size("gy") - 1)
    beyond_deep = [jnp.where(end, 0.0, other[40:41]) for end, other in zip(at_end, beyond)]
    fixes, halo_rows = [], []
    for n, other in enumerate(beyond):
        r = n * (ROWS - 1)
        here = (deep[r : r + 1] > level) & (beyond_deep[n] > level)
        fix = jnp.where(here, SIDE_RATE * (other[20:40] - keep[20 * n : 20 * n + 20, :]), 0.0)
        fixes.append(fix)
        halo_rows.append(other[0:20] - fix)
    norths, souths = halo_rows
    level = iota((1, 128), 1) % 64 % LEVELS
    row = iota((ROWS, 128), 0)
    ends = []
    for halo, at, deepest in (
        (jnp.where(odd_col, core[...], zpair[...]), 0, 84),
        (jnp.where(odd_col, zpair[...], core[...]), 1, 20),
    ):
        for n, other in enumerate(beyond):
            mine = keep[40 + 2 * n + at : 41 + 2 * n + at, 0:128]
            far = other[41 + at : 42 + at, 0:128]
            here = mine[:, deepest : deepest + 1] > level
            here = here & (jnp.where(at_end[n], 0.0, far[:, deepest : deepest + 1]) > level)
            fix = jnp.where(here, SIDE_RATE * (far - mine), 0.0)
            halo = halo + jnp.where(row == n * (ROWS - 1), fix, 0.0)
        ends.append(halo)
    west, east = ends
    row8, row = iota((8, COLS), 0), iota((ROWS, COLS), 0)
    around = [depths[n] for n in range(4)]
    around[0] = jnp.where(row == 0, beyond_deep[0], around[0])
    around[1] = jnp.where(row == ROWS - 1, beyond_deep[1], around[1])
    forcing = [planes[p] for p in range(4)]
    mixing = MIX_BASE + MIX_WIND * forcing[3]
    def whole(t, l):
        at = t * LEVELS + l
        high = old[t, l, 0:8, :] + jnp.where(row8 == 0, fixes[0][at : at + 1], 0.0)
        low = old[t, l, 8:16, :] + jnp.where(row8 == 7, fixes[1][at : at + 1], 0.0)
        return jnp.concatenate([high, low], 0)

    for t, (start, stop) in enumerate(levels):
        across, centre = None, whole(t, start)
        if start:
            across = mixing * (MIX_DECAY ** (start - 1)) * (centre - whole(t, start - 1))
            across = jnp.where(deep > start, across, 0.0)
        for l in range(start, stop):
            at = t * LEVELS + l
            below = whole(t, l + 1) if l < LEVELS - 1 else None
            change, across = column_change(centre, below, mixing, deep, l, across)
            change = change + source(t, l, forcing, centre)
            nears = beside(
                centre,
                norths[at : at + 1],
                souths[at : at + 1],
                west[:, 64 + at : 65 + at],
                east[:, at : at + 1],
            )
            change = change + side_sum(centre, nears, [d > l for d in around])
            store(t, l, centre + jnp.where(deep > l, change, 0.0))
            centre = below


def second_kernel(
    old, core, zpair, xe, xo, planes, depths, keep, depth, sources, targets, fold, panels,
    top_temp, top_salt, surface_blocks, to_dg, to_gy, to_gx,
):
    top = {}

    def store(t, l, value):
        (top_temp, top_salt)[t][l] = value
        top[t, l] = value

    second_step(TOP_LEVELS, old, core, zpair, xe, xo, planes, depths, keep, depth, store)
    deep = depth[...].astype(F32)
    wet_top = jnp.where(deep > 0, 1.0, 0.0)
    surface = (
        top[0, 0] * wet_top,
        top[1, 0] * wet_top,
        (top[0, 0] + top[0, 1] + top[0, 2]) / 3.0 * wet_top,
        wet_top,
    )
    parts = []
    for f in surface:
        parts.append(jnp.concatenate([f[:, s * 128 : (s + 1) * 128] for s in range(TILES)], 0))
    blocks = jnp.concatenate(parts, 1).astype(BF16)
    surface_blocks[...] = blocks
    kinds, outs = ((1, 1), (1, 0), (0, 1)), (to_dg, to_gy, to_gx)
    inbound_lists(kinds, blocks, sources, targets, fold[...], panels, outs)


def outer_kernel(
    old, core, zpair, xe, xo, planes, depths, keep, depth, top_temp, top_salt,
    blocks, sources, targets, fold, panels, new_temp, new_salt, own, rest, sems,
):
    pairs = []
    for t, (top, new) in enumerate(((top_temp, new_temp), (top_salt, new_salt))):
        count = TOP_LEVELS[t][1]
        pairs.append((top, new.at[0:count]))
    copies = fetch(sems.at[0:2], pairs)

    def store(t, l, value):
        rest[t, l] = value

    levels = [(stop, LEVELS) for _, stop in TOP_LEVELS]
    second_step(levels, old, core, zpair, xe, xo, planes, depths, keep, depth, store)
    pairs = []
    for t, new in enumerate((new_temp, new_salt)):
        span = slice(TOP_LEVELS[t][1], LEVELS)
        pairs.append((rest.at[t, span], new.at[span]))
    copies += fetch(sems.at[2:4], pairs)
    inbound_lists(((0, 0),), blocks[...], sources, targets, fold[...], panels, (own,))
    for copy in copies:
        copy.wait()


def final_kernel(dg, gy, gx, own, out):
    total = own[...] + gx[0:64, :] + gy[0:64, :] + dg[0:64, :]
    group = iota((8, 128), 1) // 16
    for c in range(4):
        field = jnp.zeros((8, 128), F32)
        for k in range(8):
            moved = pltpu.roll(total[k * 8 : (k + 1) * 8], (k - c) % 8 * 16, 1)
            field = jnp.where(group == k, moved, field)
        out[c] = field


def call(kernel, shapes, args, scratch=(), hbm_in=(), hbm_out=(), mib=12):
    args = [
        pltpu.with_memory_space_constraint(x, pltpu.HBM) if n in hbm_in else x
        for n, x in enumerate(args)
    ]
    shapes = [s if isinstance(s, jax.ShapeDtypeStruct) else jax.ShapeDtypeStruct(s, F32) for s in shapes]
    return pl.pallas_call(
        kernel,
        out_shape=shapes,
        in_specs=[HBM if n in hbm_in else VMEM for n in range(len(args))],
        out_specs=[HBM if n in hbm_out else VMEM for n in range(len(shapes))],
        scratch_shapes=list(scratch),
        compiler_params=pltpu.CompilerParams(vmem_limit_bytes=mib * 1024 * 1024),
    )(*args)


def send(block, step):
    wide, high = lax.axis_size("gx"), lax.axis_size("gy")
    route = []
    for i in range(wide):
        for j in range(high):
            to = step(i, j)
            route.append((i * high + j, to[0] % wide * high + to[1] % high))
    return lax.ppermute(block, ("gx", "gy"), route)


def pair(n):
    return n - 1 if n % 2 else n + 1


def other_pair(n):
    return n + 1 if n % 2 else n - 1


def row_pair(i, j):
    return (i, other_pair(j)) if 0 <= other_pair(j) < lax.axis_size("gy") else (pair(i), j)


def per_device(air, out_tables, out_panels, depth, temp, salt, in_tables, in_panels):
    out_panels = out_panels.reshape(4, 1024, 128)
    in_panels = in_panels.reshape(4, 1024, 128)
    out_tables, in_tables = out_tables[0, 0], in_tables[0, 0]
    field = (2, LEVELS, ROWS, COLS)
    rows = LIST_ROWS + ROWS
    tiled, out_tables, out_panels, temp, salt, depth, to_dg, to_z, to_core, to_gy = call(
        outbound_kernel,
        [
            jax.ShapeDtypeStruct((64, 1024), BF16),
            jax.ShapeDtypeStruct(out_tables.shape, jnp.int32),
            jax.ShapeDtypeStruct((4, 1024, 128), BF16),
            temp.shape,
            salt.shape,
            jax.ShapeDtypeStruct(depth.shape, jnp.int32),
            (rows + 24, 128),
            (rows + 16, 128),
            (rows, 128),
            (rows + 8, 128),
        ],
        [air, out_tables, out_panels, temp, salt, depth],
        [pltpu.VMEM(air.shape, BF16), pltpu.SemaphoreType.DMA((9,))],
        hbm_in=range(6),
    )
    dg = send(to_dg, lambda i, j: (i - 1, j - 1) if j else (i, j - 1))
    zpair = send(to_z, lambda i, j: (other_pair(i), j))
    gy = send(to_gy, lambda i, j: (i, j - 1))
    core = send(to_core, lambda i, j: (pair(i), j))
    ones = jax.ShapeDtypeStruct((4, 64, 64), BF16)
    own, partial, *maps = call(
        inner_kernel,
        [(LIST_ROWS, 128), field, ones, ones, jax.ShapeDtypeStruct((512, 128), BF16)],
        [tiled, out_tables, out_panels, temp, salt, depth, in_tables],
        [pltpu.VMEM(in_tables.shape, jnp.int32), pltpu.SemaphoreType.DMA],
        hbm_in=(6,),
    )
    base, west, east, depths, partial = call(
        edge_kernel,
        [(LIST_ROWS, 128), (ROWS, 128), (ROWS, 128), (4, ROWS, COLS), field],
        [own, core, zpair, partial, temp, salt, depth],
    )
    stepped, cols, planes = call(
        first_kernel,
        [field, (ROWS, 128), (4, ROWS, COLS)],
        [dg, gy, base, partial, temp, salt, depth],
    )
    row_e, row_o, keep = call(
        rows_kernel,
        [(43, COLS), (48, COLS), (44, COLS)],
        [stepped, temp, salt, depth, west, east],
    )
    xo = send(row_o, row_pair)
    xe = send(row_e, lambda i, j: (i, pair(j)))
    zpair = send(cols, lambda i, j: (other_pair(i), j))
    core = send(cols, lambda i, j: (pair(i), j))
    state = [stepped, core, zpair, xe, xo, planes, depths, keep, depth]
    top_temp, top_salt, blocks, to_dg, to_gy, to_gx = call(
        second_kernel,
        [
            (TOP_LEVELS[0][1], ROWS, COLS),
            (TOP_LEVELS[1][1], ROWS, COLS),
            jax.ShapeDtypeStruct((64, COLS), BF16),
            (80, 128),
            (72, 128),
            (64, 128),
        ],
        state + maps + [in_panels],
    )
    dg = send(to_dg, lambda i, j: (i + 1, j + 1) if j + 1 < lax.axis_size("gy") else (i, j + 1))
    gy = send(to_gy, lambda i, j: (i, j + 1))
    gx = send(to_gx, lambda i, j: (i + 1, j))
    new_temp, new_salt, own = call(
        outer_kernel,
        [temp.shape, salt.shape, (64, 128)],
        state + [top_temp, top_salt, blocks, *maps, in_panels],
        [pltpu.VMEM(field, F32), pltpu.SemaphoreType.DMA((4,))],
        hbm_out=(0, 1),
    )
    (surface,) = call(final_kernel, [(4, 8, 128)], [dg, gy, gx, own])
    return new_temp, new_salt, surface


def solution(mesh):
    in_specs = (
        P(None, "gy", "gx"),
        P("gy", "gx", None, None, None, None),
        P("gy", "gx", None, None, None, None, None),
        P("gy", "gx"),
        P(None, "gy", "gx"),
        P(None, "gy", "gx"),
        P("gy", "gx", None, None, None, None),
        P("gy", "gx", None, None, None, None, None),
    )
    out_specs = (P(None, "gy", "gx"), P(None, "gy", "gx"), P(None, "gy", "gx"))
    return jax.shard_map(
        per_device, mesh=mesh, in_specs=in_specs, out_specs=out_specs, check_vma=False
    )
```

```python
import jax
import jax.numpy as jnp
from jax import lax
from jax.experimental import pallas as pl
from jax.experimental.pallas import tpu as pltpu
from jax.sharding import PartitionSpec as P

HEAT_RATE = 0.1
SHORTWAVE_RATE = 0.1
FRESH_RATE = 0.05
SIDE_RATE = 0.18
MIX_BASE = 0.03
MIX_WIND = 0.09
MIX_DECAY = 0.8

ROWS, COLS, LEVELS = 16, 512, 10
TILES = COLS // 128
F32, BF16 = jnp.float32, jnp.bfloat16
LIST_ROWS = 4 * 64
TOP_LEVELS = ((0, 3), (0, 1))
VMEM = pl.BlockSpec(memory_space=pltpu.VMEM)
HBM = pl.BlockSpec(memory_space=pltpu.HBM)
NN = (((1,), (0,)), ((), ()))
TN = (((0,), (0,)), ((), ()))
NT = (((1,), (1,)), ((), ()))


def iota(shape, axis):
    return lax.broadcasted_iota(jnp.int32, shape, axis)


def dot(x, y, dims=NN):
    return lax.dot_general(x, y, dims, preferred_element_type=F32)


def dot_split(ones, values):
    high = values.astype(BF16)
    low = (values - high.astype(F32)).astype(BF16)
    return dot(jnp.concatenate([ones, ones], 1), jnp.concatenate([high, low], 0))


def split_dot(values, ones):
    high = values.astype(BF16)
    low = (values - high.astype(F32)).astype(BF16)
    return dot(high, ones) + dot(low, ones)


def ocean_number(shape, axis):
    place = iota(shape, axis)
    return place % ROWS * TILES + place // ROWS


def atm_number(shape, axis):
    place = iota(shape, axis)
    return place % 8 * 8 + place // 8


def one_hot(number, names):
    return jnp.where(number == names, 1.0, 0.0).astype(BF16)


def group_mask():
    return iota((8, 128), 1) // 16 == iota((8, 128), 0)


def edge_columns(levels):
    lane = iota((ROWS, 128), 1)
    block = jnp.zeros((ROWS, 128), F32)
    for at, values in enumerate(levels):
        block = jnp.where(lane == at, values[:, 0:1], block)
        block = jnp.where(lane == 64 + at, values[:, COLS - 1 : COLS], block)
    return block


def spread_air(air, mask):
    fold = (iota((128, 128), 0) % 16 == iota((128, 128), 1) % 16).astype(F32).astype(BF16)
    spread = []
    for c in range(8):
        for r in range(8):
            row = jnp.broadcast_to(air[c, r : r + 1, :].astype(F32), (8, 128))
            spread.append(jnp.where(mask, row, 0.0))
    tiled = dot(jnp.concatenate(spread, 0).astype(BF16), fold).astype(BF16)
    return jnp.concatenate([tiled[c * 64 : (c + 1) * 64] for c in range(8)], 1)


def outbound_lists(kinds, tiled, table, panels, outs, wait=lambda: None):
    mask = group_mask()
    source = iota((64, 64), 0)
    target = ocean_number((64, 64), 0)
    ones = jnp.concatenate([one_hot(source, table[a, b, 0:1, :]) for a, b in kinds], 1)
    picked = dot(ones, tiled, TN)
    wait()
    pieces = []
    for n, (a, b) in enumerate(kinds):
        planes = [[], [], [], []]
        for g in range(8):
            part = picked[n * 64 + g * 8 : n * 64 + (g + 1) * 8]
            left = [jnp.where(mask, part[:, c * 128 : (c + 1) * 128], 0.0) for c in range(8)]
            piece = dot(
                jnp.concatenate(left, 0).astype(BF16),
                panels[2 * a + b, g * 128 : (g + 1) * 128, :],
            )
            f = [piece[c * 8 : (c + 1) * 8] for c in range(8)]
            planes[0].append(f[0] + f[1] + f[2])
            planes[1].append(f[3])
            planes[2].append(f[4] - f[5] + f[6])
            planes[3].append(f[7])
        pieces.append(jnp.concatenate([jnp.concatenate(p, 0) for p in planes], 1))
    for (a, b), values, places in zip(kinds, pieces, outs):
        summed = dot_split(one_hot(target, table[a, b, 1:2, :]), values)
        for out in places:
            for p in range(4):
                out[p * 64 : (p + 1) * 64, :] = summed[:, p * 128 : (p + 1) * 128]


def fetch(sems, pairs):
    copies = [pltpu.make_async_copy(src, dst, sems.at[n]) for n, (src, dst) in enumerate(pairs)]
    for copy in copies:
        copy.start()
    return copies


def outbound_kernel(
    air_hbm, table_hbm, panels_hbm, temp_hbm, salt_hbm, depth_hbm,
    tiled, table, panels, temp, salt, depth, to_dg, to_z, to_core, to_gy, air, sems,
):
    pairs = [(air_hbm, air), (table_hbm, table)]
    pairs += [(panels_hbm.at[n], panels.at[n]) for n in range(3)]
    pairs += [(temp_hbm, temp), (salt_hbm, salt), (depth_hbm, depth)]
    copies = fetch(sems, pairs + [(panels_hbm.at[3], panels.at[3])])
    for out in (to_dg, to_z, to_gy):
        out[LIST_ROWS:, :] = jnp.zeros((out.shape[0] - LIST_ROWS, 128), F32)

    def rest():
        for copy in copies[2:8]:
            copy.wait()
        deep = depth[...].astype(F32)
        levels = [temp[l] for l in range(LEVELS)] + [salt[l] for l in range(LEVELS)] + [deep]
        block = edge_columns(levels)
        for out in (to_z, to_core):
            out[LIST_ROWS : LIST_ROWS + ROWS, :] = block

    copies[0].wait()
    spread = spread_air(air, group_mask())
    tiled[...] = spread
    copies[1].wait()
    kinds, outs = ((0, 0), (1, 0), (0, 1)), ((to_dg,), (to_z, to_core), (to_gy,))
    outbound_lists(kinds, spread, table, panels, outs, rest)
    copies[8].wait()


def beside(values, north, south, west, east):
    row, col = iota((ROWS, COLS), 0), iota((ROWS, COLS), 1)
    return (
        jnp.where(row == 0, north, pltpu.roll(values, 1, 0)),
        jnp.where(row == ROWS - 1, south, pltpu.roll(values, ROWS - 1, 0)),
        jnp.where(col == 0, west, pltpu.roll(values, 1, 1)),
        jnp.where(col == COLS - 1, east, pltpu.roll(values, COLS - 1, 1)),
    )


def side_sum(centre, nears, wets):
    side = jnp.zeros_like(centre)
    for near, there in zip(nears, wets):
        side = side + jnp.where(there, near - centre, 0.0)
    return SIDE_RATE * side


def inner_kernel(
    tiled, table, panels, temp, salt, depth, in_table_hbm, own, partial, sources, targets, fold,
    in_table, sem,
):
    copy = pltpu.make_async_copy(in_table_hbm, in_table, sem)
    copy.start()
    deep = depth[...].astype(F32)
    dry = jnp.zeros((1, 1), F32)
    around = beside(deep, dry, dry, dry, dry)
    for l in range(LEVELS):
        wet = deep > l
        wets = [d > l for d in around]
        for t, field in enumerate((temp, salt)):
            centre = field[l]
            side = side_sum(centre, beside(centre, dry, dry, dry, dry), wets)
            partial[t, l] = centre + jnp.where(wet, side, 0.0)
    outbound_lists(((1, 1),), tiled[...], table, panels, ((own,),))
    copy.wait()
    fold[...] = inbound_fold()
    eye = one_hot(iota((64, 64), 0), iota((64, 64), 1))
    source_block, target = ocean_number((64, 64), 0), atm_number((64, 64), 0)
    for n in range(4):
        ones = one_hot(source_block, in_table[n // 2, n % 2, 0:1, :])
        sources[n] = dot(ones, eye, TN).astype(BF16)
        targets[n] = one_hot(target, in_table[n // 2, n % 2, 1:2, :])


def edge_kernel(own, core, zpair, partial, temp, salt, depth, base, west, east, depths, whole):
    odd_col = lax.axis_index("gx") % 2 == 1
    base[...] = own[...] + jnp.where(
        odd_col, zpair[0:LIST_ROWS, :], core[0:LIST_ROWS, :]
    )
    at = slice(LIST_ROWS, LIST_ROWS + ROWS)
    left = jnp.where(odd_col, core[at, :], zpair[at, :])
    right = jnp.where(odd_col, zpair[at, :], core[at, :])
    west[...] = left
    east[...] = right
    deep = depth[...].astype(F32)
    dry = jnp.zeros((1, 1), F32)
    last = 2 * LEVELS
    around = beside(deep, dry, dry, left[:, 64 + last : 65 + last], right[:, last : last + 1])
    for n in range(4):
        depths[n] = around[n]
    lane = iota((ROWS, 128), 1)
    sides = ((0, left, 64, around[2], 0), (COLS - 128, right, 0, around[3], 127))
    for t, field in enumerate((temp, salt)):
        for l in range(LEVELS):
            at = t * LEVELS + l
            whole[t, l] = partial[t, l]
            for first, halo, offset, far, spot in sides:
                here = (lane == spot) & (far[:, first : first + 128] > l)
                here = here & (deep[:, first : first + 128] > l)
                near = halo[:, offset + at : offset + at + 1] - field[l, :, first : first + 128]
                whole[t, l, :, first : first + 128] += jnp.where(here, SIDE_RATE * near, 0.0)


def column_change(values, below, mixing, depth, l, across):
    change = 0.0 if l == 0 else -across
    if l < LEVELS - 1:
        across = mixing * (MIX_DECAY**l) * (below - values)
        across = jnp.where(depth > l + 1, across, 0.0)
        change = change + across
    return change, across


def source(t, l, planes, values):
    if t == 0:
        heating = planes[1] * (SHORTWAVE_RATE * 2.718281828459045 ** (-0.5 * l))
        return heating + HEAT_RATE * planes[0] if l == 0 else heating
    return -FRESH_RATE * planes[2] * values if l == 0 else 0.0


def first_kernel(
    dg, gy, base, partial, temp, salt, depth, new, cols, planes
):
    forcing = []
    for p in range(4):
        parts = []
        for s in range(TILES):
            at = p * 64 + s * ROWS
            parts.append(base[at : at + ROWS, :] + gy[at : at + ROWS, :] + dg[at : at + ROWS, :])
        forcing.append(jnp.concatenate(parts, 1))
    squared = forcing[3] * forcing[3]
    forcing[3] = squared / (1.0 + squared)
    for p in range(4):
        planes[p] = forcing[p]
    deep = depth[...].astype(F32)
    lane = iota((ROWS, 128), 1)
    mixing = MIX_BASE + MIX_WIND * forcing[3]
    block = jnp.zeros((ROWS, 128), F32)
    for t, field in enumerate((temp, salt)):
        across = None
        for l in range(LEVELS):
            at = t * LEVELS + l
            centre = field[l]
            change, across = column_change(
                centre, field[min(l + 1, LEVELS - 1)], mixing, deep, l, across
            )
            change = change + source(t, l, forcing, centre)
            value = partial[t, l] + jnp.where(deep > l, change, 0.0)
            new[t, l] = value
            block = jnp.where(lane == at, value[:, 0:1], block)
            block = jnp.where(lane == 64 + at, value[:, COLS - 1 : COLS], block)
    cols[...] = block


def rows_kernel(new, temp, salt, depth, west, east, row_e, row_o, keep):
    odd_row = lax.axis_index("gy") % 2 == 1
    deep = depth[...].astype(F32)
    edges = []
    for r in (0, ROWS - 1):
        rows = [new[0, :, r, :], new[1, :, r, :], temp[:, r, :], salt[:, r, :], deep[r : r + 1]]
        edges.append(rows + [west[r : r + 1, :], east[r : r + 1, :]])
    for out, first in ((row_e, odd_row), (row_o, jnp.logical_not(odd_row))):
        at = 0
        for a, b in zip(*edges):
            out[at : at + a.shape[0], 0 : a.shape[1]] = jnp.where(first, a, b)
            at += a.shape[0]
    row_e[43:48, :] = jnp.zeros((5, COLS), F32)
    for n in range(2):
        keep[20 * n : 20 * n + 10, :] = edges[n][2]
        keep[20 * n + 10 : 20 * n + 20, :] = edges[n][3]
        keep[40 + 2 * n : 41 + 2 * n, 0:128] = edges[n][5]
        keep[41 + 2 * n : 42 + 2 * n, 0:128] = edges[n][6]


def inbound_lists(kinds, blocks, sources, targets, fold, panels, outs):
    mask = group_mask()
    numbers = [2 * a + b for a, b in kinds]
    chosen = dot(jnp.concatenate([sources[n] for n in numbers], 0), blocks)
    lists = []
    for m, n in enumerate(numbers):
        kept = [[], [], [], []]
        for g in range(8):
            part = chosen[m * 64 + g * 8 : m * 64 + (g + 1) * 8]
            left = [part[:, c * 128 : (c + 1) * 128] for c in range(4)]
            piece = dot(
                jnp.concatenate(left, 0).astype(BF16), panels[n, g * 128 : (g + 1) * 128, :], NT
            )
            for c in range(4):
                kept[c].append(jnp.where(mask, piece[c * 8 : (c + 1) * 8], 0.0))
        lists.append(jnp.concatenate([jnp.concatenate(k, 0) for k in kept], 1))
    pieces = split_dot(jnp.concatenate(lists, 0), fold)
    for m, (n, out) in enumerate(zip(numbers, outs)):
        out[0:64, :] = dot_split(targets[n], pieces[m * 64 : (m + 1) * 64])
        if out.shape[0] > 64:
            out[64:, :] = jnp.zeros((out.shape[0] - 64, 128), F32)


def inbound_fold():
    place, lane = iota((512, 128), 0), iota((512, 128), 1)
    fold = jnp.where((place // 128 == lane // 16) & (place % 16 == lane % 16), 1.0, 0.0)
    return fold.astype(BF16)


def second_step(levels, old, core, zpair, xe, xo, planes, depths, keep, depth, store):
    odd_col = lax.axis_index("gx") % 2 == 1
    odd_row = lax.axis_index("gy") % 2 == 1
    deep = depth[...].astype(F32)
    row_e, row_o = xe[0:43, :], xo[...]
    beyond = (jnp.where(odd_row, row_e, row_o), jnp.where(odd_row, row_o, row_e))
    level = iota((2 * LEVELS, COLS), 0) % LEVELS
    at_end = (lax.axis_index("gy") == 0, lax.axis_index("gy") == lax.axis_size("gy") - 1)
    beyond_deep = [jnp.where(end, 0.0, other[40:41]) for end, other in zip(at_end, beyond)]
    fixes, halo_rows = [], []
    for n, other in enumerate(beyond):
        r = n * (ROWS - 1)
        here = (deep[r : r + 1] > level) & (beyond_deep[n] > level)
        fix = jnp.where(here, SIDE_RATE * (other[20:40] - keep[20 * n : 20 * n + 20, :]), 0.0)
        fixes.append(fix)
        halo_rows.append(other[0:20] - fix)
    norths, souths = halo_rows
    level = iota((1, 128), 1) % 64 % LEVELS
    row = iota((ROWS, 128), 0)
    ends = []
    for halo, at, deepest in (
        (jnp.where(odd_col, core[...], zpair[...]), 0, 84),
        (jnp.where(odd_col, zpair[...], core[...]), 1, 20),
    ):
        for n, other in enumerate(beyond):
            mine = keep[40 + 2 * n + at : 41 + 2 * n + at, 0:128]
            far = other[41 + at : 42 + at, 0:128]
            here = mine[:, deepest : deepest + 1] > level
            here = here & (jnp.where(at_end[n], 0.0, far[:, deepest : deepest + 1]) > level)
            fix = jnp.where(here, SIDE_RATE * (far - mine), 0.0)
            halo = halo + jnp.where(row == n * (ROWS - 1), fix, 0.0)
        ends.append(halo)
    west, east = ends
    row8, row = iota((8, COLS), 0), iota((ROWS, COLS), 0)
    around = [depths[n] for n in range(4)]
    around[0] = jnp.where(row == 0, beyond_deep[0], around[0])
    around[1] = jnp.where(row == ROWS - 1, beyond_deep[1], around[1])
    forcing = [planes[p] for p in range(4)]
    mixing = MIX_BASE + MIX_WIND * forcing[3]
    def whole(t, l):
        at = t * LEVELS + l
        high = old[t, l, 0:8, :] + jnp.where(row8 == 0, fixes[0][at : at + 1], 0.0)
        low = old[t, l, 8:16, :] + jnp.where(row8 == 7, fixes[1][at : at + 1], 0.0)
        return jnp.concatenate([high, low], 0)

    for t, (start, stop) in enumerate(levels):
        across, centre = None, whole(t, start)
        if start:
            across = mixing * (MIX_DECAY ** (start - 1)) * (centre - whole(t, start - 1))
            across = jnp.where(deep > start, across, 0.0)
        for l in range(start, stop):
            at = t * LEVELS + l
            below = whole(t, l + 1) if l < LEVELS - 1 else None
            change, across = column_change(centre, below, mixing, deep, l, across)
            change = change + source(t, l, forcing, centre)
            nears = beside(
                centre,
                norths[at : at + 1],
                souths[at : at + 1],
                west[:, 64 + at : 65 + at],
                east[:, at : at + 1],
            )
            change = change + side_sum(centre, nears, [d > l for d in around])
            store(t, l, centre + jnp.where(deep > l, change, 0.0))
            centre = below


def second_kernel(
    old, core, zpair, xe, xo, planes, depths, keep, depth, sources, targets, fold, panels,
    top_temp, top_salt, surface_blocks, to_dg, to_gy, to_gx,
):
    top = {}

    def store(t, l, value):
        (top_temp, top_salt)[t][l] = value
        top[t, l] = value

    second_step(TOP_LEVELS, old, core, zpair, xe, xo, planes, depths, keep, depth, store)
    deep = depth[...].astype(F32)
    wet_top = jnp.where(deep > 0, 1.0, 0.0)
    surface = (
        top[0, 0] * wet_top,
        top[1, 0] * wet_top,
        (top[0, 0] + top[0, 1] + top[0, 2]) / 3.0 * wet_top,
        wet_top,
    )
    parts = []
    for f in surface:
        parts.append(jnp.concatenate([f[:, s * 128 : (s + 1) * 128] for s in range(TILES)], 0))
    blocks = jnp.concatenate(parts, 1).astype(BF16)
    surface_blocks[...] = blocks
    kinds, outs = ((1, 1), (1, 0), (0, 1)), (to_dg, to_gy, to_gx)
    inbound_lists(kinds, blocks, sources, targets, fold[...], panels, outs)


def outer_kernel(
    old, core, zpair, xe, xo, planes, depths, keep, depth, top_temp, top_salt,
    blocks, sources, targets, fold, panels, new_temp, new_salt, own, rest, sems,
):
    pairs = []
    for t, (top, new) in enumerate(((top_temp, new_temp), (top_salt, new_salt))):
        count = TOP_LEVELS[t][1]
        pairs.append((top, new.at[0:count]))
    copies = fetch(sems.at[0:2], pairs)

    def store(t, l, value):
        rest[t, l] = value

    levels = [(stop, LEVELS) for _, stop in TOP_LEVELS]
    second_step(levels, old, core, zpair, xe, xo, planes, depths, keep, depth, store)
    pairs = []
    for t, new in enumerate((new_temp, new_salt)):
        span = slice(TOP_LEVELS[t][1], LEVELS)
        pairs.append((rest.at[t, span], new.at[span]))
    copies += fetch(sems.at[2:4], pairs)
    inbound_lists(((0, 0),), blocks[...], sources, targets, fold[...], panels, (own,))
    for copy in copies:
        copy.wait()


def final_kernel(dg, gy, gx, own, out):
    total = own[...] + gx[0:64, :] + gy[0:64, :] + dg[0:64, :]
    group = iota((8, 128), 1) // 16
    for c in range(4):
        field = jnp.zeros((8, 128), F32)
        for k in range(8):
            moved = pltpu.roll(total[k * 8 : (k + 1) * 8], (k - c) % 8 * 16, 1)
            field = jnp.where(group == k, moved, field)
        out[c] = field


def call(kernel, shapes, args, scratch=(), hbm_in=(), hbm_out=(), mib=12):
    args = [
        pltpu.with_memory_space_constraint(x, pltpu.HBM) if n in hbm_in else x
        for n, x in enumerate(args)
    ]
    shapes = [s if isinstance(s, jax.ShapeDtypeStruct) else jax.ShapeDtypeStruct(s, F32) for s in shapes]
    return pl.pallas_call(
        kernel,
        out_shape=shapes,
        in_specs=[HBM if n in hbm_in else VMEM for n in range(len(args))],
        out_specs=[HBM if n in hbm_out else VMEM for n in range(len(shapes))],
        scratch_shapes=list(scratch),
        compiler_params=pltpu.CompilerParams(vmem_limit_bytes=mib * 1024 * 1024),
    )(*args)


def send(block, step):
    wide, high = lax.axis_size("gx"), lax.axis_size("gy")
    route = []
    for i in range(wide):
        for j in range(high):
            to = step(i, j)
            route.append((i * high + j, to[0] % wide * high + to[1] % high))
    return lax.ppermute(block, ("gx", "gy"), route)


def pair(n):
    return n - 1 if n % 2 else n + 1


def other_pair(n):
    return n + 1 if n % 2 else n - 1


def row_pair(i, j):
    return (i, other_pair(j)) if 0 <= other_pair(j) < lax.axis_size("gy") else (pair(i), j)


def per_device(air, out_tables, out_panels, depth, temp, salt, in_tables, in_panels):
    out_panels = out_panels.reshape(4, 1024, 128)
    in_panels = in_panels.reshape(4, 1024, 128)
    out_tables, in_tables = out_tables[0, 0], in_tables[0, 0]
    field = (2, LEVELS, ROWS, COLS)
    rows = LIST_ROWS + ROWS
    tiled, out_tables, out_panels, temp, salt, depth, to_dg, to_z, to_core, to_gy = call(
        outbound_kernel,
        [
            jax.ShapeDtypeStruct((64, 1024), BF16),
            jax.ShapeDtypeStruct(out_tables.shape, jnp.int32),
            jax.ShapeDtypeStruct((4, 1024, 128), BF16),
            temp.shape,
            salt.shape,
            jax.ShapeDtypeStruct(depth.shape, jnp.int32),
            (rows + 24, 128),
            (rows + 16, 128),
            (rows, 128),
            (rows + 8, 128),
        ],
        [air, out_tables, out_panels, temp, salt, depth],
        [pltpu.VMEM(air.shape, BF16), pltpu.SemaphoreType.DMA((9,))],
        hbm_in=range(6),
    )
    dg = send(to_dg, lambda i, j: (i - 1, j - 1) if j else (i, j - 1))
    zpair = send(to_z, lambda i, j: (other_pair(i), j))
    gy = send(to_gy, lambda i, j: (i, j - 1))
    core = send(to_core, lambda i, j: (pair(i), j))
    ones = jax.ShapeDtypeStruct((4, 64, 64), BF16)
    own, partial, *maps = call(
        inner_kernel,
        [(LIST_ROWS, 128), field, ones, ones, jax.ShapeDtypeStruct((512, 128), BF16)],
        [tiled, out_tables, out_panels, temp, salt, depth, in_tables],
        [pltpu.VMEM(in_tables.shape, jnp.int32), pltpu.SemaphoreType.DMA],
        hbm_in=(6,),
    )
    base, west, east, depths, partial = call(
        edge_kernel,
        [(LIST_ROWS, 128), (ROWS, 128), (ROWS, 128), (4, ROWS, COLS), field],
        [own, core, zpair, partial, temp, salt, depth],
    )
    stepped, cols, planes = call(
        first_kernel,
        [field, (ROWS, 128), (4, ROWS, COLS)],
        [dg, gy, base, partial, temp, salt, depth],
    )
    row_e, row_o, keep = call(
        rows_kernel,
        [(48, COLS), (43, COLS), (44, COLS)],
        [stepped, temp, salt, depth, west, east],
    )
    xo = send(row_o, row_pair)
    xe = send(row_e, lambda i, j: (i, pair(j)))
    zpair = send(cols, lambda i, j: (other_pair(i), j))
    core = send(cols, lambda i, j: (pair(i), j))
    state = [stepped, core, zpair, xe, xo, planes, depths, keep, depth]
    top_temp, top_salt, blocks, to_dg, to_gy, to_gx = call(
        second_kernel,
        [
            (TOP_LEVELS[0][1], ROWS, COLS),
            (TOP_LEVELS[1][1], ROWS, COLS),
            jax.ShapeDtypeStruct((64, COLS), BF16),
            (80, 128),
            (72, 128),
            (64, 128),
        ],
        state + maps + [in_panels],
    )
    dg = send(to_dg, lambda i, j: (i + 1, j + 1) if j + 1 < lax.axis_size("gy") else (i, j + 1))
    gy = send(to_gy, lambda i, j: (i, j + 1))
    gx = send(to_gx, lambda i, j: (i + 1, j))
    new_temp, new_salt, own = call(
        outer_kernel,
        [temp.shape, salt.shape, (64, 128)],
        state + [top_temp, top_salt, blocks, *maps, in_panels],
        [pltpu.VMEM(field, F32), pltpu.SemaphoreType.DMA((4,))],
        hbm_out=(0, 1),
    )
    (surface,) = call(final_kernel, [(4, 8, 128)], [dg, gy, gx, own])
    return new_temp, new_salt, surface


def solution(mesh):
    in_specs = (
        P(None, "gy", "gx"),
        P("gy", "gx", None, None, None, None),
        P("gy", "gx", None, None, None, None, None),
        P("gy", "gx"),
        P(None, "gy", "gx"),
        P(None, "gy", "gx"),
        P("gy", "gx", None, None, None, None),
        P("gy", "gx", None, None, None, None, None),
    )
    out_specs = (P(None, "gy", "gx"), P(None, "gy", "gx"), P(None, "gy", "gx"))
    return jax.shard_map(
        per_device, mesh=mesh, in_specs=in_specs, out_specs=out_specs, check_vma=False
    )
```

```python
import jax
import jax.numpy as jnp
from jax import lax
from jax.experimental import pallas as pl
from jax.experimental.pallas import tpu as pltpu
from jax.sharding import PartitionSpec as P

HEAT_RATE = 0.1
SHORTWAVE_RATE = 0.1
FRESH_RATE = 0.05
SIDE_RATE = 0.18
MIX_BASE = 0.03
MIX_WIND = 0.09
MIX_DECAY = 0.8

ROWS, COLS, LEVELS = 16, 512, 10
TILES = COLS // 128
F32, BF16 = jnp.float32, jnp.bfloat16
LIST_ROWS = 4 * 64
TOP_LEVELS = ((0, 3), (0, 1))
VMEM = pl.BlockSpec(memory_space=pltpu.VMEM)
HBM = pl.BlockSpec(memory_space=pltpu.HBM)
NN = (((1,), (0,)), ((), ()))
TN = (((0,), (0,)), ((), ()))
NT = (((1,), (1,)), ((), ()))


def iota(shape, axis):
    return lax.broadcasted_iota(jnp.int32, shape, axis)


def dot(x, y, dims=NN):
    return lax.dot_general(x, y, dims, preferred_element_type=F32)


def dot_split(ones, values):
    high = values.astype(BF16)
    low = (values - high.astype(F32)).astype(BF16)
    return dot(jnp.concatenate([ones, ones], 1), jnp.concatenate([high, low], 0))


def split_dot(values, ones):
    high = values.astype(BF16)
    low = (values - high.astype(F32)).astype(BF16)
    return dot(high, ones) + dot(low, ones)


def ocean_number(shape, axis):
    place = iota(shape, axis)
    return place % ROWS * TILES + place // ROWS


def atm_number(shape, axis):
    place = iota(shape, axis)
    return place % 8 * 8 + place // 8


def one_hot(number, names):
    return jnp.where(number == names, 1.0, 0.0).astype(BF16)


def group_mask():
    return iota((8, 128), 1) // 16 == iota((8, 128), 0)


def edge_columns(levels):
    lane = iota((ROWS, 128), 1)
    block = jnp.zeros((ROWS, 128), F32)
    for at, values in enumerate(levels):
        block = jnp.where(lane == at, values[:, 0:1], block)
        block = jnp.where(lane == 64 + at, values[:, COLS - 1 : COLS], block)
    return block


def spread_air(air, mask):
    fold = (iota((128, 128), 0) % 16 == iota((128, 128), 1) % 16).astype(F32).astype(BF16)
    spread = []
    for c in range(8):
        for r in range(8):
            row = jnp.broadcast_to(air[c, r : r + 1, :].astype(F32), (8, 128))
            spread.append(jnp.where(mask, row, 0.0))
    tiled = dot(jnp.concatenate(spread, 0).astype(BF16), fold).astype(BF16)
    return jnp.concatenate([tiled[c * 64 : (c + 1) * 64] for c in range(8)], 1)


def outbound_lists(kinds, tiled, table, panels, outs, wait=lambda: None):
    mask = group_mask()
    source = iota((64, 64), 0)
    target = ocean_number((64, 64), 0)
    ones = jnp.concatenate([one_hot(source, table[a, b, 0:1, :]) for a, b in kinds], 1)
    picked = dot(ones, tiled, TN)
    wait()
    pieces = []
    for n, (a, b) in enumerate(kinds):
        planes = [[], [], [], []]
        for g in range(8):
            part = picked[n * 64 + g * 8 : n * 64 + (g + 1) * 8]
            left = [jnp.where(mask, part[:, c * 128 : (c + 1) * 128], 0.0) for c in range(8)]
            piece = dot(
                jnp.concatenate(left, 0).astype(BF16),
                panels[2 * a + b, g * 128 : (g + 1) * 128, :],
            )
            f = [piece[c * 8 : (c + 1) * 8] for c in range(8)]
            planes[0].append(f[0] + f[1] + f[2])
            planes[1].append(f[3])
            planes[2].append(f[4] - f[5] + f[6])
            planes[3].append(f[7])
        pieces.append(jnp.concatenate([jnp.concatenate(p, 0) for p in planes], 1))
    for (a, b), values, places in zip(kinds, pieces, outs):
        summed = dot_split(one_hot(target, table[a, b, 1:2, :]), values)
        for out in places:
            for p in range(4):
                out[p * 64 : (p + 1) * 64, :] = summed[:, p * 128 : (p + 1) * 128]


def fetch(sems, pairs):
    copies = [pltpu.make_async_copy(src, dst, sems.at[n]) for n, (src, dst) in enumerate(pairs)]
    for copy in copies:
        copy.start()
    return copies


def outbound_kernel(
    air_hbm, table_hbm, panels_hbm, temp_hbm, salt_hbm, depth_hbm,
    tiled, table, panels, temp, salt, depth, to_dg, to_z, to_core, to_gy, air, sems,
):
    pairs = [(air_hbm, air), (table_hbm, table)]
    pairs += [(panels_hbm.at[n], panels.at[n]) for n in range(3)]
    pairs += [(temp_hbm, temp), (salt_hbm, salt), (depth_hbm, depth)]
    copies = fetch(sems, pairs + [(panels_hbm.at[3], panels.at[3])])
    for out in (to_dg, to_z, to_gy):
        out[LIST_ROWS:, :] = jnp.zeros((out.shape[0] - LIST_ROWS, 128), F32)

    def rest():
        for copy in copies[2:8]:
            copy.wait()
        deep = depth[...].astype(F32)
        levels = [temp[l] for l in range(LEVELS)] + [salt[l] for l in range(LEVELS)] + [deep]
        block = edge_columns(levels)
        for out in (to_z, to_core):
            out[LIST_ROWS : LIST_ROWS + ROWS, :] = block

    copies[0].wait()
    spread = spread_air(air, group_mask())
    tiled[...] = spread
    copies[1].wait()
    kinds, outs = ((0, 0), (1, 0), (0, 1)), ((to_dg,), (to_z, to_core), (to_gy,))
    outbound_lists(kinds, spread, table, panels, outs, rest)
    copies[8].wait()


def beside(values, north, south, west, east):
    row, col = iota((ROWS, COLS), 0), iota((ROWS, COLS), 1)
    return (
        jnp.where(row == 0, north, pltpu.roll(values, 1, 0)),
        jnp.where(row == ROWS - 1, south, pltpu.roll(values, ROWS - 1, 0)),
        jnp.where(col == 0, west, pltpu.roll(values, 1, 1)),
        jnp.where(col == COLS - 1, east, pltpu.roll(values, COLS - 1, 1)),
    )


def side_sum(centre, nears, wets):
    side = jnp.zeros_like(centre)
    for near, there in zip(nears, wets):
        side = side + jnp.where(there, near - centre, 0.0)
    return SIDE_RATE * side


def inner_kernel(
    tiled, table, panels, temp, salt, depth, in_table_hbm, own, partial, sources, targets, fold,
    in_table, sem,
):
    copy = pltpu.make_async_copy(in_table_hbm, in_table, sem)
    copy.start()
    deep = depth[...].astype(F32)
    dry = jnp.zeros((1, 1), F32)
    around = beside(deep, dry, dry, dry, dry)
    for l in range(LEVELS):
        wet = deep > l
        wets = [d > l for d in around]
        for t, field in enumerate((temp, salt)):
            centre = field[l]
            side = side_sum(centre, beside(centre, dry, dry, dry, dry), wets)
            partial[t, l] = centre + jnp.where(wet, side, 0.0)
    outbound_lists(((1, 1),), tiled[...], table, panels, ((own,),))
    copy.wait()
    fold[...] = inbound_fold()
    eye = one_hot(iota((64, 64), 0), iota((64, 64), 1))
    source_block, target = ocean_number((64, 64), 0), atm_number((64, 64), 0)
    for n in range(4):
        ones = one_hot(source_block, in_table[n // 2, n % 2, 0:1, :])
        sources[n] = dot(ones, eye, TN).astype(BF16)
        targets[n] = one_hot(target, in_table[n // 2, n % 2, 1:2, :])


def edge_kernel(own, core, zpair, partial, temp, salt, depth, base, west, east, depths, whole):
    odd_col = lax.axis_index("gx") % 2 == 1
    base[...] = own[...] + jnp.where(
        odd_col, zpair[0:LIST_ROWS, :], core[0:LIST_ROWS, :]
    )
    at = slice(LIST_ROWS, LIST_ROWS + ROWS)
    left = jnp.where(odd_col, core[at, :], zpair[at, :])
    right = jnp.where(odd_col, zpair[at, :], core[at, :])
    west[...] = left
    east[...] = right
    deep = depth[...].astype(F32)
    dry = jnp.zeros((1, 1), F32)
    last = 2 * LEVELS
    around = beside(deep, dry, dry, left[:, 64 + last : 65 + last], right[:, last : last + 1])
    for n in range(4):
        depths[n] = around[n]
    lane = iota((ROWS, 128), 1)
    sides = ((0, left, 64, around[2], 0), (COLS - 128, right, 0, around[3], 127))
    for t, field in enumerate((temp, salt)):
        for l in range(LEVELS):
            at = t * LEVELS + l
            whole[t, l] = partial[t, l]
            for first, halo, offset, far, spot in sides:
                here = (lane == spot) & (far[:, first : first + 128] > l)
                here = here & (deep[:, first : first + 128] > l)
                near = halo[:, offset + at : offset + at + 1] - field[l, :, first : first + 128]
                whole[t, l, :, first : first + 128] += jnp.where(here, SIDE_RATE * near, 0.0)


def column_change(values, below, mixing, depth, l, across):
    change = 0.0 if l == 0 else -across
    if l < LEVELS - 1:
        across = mixing * (MIX_DECAY**l) * (below - values)
        across = jnp.where(depth > l + 1, across, 0.0)
        change = change + across
    return change, across


def source(t, l, planes, values):
    if t == 0:
        heating = planes[1] * (SHORTWAVE_RATE * 2.718281828459045 ** (-0.5 * l))
        return heating + HEAT_RATE * planes[0] if l == 0 else heating
    return -FRESH_RATE * planes[2] * values if l == 0 else 0.0


def first_kernel(
    dg, gy, base, partial, temp, salt, depth, new, cols, planes
):
    forcing = []
    for p in range(4):
        parts = []
        for s in range(TILES):
            at = p * 64 + s * ROWS
            parts.append(base[at : at + ROWS, :] + gy[at : at + ROWS, :] + dg[at : at + ROWS, :])
        forcing.append(jnp.concatenate(parts, 1))
    squared = forcing[3] * forcing[3]
    forcing[3] = squared / (1.0 + squared)
    for p in range(4):
        planes[p] = forcing[p]
    deep = depth[...].astype(F32)
    lane = iota((ROWS, 128), 1)
    mixing = MIX_BASE + MIX_WIND * forcing[3]
    block = jnp.zeros((ROWS, 128), F32)
    for t, field in enumerate((temp, salt)):
        across = None
        for l in range(LEVELS):
            at = t * LEVELS + l
            centre = field[l]
            change, across = column_change(
                centre, field[min(l + 1, LEVELS - 1)], mixing, deep, l, across
            )
            change = change + source(t, l, forcing, centre)
            value = partial[t, l] + jnp.where(deep > l, change, 0.0)
            new[t, l] = value
            block = jnp.where(lane == at, value[:, 0:1], block)
            block = jnp.where(lane == 64 + at, value[:, COLS - 1 : COLS], block)
    cols[...] = block


def rows_kernel(new, temp, salt, depth, west, east, row_e, row_o, keep):
    odd_row = lax.axis_index("gy") % 2 == 1
    deep = depth[...].astype(F32)
    edges = []
    for r in (0, ROWS - 1):
        rows = [new[0, :, r, :], new[1, :, r, :], temp[:, r, :], salt[:, r, :], deep[r : r + 1]]
        edges.append(rows + [west[r : r + 1, :], east[r : r + 1, :]])
    for out, first in ((row_e, odd_row), (row_o, jnp.logical_not(odd_row))):
        at = 0
        for a, b in zip(*edges):
            out[at : at + a.shape[0], 0 : a.shape[1]] = jnp.where(first, a, b)
            at += a.shape[0]
    row_e[43:48, :] = jnp.zeros((5, COLS), F32)
    for n in range(2):
        keep[20 * n : 20 * n + 10, :] = edges[n][2]
        keep[20 * n + 10 : 20 * n + 20, :] = edges[n][3]
        keep[40 + 2 * n : 41 + 2 * n, 0:128] = edges[n][5]
        keep[41 + 2 * n : 42 + 2 * n, 0:128] = edges[n][6]


def inbound_lists(kinds, blocks, sources, targets, fold, panels, outs):
    mask = group_mask()
    numbers = [2 * a + b for a, b in kinds]
    chosen = dot(jnp.concatenate([sources[n] for n in numbers], 0), blocks)
    lists = []
    for m, n in enumerate(numbers):
        kept = [[], [], [], []]
        for g in range(8):
            part = chosen[m * 64 + g * 8 : m * 64 + (g + 1) * 8]
            left = [part[:, c * 128 : (c + 1) * 128] for c in range(4)]
            piece = dot(
                jnp.concatenate(left, 0).astype(BF16), panels[n, g * 128 : (g + 1) * 128, :], NT
            )
            for c in range(4):
                kept[c].append(jnp.where(mask, piece[c * 8 : (c + 1) * 8], 0.0))
        lists.append(jnp.concatenate([jnp.concatenate(k, 0) for k in kept], 1))
    pieces = split_dot(jnp.concatenate(lists, 0), fold)
    for m, (n, out) in enumerate(zip(numbers, outs)):
        summed = dot_split(targets[n], pieces[m * 64 : (m + 1) * 64])
        out[0:32, :] = summed[0:32] + pltpu.roll(summed[32:64], 64, 1)
        if out.shape[0] > 32:
            out[32:, :] = jnp.zeros((out.shape[0] - 32, 128), F32)


def inbound_fold():
    place, lane = iota((512, 128), 0), iota((512, 128), 1)
    fold = jnp.where((place // 128 == lane // 16) & (place % 16 == lane % 16), 1.0, 0.0)
    return fold.astype(BF16)


def second_step(levels, old, core, zpair, xe, xo, planes, depths, keep, depth, store):
    odd_col = lax.axis_index("gx") % 2 == 1
    odd_row = lax.axis_index("gy") % 2 == 1
    deep = depth[...].astype(F32)
    row_e, row_o = xe[0:43, :], xo[...]
    beyond = (jnp.where(odd_row, row_e, row_o), jnp.where(odd_row, row_o, row_e))
    level = iota((2 * LEVELS, COLS), 0) % LEVELS
    at_end = (lax.axis_index("gy") == 0, lax.axis_index("gy") == lax.axis_size("gy") - 1)
    beyond_deep = [jnp.where(end, 0.0, other[40:41]) for end, other in zip(at_end, beyond)]
    fixes, halo_rows = [], []
    for n, other in enumerate(beyond):
        r = n * (ROWS - 1)
        here = (deep[r : r + 1] > level) & (beyond_deep[n] > level)
        fix = jnp.where(here, SIDE_RATE * (other[20:40] - keep[20 * n : 20 * n + 20, :]), 0.0)
        fixes.append(fix)
        halo_rows.append(other[0:20] - fix)
    norths, souths = halo_rows
    level = iota((1, 128), 1) % 64 % LEVELS
    row = iota((ROWS, 128), 0)
    ends = []
    for halo, at, deepest in (
        (jnp.where(odd_col, core[...], zpair[...]), 0, 84),
        (jnp.where(odd_col, zpair[...], core[...]), 1, 20),
    ):
        for n, other in enumerate(beyond):
            mine = keep[40 + 2 * n + at : 41 + 2 * n + at, 0:128]
            far = other[41 + at : 42 + at, 0:128]
            here = mine[:, deepest : deepest + 1] > level
            here = here & (jnp.where(at_end[n], 0.0, far[:, deepest : deepest + 1]) > level)
            fix = jnp.where(here, SIDE_RATE * (far - mine), 0.0)
            halo = halo + jnp.where(row == n * (ROWS - 1), fix, 0.0)
        ends.append(halo)
    west, east = ends
    row8, row = iota((8, COLS), 0), iota((ROWS, COLS), 0)
    around = [depths[n] for n in range(4)]
    around[0] = jnp.where(row == 0, beyond_deep[0], around[0])
    around[1] = jnp.where(row == ROWS - 1, beyond_deep[1], around[1])
    forcing = [planes[p] for p in range(4)]
    mixing = MIX_BASE + MIX_WIND * forcing[3]
    def whole(t, l):
        at = t * LEVELS + l
        high = old[t, l, 0:8, :] + jnp.where(row8 == 0, fixes[0][at : at + 1], 0.0)
        low = old[t, l, 8:16, :] + jnp.where(row8 == 7, fixes[1][at : at + 1], 0.0)
        return jnp.concatenate([high, low], 0)

    for t, (start, stop) in enumerate(levels):
        across, centre = None, whole(t, start)
        if start:
            across = mixing * (MIX_DECAY ** (start - 1)) * (centre - whole(t, start - 1))
            across = jnp.where(deep > start, across, 0.0)
        for l in range(start, stop):
            at = t * LEVELS + l
            below = whole(t, l + 1) if l < LEVELS - 1 else None
            change, across = column_change(centre, below, mixing, deep, l, across)
            change = change + source(t, l, forcing, centre)
            nears = beside(
                centre,
                norths[at : at + 1],
                souths[at : at + 1],
                west[:, 64 + at : 65 + at],
                east[:, at : at + 1],
            )
            change = change + side_sum(centre, nears, [d > l for d in around])
            store(t, l, centre + jnp.where(deep > l, change, 0.0))
            centre = below


def second_kernel(
    old, core, zpair, xe, xo, planes, depths, keep, depth, sources, targets, fold, panels,
    top_temp, top_salt, surface_blocks, to_dg, to_gy, to_gx,
):
    top = {}

    def store(t, l, value):
        (top_temp, top_salt)[t][l] = value
        top[t, l] = value

    second_step(TOP_LEVELS, old, core, zpair, xe, xo, planes, depths, keep, depth, store)
    deep = depth[...].astype(F32)
    wet_top = jnp.where(deep > 0, 1.0, 0.0)
    surface = (
        top[0, 0] * wet_top,
        top[1, 0] * wet_top,
        (top[0, 0] + top[0, 1] + top[0, 2]) / 3.0 * wet_top,
        wet_top,
    )
    parts = []
    for f in surface:
        parts.append(jnp.concatenate([f[:, s * 128 : (s + 1) * 128] for s in range(TILES)], 0))
    blocks = jnp.concatenate(parts, 1).astype(BF16)
    surface_blocks[...] = blocks
    kinds, outs = ((1, 1), (1, 0), (0, 1)), (to_dg, to_gy, to_gx)
    inbound_lists(kinds, blocks, sources, targets, fold[...], panels, outs)


def outer_kernel(
    old, core, zpair, xe, xo, planes, depths, keep, depth, top_temp, top_salt,
    blocks, sources, targets, fold, panels, new_temp, new_salt, own, rest, sems,
):
    pairs = []
    for t, (top, new) in enumerate(((top_temp, new_temp), (top_salt, new_salt))):
        count = TOP_LEVELS[t][1]
        pairs.append((top, new.at[0:count]))
    copies = fetch(sems.at[0:2], pairs)

    def store(t, l, value):
        rest[t, l] = value

    levels = [(stop, LEVELS) for _, stop in TOP_LEVELS]
    second_step(levels, old, core, zpair, xe, xo, planes, depths, keep, depth, store)
    pairs = []
    for t, new in enumerate((new_temp, new_salt)):
        span = slice(TOP_LEVELS[t][1], LEVELS)
        pairs.append((rest.at[t, span], new.at[span]))
    copies += fetch(sems.at[2:4], pairs)
    inbound_lists(((0, 0),), blocks[...], sources, targets, fold[...], panels, (own,))
    for copy in copies:
        copy.wait()


def final_kernel(dg, gy, gx, own, out):
    total = own[...] + gx[0:32, :] + gy[0:32, :] + dg[0:32, :]
    group = iota((8, 128), 1) // 16
    for c in range(4):
        field = jnp.zeros((8, 128), F32)
        for k in range(8):
            part = total[k % 4 * 8 : (k % 4 + 1) * 8]
            moved = pltpu.roll(part, (k - c - k // 4 * 4) % 8 * 16, 1)
            field = jnp.where(group == k, moved, field)
        out[c] = field


def call(kernel, shapes, args, scratch=(), hbm_in=(), hbm_out=(), mib=12):
    args = [
        pltpu.with_memory_space_constraint(x, pltpu.HBM) if n in hbm_in else x
        for n, x in enumerate(args)
    ]
    shapes = [s if isinstance(s, jax.ShapeDtypeStruct) else jax.ShapeDtypeStruct(s, F32) for s in shapes]
    return pl.pallas_call(
        kernel,
        out_shape=shapes,
        in_specs=[HBM if n in hbm_in else VMEM for n in range(len(args))],
        out_specs=[HBM if n in hbm_out else VMEM for n in range(len(shapes))],
        scratch_shapes=list(scratch),
        compiler_params=pltpu.CompilerParams(vmem_limit_bytes=mib * 1024 * 1024),
    )(*args)


def send(block, step):
    wide, high = lax.axis_size("gx"), lax.axis_size("gy")
    route = []
    for i in range(wide):
        for j in range(high):
            to = step(i, j)
            route.append((i * high + j, to[0] % wide * high + to[1] % high))
    return lax.ppermute(block, ("gx", "gy"), route)


def pair(n):
    return n - 1 if n % 2 else n + 1


def other_pair(n):
    return n + 1 if n % 2 else n - 1


def row_pair(i, j):
    return (i, other_pair(j)) if 0 <= other_pair(j) < lax.axis_size("gy") else (pair(i), j)


def per_device(air, out_tables, out_panels, depth, temp, salt, in_tables, in_panels):
    out_panels = out_panels.reshape(4, 1024, 128)
    in_panels = in_panels.reshape(4, 1024, 128)
    out_tables, in_tables = out_tables[0, 0], in_tables[0, 0]
    field = (2, LEVELS, ROWS, COLS)
    rows = LIST_ROWS + ROWS
    tiled, out_tables, out_panels, temp, salt, depth, to_dg, to_z, to_core, to_gy = call(
        outbound_kernel,
        [
            jax.ShapeDtypeStruct((64, 1024), BF16),
            jax.ShapeDtypeStruct(out_tables.shape, jnp.int32),
            jax.ShapeDtypeStruct((4, 1024, 128), BF16),
            temp.shape,
            salt.shape,
            jax.ShapeDtypeStruct(depth.shape, jnp.int32),
            (rows + 24, 128),
            (rows + 16, 128),
            (rows, 128),
            (rows + 8, 128),
        ],
        [air, out_tables, out_panels, temp, salt, depth],
        [pltpu.VMEM(air.shape, BF16), pltpu.SemaphoreType.DMA((9,))],
        hbm_in=range(6),
    )
    dg = send(to_dg, lambda i, j: (i - 1, j - 1) if j else (i, j - 1))
    zpair = send(to_z, lambda i, j: (other_pair(i), j))
    gy = send(to_gy, lambda i, j: (i, j - 1))
    core = send(to_core, lambda i, j: (pair(i), j))
    ones = jax.ShapeDtypeStruct((4, 64, 64), BF16)
    own, partial, *maps = call(
        inner_kernel,
        [(LIST_ROWS, 128), field, ones, ones, jax.ShapeDtypeStruct((512, 128), BF16)],
        [tiled, out_tables, out_panels, temp, salt, depth, in_tables],
        [pltpu.VMEM(in_tables.shape, jnp.int32), pltpu.SemaphoreType.DMA],
        hbm_in=(6,),
    )
    base, west, east, depths, partial = call(
        edge_kernel,
        [(LIST_ROWS, 128), (ROWS, 128), (ROWS, 128), (4, ROWS, COLS), field],
        [own, core, zpair, partial, temp, salt, depth],
    )
    stepped, cols, planes = call(
        first_kernel,
        [field, (ROWS, 128), (4, ROWS, COLS)],
        [dg, gy, base, partial, temp, salt, depth],
    )
    row_e, row_o, keep = call(
        rows_kernel,
        [(48, COLS), (43, COLS), (44, COLS)],
        [stepped, temp, salt, depth, west, east],
    )
    xo = send(row_o, row_pair)
    xe = send(row_e, lambda i, j: (i, pair(j)))
    zpair = send(cols, lambda i, j: (other_pair(i), j))
    core = send(cols, lambda i, j: (pair(i), j))
    state = [stepped, core, zpair, xe, xo, planes, depths, keep, depth]
    top_temp, top_salt, blocks, to_dg, to_gy, to_gx = call(
        second_kernel,
        [
            (TOP_LEVELS[0][1], ROWS, COLS),
            (TOP_LEVELS[1][1], ROWS, COLS),
            jax.ShapeDtypeStruct((64, COLS), BF16),
            (48, 128),
            (40, 128),
            (32, 128),
        ],
        state + maps + [in_panels],
    )
    dg = send(to_dg, lambda i, j: (i + 1, j + 1) if j + 1 < lax.axis_size("gy") else (i, j + 1))
    gy = send(to_gy, lambda i, j: (i, j + 1))
    gx = send(to_gx, lambda i, j: (i + 1, j))
    new_temp, new_salt, own = call(
        outer_kernel,
        [temp.shape, salt.shape, (32, 128)],
        state + [top_temp, top_salt, blocks, *maps, in_panels],
        [pltpu.VMEM(field, F32), pltpu.SemaphoreType.DMA((4,))],
        hbm_out=(0, 1),
    )
    (surface,) = call(final_kernel, [(4, 8, 128)], [dg, gy, gx, own])
    return new_temp, new_salt, surface


def solution(mesh):
    in_specs = (
        P(None, "gy", "gx"),
        P("gy", "gx", None, None, None, None),
        P("gy", "gx", None, None, None, None, None),
        P("gy", "gx"),
        P(None, "gy", "gx"),
        P(None, "gy", "gx"),
        P("gy", "gx", None, None, None, None),
        P("gy", "gx", None, None, None, None, None),
    )
    out_specs = (P(None, "gy", "gx"), P(None, "gy", "gx"), P(None, "gy", "gx"))
    return jax.shard_map(
        per_device, mesh=mesh, in_specs=in_specs, out_specs=out_specs, check_vma=False
    )
```

```python
import jax
import jax.numpy as jnp
from jax import lax
from jax.experimental import pallas as pl
from jax.experimental.pallas import tpu as pltpu
from jax.sharding import PartitionSpec as P

HEAT_RATE = 0.1
SHORTWAVE_RATE = 0.1
FRESH_RATE = 0.05
SIDE_RATE = 0.18
MIX_BASE = 0.03
MIX_WIND = 0.09
MIX_DECAY = 0.8

ROWS, COLS, LEVELS = 16, 512, 10
TILES = COLS // 128
F32, BF16 = jnp.float32, jnp.bfloat16
LIST_ROWS = 4 * 64
TOP_LEVELS = ((0, 3), (0, 1))
VMEM = pl.BlockSpec(memory_space=pltpu.VMEM)
HBM = pl.BlockSpec(memory_space=pltpu.HBM)
NN = (((1,), (0,)), ((), ()))
TN = (((0,), (0,)), ((), ()))
NT = (((1,), (1,)), ((), ()))


def iota(shape, axis):
    return lax.broadcasted_iota(jnp.int32, shape, axis)


def dot(x, y, dims=NN):
    return lax.dot_general(x, y, dims, preferred_element_type=F32)


def dot_split(ones, values):
    high = values.astype(BF16)
    low = (values - high.astype(F32)).astype(BF16)
    return dot(jnp.concatenate([ones, ones], 1), jnp.concatenate([high, low], 0))


def split_dot(values, ones):
    high = values.astype(BF16)
    low = (values - high.astype(F32)).astype(BF16)
    return dot(high, ones) + dot(low, ones)


def ocean_number(shape, axis):
    place = iota(shape, axis)
    return place % ROWS * TILES + place // ROWS


def atm_number(shape, axis):
    place = iota(shape, axis)
    return place % 8 * 8 + place // 8


def one_hot(number, names):
    return jnp.where(number == names, 1.0, 0.0).astype(BF16)


def group_mask():
    return iota((8, 128), 1) // 16 == iota((8, 128), 0)


def edge_columns(levels):
    lane = iota((ROWS, 128), 1)
    block = jnp.zeros((ROWS, 128), F32)
    for at, values in enumerate(levels):
        block = jnp.where(lane == at, values[:, 0:1], block)
        block = jnp.where(lane == 64 + at, values[:, COLS - 1 : COLS], block)
    return block


def spread_air(air, mask):
    fold = (iota((128, 128), 0) % 16 == iota((128, 128), 1) % 16).astype(F32).astype(BF16)
    spread = []
    for c in range(8):
        field = air[c].astype(F32)
        for r in range(8):
            row = jnp.broadcast_to(field[r : r + 1], (8, 128))
            spread.append(jnp.where(mask, row, 0.0))
    tiled = dot(jnp.concatenate(spread, 0).astype(BF16), fold).astype(BF16)
    return jnp.concatenate([tiled[c * 64 : (c + 1) * 64] for c in range(8)], 1)


def outbound_lists(kinds, tiled, table, panels, outs, wait=lambda: None):
    mask = group_mask()
    source = iota((64, 64), 0)
    target = ocean_number((64, 64), 0)
    ones = jnp.concatenate([one_hot(source, table[a, b, 0:1, :]) for a, b in kinds], 1)
    picked = dot(ones, tiled, TN)
    wait()
    pieces = []
    for n, (a, b) in enumerate(kinds):
        planes = [[], [], [], []]
        for g in range(8):
            part = picked[n * 64 + g * 8 : n * 64 + (g + 1) * 8]
            left = [jnp.where(mask, part[:, c * 128 : (c + 1) * 128], 0.0) for c in range(8)]
            piece = dot(
                jnp.concatenate(left, 0).astype(BF16),
                panels[2 * a + b, g * 128 : (g + 1) * 128, :],
            )
            f = [piece[c * 8 : (c + 1) * 8] for c in range(8)]
            planes[0].append(f[0] + f[1] + f[2])
            planes[1].append(f[3])
            planes[2].append(f[4] - f[5] + f[6])
            planes[3].append(f[7])
        pieces.append(jnp.concatenate([jnp.concatenate(p, 0) for p in planes], 1))
    for (a, b), values, places in zip(kinds, pieces, outs):
        summed = dot_split(one_hot(target, table[a, b, 1:2, :]), values)
        for out in places:
            for p in range(4):
                out[p * 64 : (p + 1) * 64, :] = summed[:, p * 128 : (p + 1) * 128]


def fetch(sems, pairs):
    copies = [pltpu.make_async_copy(src, dst, sems.at[n]) for n, (src, dst) in enumerate(pairs)]
    for copy in copies:
        copy.start()
    return copies


def outbound_kernel(
    air_hbm, table_hbm, panels_hbm, temp_hbm, salt_hbm, depth_hbm,
    tiled, table, panels, temp, salt, depth, to_dg, to_z, to_core, to_gy, air, sems,
):
    pairs = [(air_hbm, air), (table_hbm, table)]
    pairs += [(panels_hbm.at[n], panels.at[n]) for n in range(3)]
    pairs += [(temp_hbm, temp), (salt_hbm, salt), (depth_hbm, depth)]
    copies = fetch(sems, pairs + [(panels_hbm.at[3], panels.at[3])])
    for out in (to_dg, to_z, to_gy):
        out[LIST_ROWS:, :] = jnp.zeros((out.shape[0] - LIST_ROWS, 128), F32)

    def rest():
        for copy in copies[2:8]:
            copy.wait()
        deep = depth[...].astype(F32)
        levels = [temp[l] for l in range(LEVELS)] + [salt[l] for l in range(LEVELS)] + [deep]
        block = edge_columns(levels)
        for out in (to_z, to_core):
            out[LIST_ROWS : LIST_ROWS + ROWS, :] = block

    copies[0].wait()
    spread = spread_air(air, group_mask())
    tiled[...] = spread
    copies[1].wait()
    kinds, outs = ((0, 0), (1, 0), (0, 1)), ((to_dg,), (to_z, to_core), (to_gy,))
    outbound_lists(kinds, spread, table, panels, outs, rest)
    copies[8].wait()


def beside(values, north, south, west, east):
    row, col = iota((ROWS, COLS), 0), iota((ROWS, COLS), 1)
    return (
        jnp.where(row == 0, north, pltpu.roll(values, 1, 0)),
        jnp.where(row == ROWS - 1, south, pltpu.roll(values, ROWS - 1, 0)),
        jnp.where(col == 0, west, pltpu.roll(values, 1, 1)),
        jnp.where(col == COLS - 1, east, pltpu.roll(values, COLS - 1, 1)),
    )


def side_sum(centre, nears, wets):
    side = jnp.zeros_like(centre)
    for near, there in zip(nears, wets):
        side = side + jnp.where(there, near - centre, 0.0)
    return SIDE_RATE * side


def inner_kernel(
    tiled, table, panels, temp, salt, depth, in_table_hbm, own, partial, sources, targets, fold,
    in_table, sem,
):
    copy = pltpu.make_async_copy(in_table_hbm, in_table, sem)
    copy.start()
    deep = depth[...].astype(F32)
    dry = jnp.zeros((1, 1), F32)
    around = beside(deep, dry, dry, dry, dry)
    for l in range(LEVELS):
        wet = deep > l
        wets = [d > l for d in around]
        for t, field in enumerate((temp, salt)):
            centre = field[l]
            side = side_sum(centre, beside(centre, dry, dry, dry, dry), wets)
            partial[t, l] = centre + jnp.where(wet, side, 0.0)
    outbound_lists(((1, 1),), tiled[...], table, panels, ((own,),))
    copy.wait()
    fold[...] = inbound_fold()
    eye = one_hot(iota((64, 64), 0), iota((64, 64), 1))
    source_block, target = ocean_number((64, 64), 0), atm_number((64, 64), 0)
    for n in range(4):
        ones = one_hot(source_block, in_table[n // 2, n % 2, 0:1, :])
        sources[n] = dot(ones, eye, TN).astype(BF16)
        targets[n] = one_hot(target, in_table[n // 2, n % 2, 1:2, :])


def edge_kernel(own, core, zpair, partial, temp, salt, depth, base, west, east, depths, whole):
    odd_col = lax.axis_index("gx") % 2 == 1
    base[...] = own[...] + jnp.where(
        odd_col, zpair[0:LIST_ROWS, :], core[0:LIST_ROWS, :]
    )
    at = slice(LIST_ROWS, LIST_ROWS + ROWS)
    left = jnp.where(odd_col, core[at, :], zpair[at, :])
    right = jnp.where(odd_col, zpair[at, :], core[at, :])
    west[...] = left
    east[...] = right
    deep = depth[...].astype(F32)
    dry = jnp.zeros((1, 1), F32)
    last = 2 * LEVELS
    around = beside(deep, dry, dry, left[:, 64 + last : 65 + last], right[:, last : last + 1])
    for n in range(4):
        depths[n] = around[n]
    lane = iota((ROWS, 128), 1)
    sides = ((0, left, 64, around[2], 0), (COLS - 128, right, 0, around[3], 127))
    for t, field in enumerate((temp, salt)):
        for l in range(LEVELS):
            at = t * LEVELS + l
            whole[t, l] = partial[t, l]
            for first, halo, offset, far, spot in sides:
                here = (lane == spot) & (far[:, first : first + 128] > l)
                here = here & (deep[:, first : first + 128] > l)
                near = halo[:, offset + at : offset + at + 1] - field[l, :, first : first + 128]
                whole[t, l, :, first : first + 128] += jnp.where(here, SIDE_RATE * near, 0.0)


def column_change(values, below, mixing, depth, l, across):
    change = 0.0 if l == 0 else -across
    if l < LEVELS - 1:
        across = mixing * (MIX_DECAY**l) * (below - values)
        across = jnp.where(depth > l + 1, across, 0.0)
        change = change + across
    return change, across


def source(t, l, planes, values):
    if t == 0:
        heating = planes[1] * (SHORTWAVE_RATE * 2.718281828459045 ** (-0.5 * l))
        return heating + HEAT_RATE * planes[0] if l == 0 else heating
    return -FRESH_RATE * planes[2] * values if l == 0 else 0.0


def first_kernel(
    dg, gy, base, partial, temp, salt, depth, new, cols, planes
):
    forcing = []
    for p in range(4):
        parts = []
        for s in range(TILES):
            at = p * 64 + s * ROWS
            parts.append(base[at : at + ROWS, :] + gy[at : at + ROWS, :] + dg[at : at + ROWS, :])
        forcing.append(jnp.concatenate(parts, 1))
    squared = forcing[3] * forcing[3]
    forcing[3] = squared / (1.0 + squared)
    for p in range(4):
        planes[p] = forcing[p]
    deep = depth[...].astype(F32)
    lane = iota((ROWS, 128), 1)
    mixing = MIX_BASE + MIX_WIND * forcing[3]
    block = jnp.zeros((ROWS, 128), F32)
    for t, field in enumerate((temp, salt)):
        across = None
        for l in range(LEVELS):
            at = t * LEVELS + l
            centre = field[l]
            change, across = column_change(
                centre, field[min(l + 1, LEVELS - 1)], mixing, deep, l, across
            )
            change = change + source(t, l, forcing, centre)
            value = partial[t, l] + jnp.where(deep > l, change, 0.0)
            new[t, l] = value
            block = jnp.where(lane == at, value[:, 0:1], block)
            block = jnp.where(lane == 64 + at, value[:, COLS - 1 : COLS], block)
    cols[...] = block


def rows_kernel(new, temp, salt, depth, west, east, row_e, row_o, keep):
    odd_row = lax.axis_index("gy") % 2 == 1
    deep = depth[...].astype(F32)
    edges = []
    for r in (0, ROWS - 1):
        rows = [new[0, :, r, :], new[1, :, r, :], temp[:, r, :], salt[:, r, :], deep[r : r + 1]]
        edges.append(rows + [west[r : r + 1, :], east[r : r + 1, :]])
    for out, first in ((row_e, odd_row), (row_o, jnp.logical_not(odd_row))):
        at = 0
        for a, b in zip(*edges):
            out[at : at + a.shape[0], 0 : a.shape[1]] = jnp.where(first, a, b)
            at += a.shape[0]
    row_e[43:48, :] = jnp.zeros((5, COLS), F32)
    for n in range(2):
        keep[20 * n : 20 * n + 10, :] = edges[n][2]
        keep[20 * n + 10 : 20 * n + 20, :] = edges[n][3]
        keep[40 + 2 * n : 41 + 2 * n, 0:128] = edges[n][5]
        keep[41 + 2 * n : 42 + 2 * n, 0:128] = edges[n][6]


def inbound_lists(kinds, blocks, sources, targets, fold, panels, outs):
    mask = group_mask()
    numbers = [2 * a + b for a, b in kinds]
    chosen = dot(jnp.concatenate([sources[n] for n in numbers], 0), blocks)
    lists = []
    for m, n in enumerate(numbers):
        kept = [[], [], [], []]
        for g in range(8):
            part = chosen[m * 64 + g * 8 : m * 64 + (g + 1) * 8]
            left = [part[:, c * 128 : (c + 1) * 128] for c in range(4)]
            piece = dot(
                jnp.concatenate(left, 0).astype(BF16), panels[n, g * 128 : (g + 1) * 128, :], NT
            )
            for c in range(4):
                kept[c].append(jnp.where(mask, piece[c * 8 : (c + 1) * 8], 0.0))
        lists.append(jnp.concatenate([jnp.concatenate(k, 0) for k in kept], 1))
    pieces = split_dot(jnp.concatenate(lists, 0), fold)
    for m, (n, out) in enumerate(zip(numbers, outs)):
        summed = dot_split(targets[n], pieces[m * 64 : (m + 1) * 64])
        out[0:32, :] = summed[0:32] + pltpu.roll(summed[32:64], 64, 1)
        if out.shape[0] > 32:
            out[32:, :] = jnp.zeros((out.shape[0] - 32, 128), F32)


def inbound_fold():
    place, lane = iota((512, 128), 0), iota((512, 128), 1)
    fold = jnp.where((place // 128 == lane // 16) & (place % 16 == lane % 16), 1.0, 0.0)
    return fold.astype(BF16)


def second_step(levels, old, core, zpair, xe, xo, planes, depths, keep, depth, store):
    odd_col = lax.axis_index("gx") % 2 == 1
    odd_row = lax.axis_index("gy") % 2 == 1
    deep = depth[...].astype(F32)
    row_e, row_o = xe[0:43, :], xo[...]
    beyond = (jnp.where(odd_row, row_e, row_o), jnp.where(odd_row, row_o, row_e))
    level = iota((2 * LEVELS, COLS), 0) % LEVELS
    at_end = (lax.axis_index("gy") == 0, lax.axis_index("gy") == lax.axis_size("gy") - 1)
    beyond_deep = [jnp.where(end, 0.0, other[40:41]) for end, other in zip(at_end, beyond)]
    fixes, halo_rows = [], []
    for n, other in enumerate(beyond):
        r = n * (ROWS - 1)
        here = (deep[r : r + 1] > level) & (beyond_deep[n] > level)
        fix = jnp.where(here, SIDE_RATE * (other[20:40] - keep[20 * n : 20 * n + 20, :]), 0.0)
        fixes.append(fix)
        halo_rows.append(other[0:20] - fix)
    norths, souths = halo_rows
    level = iota((1, 128), 1) % 64 % LEVELS
    row = iota((ROWS, 128), 0)
    ends = []
    for halo, at, deepest in (
        (jnp.where(odd_col, core[...], zpair[...]), 0, 84),
        (jnp.where(odd_col, zpair[...], core[...]), 1, 20),
    ):
        for n, other in enumerate(beyond):
            mine = keep[40 + 2 * n + at : 41 + 2 * n + at, 0:128]
            far = other[41 + at : 42 + at, 0:128]
            here = mine[:, deepest : deepest + 1] > level
            here = here & (jnp.where(at_end[n], 0.0, far[:, deepest : deepest + 1]) > level)
            fix = jnp.where(here, SIDE_RATE * (far - mine), 0.0)
            halo = halo + jnp.where(row == n * (ROWS - 1), fix, 0.0)
        ends.append(halo)
    west, east = ends
    row8, row = iota((8, COLS), 0), iota((ROWS, COLS), 0)
    around = [depths[n] for n in range(4)]
    around[0] = jnp.where(row == 0, beyond_deep[0], around[0])
    around[1] = jnp.where(row == ROWS - 1, beyond_deep[1], around[1])
    forcing = [planes[p] for p in range(4)]
    mixing = MIX_BASE + MIX_WIND * forcing[3]
    def whole(t, l):
        at = t * LEVELS + l
        high = old[t, l, 0:8, :] + jnp.where(row8 == 0, fixes[0][at : at + 1], 0.0)
        low = old[t, l, 8:16, :] + jnp.where(row8 == 7, fixes[1][at : at + 1], 0.0)
        return jnp.concatenate([high, low], 0)

    for t, (start, stop) in enumerate(levels):
        across, centre = None, whole(t, start)
        if start:
            across = mixing * (MIX_DECAY ** (start - 1)) * (centre - whole(t, start - 1))
            across = jnp.where(deep > start, across, 0.0)
        for l in range(start, stop):
            at = t * LEVELS + l
            below = whole(t, l + 1) if l < LEVELS - 1 else None
            change, across = column_change(centre, below, mixing, deep, l, across)
            change = change + source(t, l, forcing, centre)
            nears = beside(
                centre,
                norths[at : at + 1],
                souths[at : at + 1],
                west[:, 64 + at : 65 + at],
                east[:, at : at + 1],
            )
            change = change + side_sum(centre, nears, [d > l for d in around])
            store(t, l, centre + jnp.where(deep > l, change, 0.0))
            centre = below


def second_kernel(
    old, core, zpair, xe, xo, planes, depths, keep, depth, sources, targets, fold, panels,
    top_temp, top_salt, surface_blocks, to_dg, to_gy, to_gx,
):
    top = {}

    def store(t, l, value):
        (top_temp, top_salt)[t][l] = value
        top[t, l] = value

    second_step(TOP_LEVELS, old, core, zpair, xe, xo, planes, depths, keep, depth, store)
    deep = depth[...].astype(F32)
    wet_top = jnp.where(deep > 0, 1.0, 0.0)
    surface = (
        top[0, 0] * wet_top,
        top[1, 0] * wet_top,
        (top[0, 0] + top[0, 1] + top[0, 2]) / 3.0 * wet_top,
        wet_top,
    )
    parts = []
    for f in surface:
        parts.append(jnp.concatenate([f[:, s * 128 : (s + 1) * 128] for s in range(TILES)], 0))
    blocks = jnp.concatenate(parts, 1).astype(BF16)
    surface_blocks[...] = blocks
    kinds, outs = ((1, 1), (1, 0), (0, 1)), (to_dg, to_gy, to_gx)
    inbound_lists(kinds, blocks, sources, targets, fold[...], panels, outs)


def outer_kernel(
    old, core, zpair, xe, xo, planes, depths, keep, depth, top_temp, top_salt,
    blocks, sources, targets, fold, panels, new_temp, new_salt, own, rest, sems,
):
    pairs = []
    for t, (top, new) in enumerate(((top_temp, new_temp), (top_salt, new_salt))):
        count = TOP_LEVELS[t][1]
        pairs.append((top, new.at[0:count]))
    copies = fetch(sems.at[0:2], pairs)

    def store(t, l, value):
        rest[t, l] = value

    levels = [(stop, LEVELS) for _, stop in TOP_LEVELS]
    second_step(levels, old, core, zpair, xe, xo, planes, depths, keep, depth, store)
    pairs = []
    for t, new in enumerate((new_temp, new_salt)):
        span = slice(TOP_LEVELS[t][1], LEVELS)
        pairs.append((rest.at[t, span], new.at[span]))
    copies += fetch(sems.at[2:4], pairs)
    inbound_lists(((0, 0),), blocks[...], sources, targets, fold[...], panels, (own,))
    for copy in copies:
        copy.wait()


def final_kernel(dg, gy, gx, own, out):
    total = own[...] + gx[0:32, :] + gy[0:32, :] + dg[0:32, :]
    group = iota((8, 128), 1) // 16
    for c in range(4):
        field = jnp.zeros((8, 128), F32)
        for k in range(8):
            part = total[k % 4 * 8 : (k % 4 + 1) * 8]
            moved = pltpu.roll(part, (k - c - k // 4 * 4) % 8 * 16, 1)
            field = jnp.where(group == k, moved, field)
        out[c] = field


def call(kernel, shapes, args, scratch=(), hbm_in=(), hbm_out=(), mib=12):
    args = [
        pltpu.with_memory_space_constraint(x, pltpu.HBM) if n in hbm_in else x
        for n, x in enumerate(args)
    ]
    shapes = [s if isinstance(s, jax.ShapeDtypeStruct) else jax.ShapeDtypeStruct(s, F32) for s in shapes]
    return pl.pallas_call(
        kernel,
        out_shape=shapes,
        in_specs=[HBM if n in hbm_in else VMEM for n in range(len(args))],
        out_specs=[HBM if n in hbm_out else VMEM for n in range(len(shapes))],
        scratch_shapes=list(scratch),
        compiler_params=pltpu.CompilerParams(vmem_limit_bytes=mib * 1024 * 1024),
    )(*args)


def send(block, step):
    wide, high = lax.axis_size("gx"), lax.axis_size("gy")
    route = []
    for i in range(wide):
        for j in range(high):
            to = step(i, j)
            route.append((i * high + j, to[0] % wide * high + to[1] % high))
    return lax.ppermute(block, ("gx", "gy"), route)


def pair(n):
    return n - 1 if n % 2 else n + 1


def other_pair(n):
    return n + 1 if n % 2 else n - 1


def row_pair(i, j):
    return (i, other_pair(j)) if 0 <= other_pair(j) < lax.axis_size("gy") else (pair(i), j)


def per_device(air, out_tables, out_panels, depth, temp, salt, in_tables, in_panels):
    out_panels = out_panels.reshape(4, 1024, 128)
    in_panels = in_panels.reshape(4, 1024, 128)
    out_tables, in_tables = out_tables[0, 0], in_tables[0, 0]
    field = (2, LEVELS, ROWS, COLS)
    rows = LIST_ROWS + ROWS
    tiled, out_tables, out_panels, temp, salt, depth, to_dg, to_z, to_core, to_gy = call(
        outbound_kernel,
        [
            jax.ShapeDtypeStruct((64, 1024), BF16),
            jax.ShapeDtypeStruct(out_tables.shape, jnp.int32),
            jax.ShapeDtypeStruct((4, 1024, 128), BF16),
            temp.shape,
            salt.shape,
            jax.ShapeDtypeStruct(depth.shape, jnp.int32),
            (rows + 24, 128),
            (rows + 16, 128),
            (rows, 128),
            (rows + 8, 128),
        ],
        [air, out_tables, out_panels, temp, salt, depth],
        [pltpu.VMEM(air.shape, BF16), pltpu.SemaphoreType.DMA((9,))],
        hbm_in=range(6),
    )
    dg = send(to_dg, lambda i, j: (i - 1, j - 1) if j else (i, j - 1))
    zpair = send(to_z, lambda i, j: (other_pair(i), j))
    gy = send(to_gy, lambda i, j: (i, j - 1))
    core = send(to_core, lambda i, j: (pair(i), j))
    ones = jax.ShapeDtypeStruct((4, 64, 64), BF16)
    own, partial, *maps = call(
        inner_kernel,
        [(LIST_ROWS, 128), field, ones, ones, jax.ShapeDtypeStruct((512, 128), BF16)],
        [tiled, out_tables, out_panels, temp, salt, depth, in_tables],
        [pltpu.VMEM(in_tables.shape, jnp.int32), pltpu.SemaphoreType.DMA],
        hbm_in=(6,),
    )
    base, west, east, depths, partial = call(
        edge_kernel,
        [(LIST_ROWS, 128), (ROWS, 128), (ROWS, 128), (4, ROWS, COLS), field],
        [own, core, zpair, partial, temp, salt, depth],
    )
    stepped, cols, planes = call(
        first_kernel,
        [field, (ROWS, 128), (4, ROWS, COLS)],
        [dg, gy, base, partial, temp, salt, depth],
    )
    row_e, row_o, keep = call(
        rows_kernel,
        [(48, COLS), (43, COLS), (44, COLS)],
        [stepped, temp, salt, depth, west, east],
    )
    xo = send(row_o, row_pair)
    xe = send(row_e, lambda i, j: (i, pair(j)))
    zpair = send(cols, lambda i, j: (other_pair(i), j))
    core = send(cols, lambda i, j: (pair(i), j))
    state = [stepped, core, zpair, xe, xo, planes, depths, keep, depth]
    top_temp, top_salt, blocks, to_dg, to_gy, to_gx = call(
        second_kernel,
        [
            (TOP_LEVELS[0][1], ROWS, COLS),
            (TOP_LEVELS[1][1], ROWS, COLS),
            jax.ShapeDtypeStruct((64, COLS), BF16),
            (48, 128),
            (40, 128),
            (32, 128),
        ],
        state + maps + [in_panels],
    )
    dg = send(to_dg, lambda i, j: (i + 1, j + 1) if j + 1 < lax.axis_size("gy") else (i, j + 1))
    gy = send(to_gy, lambda i, j: (i, j + 1))
    gx = send(to_gx, lambda i, j: (i + 1, j))
    new_temp, new_salt, own = call(
        outer_kernel,
        [temp.shape, salt.shape, (32, 128)],
        state + [top_temp, top_salt, blocks, *maps, in_panels],
        [pltpu.VMEM(field, F32), pltpu.SemaphoreType.DMA((4,))],
        hbm_out=(0, 1),
    )
    (surface,) = call(final_kernel, [(4, 8, 128)], [dg, gy, gx, own])
    return new_temp, new_salt, surface


def solution(mesh):
    in_specs = (
        P(None, "gy", "gx"),
        P("gy", "gx", None, None, None, None),
        P("gy", "gx", None, None, None, None, None),
        P("gy", "gx"),
        P(None, "gy", "gx"),
        P(None, "gy", "gx"),
        P("gy", "gx", None, None, None, None),
        P("gy", "gx", None, None, None, None, None),
    )
    out_specs = (P(None, "gy", "gx"), P(None, "gy", "gx"), P(None, "gy", "gx"))
    return jax.shard_map(
        per_device, mesh=mesh, in_specs=in_specs, out_specs=out_specs, check_vma=False
    )
```

```python
import jax
import jax.numpy as jnp
from jax import lax
from jax.experimental import pallas as pl
from jax.experimental.pallas import tpu as pltpu
from jax.sharding import PartitionSpec as P

HEAT_RATE = 0.1
SHORTWAVE_RATE = 0.1
FRESH_RATE = 0.05
SIDE_RATE = 0.18
MIX_BASE = 0.03
MIX_WIND = 0.09
MIX_DECAY = 0.8

ROWS, COLS, LEVELS = 16, 512, 10
TILES = COLS // 128
F32, BF16 = jnp.float32, jnp.bfloat16
LIST_ROWS = 4 * 64
TOP_LEVELS = ((0, 3), (0, 1))
VMEM = pl.BlockSpec(memory_space=pltpu.VMEM)
HBM = pl.BlockSpec(memory_space=pltpu.HBM)
NN = (((1,), (0,)), ((), ()))
TN = (((0,), (0,)), ((), ()))
NT = (((1,), (1,)), ((), ()))


def iota(shape, axis):
    return lax.broadcasted_iota(jnp.int32, shape, axis)


def dot(x, y, dims=NN):
    return lax.dot_general(x, y, dims, preferred_element_type=F32)


def dot_split(ones, values):
    high = values.astype(BF16)
    low = (values - high.astype(F32)).astype(BF16)
    return dot(jnp.concatenate([ones, ones], 1), jnp.concatenate([high, low], 0))


def split_dot(values, ones):
    high = values.astype(BF16)
    low = (values - high.astype(F32)).astype(BF16)
    return dot(high, ones) + dot(low, ones)


def ocean_number(shape, axis):
    place = iota(shape, axis)
    return place % ROWS * TILES + place // ROWS


def atm_number(shape, axis):
    place = iota(shape, axis)
    return place % 8 * 8 + place // 8


def one_hot(number, names):
    return jnp.where(number == names, 1.0, 0.0).astype(BF16)


def group_mask():
    return iota((8, 128), 1) // 16 == iota((8, 128), 0)


def edge_columns(levels):
    lane = iota((ROWS, 128), 1)
    block = jnp.zeros((ROWS, 128), F32)
    for at, values in enumerate(levels):
        block = jnp.where(lane == at, values[:, 0:1], block)
        block = jnp.where(lane == 64 + at, values[:, COLS - 1 : COLS], block)
    return block


def spread_air(air, mask):
    fold = (iota((128, 128), 0) % 16 == iota((128, 128), 1) % 16).astype(F32).astype(BF16)
    spread = []
    for c in range(8):
        field = air[c].astype(F32)
        for r in range(8):
            row = jnp.broadcast_to(field[r : r + 1], (8, 128))
            spread.append(jnp.where(mask, row, 0.0))
    tiled = dot(jnp.concatenate(spread, 0).astype(BF16), fold).astype(BF16)
    return jnp.concatenate([tiled[c * 64 : (c + 1) * 64] for c in range(8)], 1)


def outbound_lists(kinds, tiled, table, panels, outs, wait=lambda: None):
    mask = group_mask()
    source = iota((64, 64), 0)
    target = ocean_number((64, 64), 0)
    ones = jnp.concatenate([one_hot(source, table[a, b, 0:1, :]) for a, b in kinds], 1)
    picked = dot(ones, tiled, TN)
    wait()
    pieces = []
    for n, (a, b) in enumerate(kinds):
        planes = [[], [], [], []]
        for g in range(8):
            part = picked[n * 64 + g * 8 : n * 64 + (g + 1) * 8]
            left = [jnp.where(mask, part[:, c * 128 : (c + 1) * 128], 0.0) for c in range(8)]
            piece = dot(
                jnp.concatenate(left, 0).astype(BF16),
                panels[2 * a + b, g * 128 : (g + 1) * 128, :],
            )
            f = [piece[c * 8 : (c + 1) * 8] for c in range(8)]
            planes[0].append(f[0] + f[1] + f[2])
            planes[1].append(f[3])
            planes[2].append(f[4] - f[5] + f[6])
            planes[3].append(f[7])
        pieces.append(jnp.concatenate([jnp.concatenate(p, 0) for p in planes], 1))
    for (a, b), values, places in zip(kinds, pieces, outs):
        summed = dot_split(one_hot(target, table[a, b, 1:2, :]), values)
        for out in places:
            for p in range(4):
                out[p * 64 : (p + 1) * 64, :] = summed[:, p * 128 : (p + 1) * 128]


def fetch(sems, pairs):
    copies = [pltpu.make_async_copy(src, dst, sems.at[n]) for n, (src, dst) in enumerate(pairs)]
    for copy in copies:
        copy.start()
    return copies


def outbound_kernel(
    air_hbm, table_hbm, panels_hbm, temp_hbm, salt_hbm, depth_hbm,
    tiled, table, panels, temp, salt, depth, to_dg, to_z, to_core, to_gy, air, sems,
):
    pairs = [(air_hbm, air), (table_hbm, table)]
    pairs += [(panels_hbm.at[n], panels.at[n]) for n in range(3)]
    pairs += [(temp_hbm, temp), (salt_hbm, salt), (depth_hbm, depth)]
    copies = fetch(sems, pairs + [(panels_hbm.at[3], panels.at[3])])
    for out in (to_dg, to_z, to_gy):
        out[LIST_ROWS:, :] = jnp.zeros((out.shape[0] - LIST_ROWS, 128), F32)

    def rest():
        for copy in copies[2:8]:
            copy.wait()
        deep = depth[...].astype(F32)
        levels = [temp[l] for l in range(LEVELS)] + [salt[l] for l in range(LEVELS)] + [deep]
        block = edge_columns(levels)
        for out in (to_z, to_core):
            out[LIST_ROWS : LIST_ROWS + ROWS, :] = block

    copies[0].wait()
    spread = spread_air(air, group_mask())
    tiled[...] = spread
    copies[1].wait()
    kinds, outs = ((0, 0), (1, 0), (0, 1)), ((to_dg,), (to_z, to_core), (to_gy,))
    outbound_lists(kinds, spread, table, panels, outs, rest)
    copies[8].wait()


def beside(values, north, south, west, east):
    row, col = iota((ROWS, COLS), 0), iota((ROWS, COLS), 1)
    return (
        jnp.where(row == 0, north, pltpu.roll(values, 1, 0)),
        jnp.where(row == ROWS - 1, south, pltpu.roll(values, ROWS - 1, 0)),
        jnp.where(col == 0, west, pltpu.roll(values, 1, 1)),
        jnp.where(col == COLS - 1, east, pltpu.roll(values, COLS - 1, 1)),
    )


def side_sum(centre, nears, wets):
    side = jnp.zeros_like(centre)
    for near, there in zip(nears, wets):
        side = side + jnp.where(there, near - centre, 0.0)
    return SIDE_RATE * side


def inner_kernel(
    tiled, table, panels, temp, salt, depth, in_table_hbm, own, partial, sources, targets, fold,
    in_table, sem,
):
    copy = pltpu.make_async_copy(in_table_hbm, in_table, sem)
    copy.start()
    deep = depth[...].astype(F32)
    dry = jnp.zeros((1, 1), F32)
    around = beside(deep, dry, dry, dry, dry)
    for l in range(LEVELS):
        wet = deep > l
        wets = [d > l for d in around]
        for t, field in enumerate((temp, salt)):
            centre = field[l]
            side = side_sum(centre, beside(centre, dry, dry, dry, dry), wets)
            partial[t, l] = centre + jnp.where(wet, side, 0.0)
    outbound_lists(((1, 1),), tiled[...], table, panels, ((own,),))
    copy.wait()
    fold[...] = inbound_fold()
    eye = one_hot(iota((64, 64), 0), iota((64, 64), 1))
    source_block, target = ocean_number((64, 64), 0), atm_number((64, 64), 0)
    for n in range(4):
        ones = one_hot(source_block, in_table[n // 2, n % 2, 0:1, :])
        sources[n] = dot(ones, eye, TN).astype(BF16)
        targets[n] = one_hot(target, in_table[n // 2, n % 2, 1:2, :])


def edge_kernel(own, core, zpair, partial, temp, salt, depth, base, west, east, depths, whole):
    odd_col = lax.axis_index("gx") % 2 == 1
    base[...] = own[...] + jnp.where(
        odd_col, zpair[0:LIST_ROWS, :], core[0:LIST_ROWS, :]
    )
    at = slice(LIST_ROWS, LIST_ROWS + ROWS)
    left = jnp.where(odd_col, core[at, :], zpair[at, :])
    right = jnp.where(odd_col, zpair[at, :], core[at, :])
    west[...] = left
    east[...] = right
    deep = depth[...].astype(F32)
    dry = jnp.zeros((1, 1), F32)
    last = 2 * LEVELS
    around = beside(deep, dry, dry, left[:, 64 + last : 65 + last], right[:, last : last + 1])
    for n in range(4):
        depths[n] = around[n]
    lane = iota((ROWS, 128), 1)
    sides = ((0, left, 64, around[2], 0), (COLS - 128, right, 0, around[3], 127))
    for t, field in enumerate((temp, salt)):
        for l in range(LEVELS):
            at = t * LEVELS + l
            whole[t, l] = partial[t, l]
            for first, halo, offset, far, spot in sides:
                here = (lane == spot) & (far[:, first : first + 128] > l)
                here = here & (deep[:, first : first + 128] > l)
                near = halo[:, offset + at : offset + at + 1] - field[l, :, first : first + 128]
                whole[t, l, :, first : first + 128] += jnp.where(here, SIDE_RATE * near, 0.0)


def column_change(values, below, mixing, depth, l, across):
    change = 0.0 if l == 0 else -across
    if l < LEVELS - 1:
        across = mixing * (MIX_DECAY**l) * (below - values)
        across = jnp.where(depth > l + 1, across, 0.0)
        change = change + across
    return change, across


def source(t, l, planes, values):
    if t == 0:
        heating = planes[1] * (SHORTWAVE_RATE * 2.718281828459045 ** (-0.5 * l))
        return heating + HEAT_RATE * planes[0] if l == 0 else heating
    return -FRESH_RATE * planes[2] * values if l == 0 else 0.0


def first_kernel(
    dg, gy, base, partial, temp, salt, depth, new, cols, planes
):
    forcing = []
    for p in range(4):
        parts = []
        for s in range(TILES):
            at = p * 64 + s * ROWS
            parts.append(base[at : at + ROWS, :] + gy[at : at + ROWS, :] + dg[at : at + ROWS, :])
        forcing.append(jnp.concatenate(parts, 1))
    squared = forcing[3] * forcing[3]
    forcing[3] = squared / (1.0 + squared)
    for p in range(4):
        planes[p] = forcing[p]
    deep = depth[...].astype(F32)
    lane = iota((ROWS, 128), 1)
    mixing = MIX_BASE + MIX_WIND * forcing[3]
    block = jnp.zeros((ROWS, 128), F32)
    for t, field in enumerate((temp, salt)):
        across = None
        for l in range(LEVELS):
            at = t * LEVELS + l
            centre = field[l]
            change, across = column_change(
                centre, field[min(l + 1, LEVELS - 1)], mixing, deep, l, across
            )
            change = change + source(t, l, forcing, centre)
            value = partial[t, l] + jnp.where(deep > l, change, 0.0)
            new[t, l] = value
            block = jnp.where(lane == at, value[:, 0:1], block)
            block = jnp.where(lane == 64 + at, value[:, COLS - 1 : COLS], block)
    cols[...] = block


def rows_kernel(new, temp, salt, depth, west, east, row_e, row_o, keep):
    odd_row = lax.axis_index("gy") % 2 == 1
    deep = depth[...].astype(F32)
    edges = []
    for r in (0, ROWS - 1):
        rows = [new[0, :, r, :], new[1, :, r, :], temp[:, r, :], salt[:, r, :], deep[r : r + 1]]
        edges.append(rows + [west[r : r + 1, :], east[r : r + 1, :]])
    for out, first in ((row_e, odd_row), (row_o, jnp.logical_not(odd_row))):
        at = 0
        for a, b in zip(*edges):
            out[at : at + a.shape[0], 0 : a.shape[1]] = jnp.where(first, a, b)
            at += a.shape[0]
    row_e[43:48, :] = jnp.zeros((5, COLS), F32)
    for n in range(2):
        keep[20 * n : 20 * n + 10, :] = edges[n][2]
        keep[20 * n + 10 : 20 * n + 20, :] = edges[n][3]
        keep[40 + 2 * n : 41 + 2 * n, 0:128] = edges[n][5]
        keep[41 + 2 * n : 42 + 2 * n, 0:128] = edges[n][6]


def inbound_lists(kinds, blocks, sources, targets, fold, panels, outs):
    mask = group_mask()
    numbers = [2 * a + b for a, b in kinds]
    chosen = dot(jnp.concatenate([sources[n] for n in numbers], 0), blocks)
    lists = []
    for m, n in enumerate(numbers):
        kept = [[], [], [], []]
        for g in range(8):
            part = chosen[m * 64 + g * 8 : m * 64 + (g + 1) * 8]
            left = [part[:, c * 128 : (c + 1) * 128] for c in range(4)]
            piece = dot(
                jnp.concatenate(left, 0).astype(BF16), panels[n, g * 128 : (g + 1) * 128, :], NT
            )
            for c in range(4):
                kept[c].append(jnp.where(mask, piece[c * 8 : (c + 1) * 8], 0.0))
        lists.append(jnp.concatenate([jnp.concatenate(k, 0) for k in kept], 1))
    pieces = split_dot(jnp.concatenate(lists, 0), fold)
    for m, (n, out) in enumerate(zip(numbers, outs)):
        summed = dot_split(targets[n], pieces[m * 64 : (m + 1) * 64])
        out[0:32, :] = summed[0:32] + pltpu.roll(summed[32:64], 64, 1)
        if out.shape[0] > 32:
            out[32:, :] = jnp.zeros((out.shape[0] - 32, 128), F32)


def inbound_fold():
    place, lane = iota((512, 128), 0), iota((512, 128), 1)
    fold = jnp.where((place // 128 == lane // 16) & (place % 16 == lane % 16), 1.0, 0.0)
    return fold.astype(BF16)


def second_step(levels, old, core, zpair, xe, xo, planes, depths, keep, depth, store):
    odd_col = lax.axis_index("gx") % 2 == 1
    odd_row = lax.axis_index("gy") % 2 == 1
    deep = depth[...].astype(F32)
    row_e, row_o = xe[0:43, :], xo[...]
    beyond = (jnp.where(odd_row, row_e, row_o), jnp.where(odd_row, row_o, row_e))
    level = iota((2 * LEVELS, COLS), 0) % LEVELS
    at_end = (lax.axis_index("gy") == 0, lax.axis_index("gy") == lax.axis_size("gy") - 1)
    beyond_deep = [jnp.where(end, 0.0, other[40:41]) for end, other in zip(at_end, beyond)]
    fixes, halo_rows = [], []
    for n, other in enumerate(beyond):
        r = n * (ROWS - 1)
        here = (deep[r : r + 1] > level) & (beyond_deep[n] > level)
        fix = jnp.where(here, SIDE_RATE * (other[20:40] - keep[20 * n : 20 * n + 20, :]), 0.0)
        fixes.append(fix)
        halo_rows.append(other[0:20] - fix)
    norths, souths = halo_rows
    level = iota((1, 128), 1) % 64 % LEVELS
    row = iota((ROWS, 128), 0)
    ends = []
    for halo, at, deepest in (
        (jnp.where(odd_col, core[...], zpair[...]), 0, 84),
        (jnp.where(odd_col, zpair[...], core[...]), 1, 20),
    ):
        for n, other in enumerate(beyond):
            mine = keep[40 + 2 * n + at : 41 + 2 * n + at, 0:128]
            far = other[41 + at : 42 + at, 0:128]
            here = mine[:, deepest : deepest + 1] > level
            here = here & (jnp.where(at_end[n], 0.0, far[:, deepest : deepest + 1]) > level)
            fix = jnp.where(here, SIDE_RATE * (far - mine), 0.0)
            halo = halo + jnp.where(row == n * (ROWS - 1), fix, 0.0)
        ends.append(halo)
    west, east = ends
    row8, row = iota((8, COLS), 0), iota((ROWS, COLS), 0)
    around = [depths[n] for n in range(4)]
    around[0] = jnp.where(row == 0, beyond_deep[0], around[0])
    around[1] = jnp.where(row == ROWS - 1, beyond_deep[1], around[1])
    forcing = [planes[p] for p in range(4)]
    mixing = MIX_BASE + MIX_WIND * forcing[3]
    def whole(t, l):
        at = t * LEVELS + l
        high = old[t, l, 0:8, :] + jnp.where(row8 == 0, fixes[0][at : at + 1], 0.0)
        low = old[t, l, 8:16, :] + jnp.where(row8 == 7, fixes[1][at : at + 1], 0.0)
        return jnp.concatenate([high, low], 0)

    for t, (start, stop) in enumerate(levels):
        across, centre = None, whole(t, start)
        if start:
            across = mixing * (MIX_DECAY ** (start - 1)) * (centre - whole(t, start - 1))
            across = jnp.where(deep > start, across, 0.0)
        for l in range(start, stop):
            at = t * LEVELS + l
            below = whole(t, l + 1) if l < LEVELS - 1 else None
            change, across = column_change(centre, below, mixing, deep, l, across)
            change = change + source(t, l, forcing, centre)
            nears = beside(
                centre,
                norths[at : at + 1],
                souths[at : at + 1],
                west[:, 64 + at : 65 + at],
                east[:, at : at + 1],
            )
            change = change + side_sum(centre, nears, [d > l for d in around])
            store(t, l, centre + jnp.where(deep > l, change, 0.0))
            centre = below


def second_kernel(
    old, core, zpair, xe, xo, planes, depths, keep, depth, sources, targets, fold, panels,
    top_temp, top_salt, surface_blocks, to_dg, to_gy, to_gx,
):
    top = {}

    def store(t, l, value):
        (top_temp, top_salt)[t][l] = value
        top[t, l] = value

    second_step(TOP_LEVELS, old, core, zpair, xe, xo, planes, depths, keep, depth, store)
    deep = depth[...].astype(F32)
    wet_top = jnp.where(deep > 0, 1.0, 0.0)
    surface = (
        top[0, 0] * wet_top,
        top[1, 0] * wet_top,
        (top[0, 0] + top[0, 1] + top[0, 2]) / 3.0 * wet_top,
        wet_top,
    )
    parts = []
    for f in surface:
        parts.append(jnp.concatenate([f[:, s * 128 : (s + 1) * 128] for s in range(TILES)], 0))
    blocks = jnp.concatenate(parts, 1).astype(BF16)
    surface_blocks[...] = blocks
    kinds, outs = ((1, 1), (1, 0), (0, 1)), (to_dg, to_gy, to_gx)
    inbound_lists(kinds, blocks, sources, targets, fold[...], panels, outs)


def outer_kernel(
    old, core, zpair, xe, xo, planes, depths, keep, depth, top_temp, top_salt,
    blocks, sources, targets, fold, panels, new_temp, new_salt, own, rest, sems,
):
    pairs = []
    for t, (top, new) in enumerate(((top_temp, new_temp), (top_salt, new_salt))):
        count = TOP_LEVELS[t][1]
        pairs.append((top, new.at[0:count]))
    copies = fetch(sems.at[0:2], pairs)

    def store(t, l, value):
        rest[t, l] = value

    levels = [(stop, LEVELS) for _, stop in TOP_LEVELS]
    second_step(levels, old, core, zpair, xe, xo, planes, depths, keep, depth, store)
    pairs = []
    for t, new in enumerate((new_temp, new_salt)):
        span = slice(TOP_LEVELS[t][1], LEVELS)
        pairs.append((rest.at[t, span], new.at[span]))
    copies += fetch(sems.at[2:4], pairs)
    inbound_lists(((0, 0),), blocks[...], sources, targets, fold[...], panels, (own,))
    for copy in copies:
        copy.wait()


def final_kernel(dg, gy, gx, own, out):
    total = own[...] + gx[0:32, :] + gy[0:32, :] + dg[0:32, :]
    group = iota((8, 128), 1) // 16
    for c in range(4):
        field = jnp.zeros((8, 128), F32)
        for k in range(8):
            part = total[k % 4 * 8 : (k % 4 + 1) * 8]
            moved = pltpu.roll(part, (k - c - k // 4 * 4) % 8 * 16, 1)
            field = jnp.where(group == k, moved, field)
        out[c] = field


def call(kernel, shapes, args, scratch=(), hbm_in=(), hbm_out=(), mib=12):
    args = [
        pltpu.with_memory_space_constraint(x, pltpu.HBM) if n in hbm_in else x
        for n, x in enumerate(args)
    ]
    shapes = [s if isinstance(s, jax.ShapeDtypeStruct) else jax.ShapeDtypeStruct(s, F32) for s in shapes]
    return pl.pallas_call(
        kernel,
        out_shape=shapes,
        in_specs=[HBM if n in hbm_in else VMEM for n in range(len(args))],
        out_specs=[HBM if n in hbm_out else VMEM for n in range(len(shapes))],
        scratch_shapes=list(scratch),
        compiler_params=pltpu.CompilerParams(vmem_limit_bytes=mib * 1024 * 1024),
    )(*args)


def send(block, step):
    wide, high = lax.axis_size("gx"), lax.axis_size("gy")
    route = []
    for i in range(wide):
        for j in range(high):
            to = step(i, j)
            route.append((i * high + j, to[0] % wide * high + to[1] % high))
    return lax.ppermute(block, ("gx", "gy"), route)


def pair(n):
    return n - 1 if n % 2 else n + 1


def other_pair(n):
    return n + 1 if n % 2 else n - 1


def row_pair(i, j):
    return (i, other_pair(j)) if 0 <= other_pair(j) < lax.axis_size("gy") else (pair(i), j)


def per_device(air, out_tables, out_panels, depth, temp, salt, in_tables, in_panels):
    out_panels = out_panels.reshape(4, 1024, 128)
    in_panels = in_panels.reshape(4, 1024, 128)
    out_tables, in_tables = out_tables[0, 0], in_tables[0, 0]
    field = (2, LEVELS, ROWS, COLS)
    rows = LIST_ROWS + ROWS
    tiled, out_tables, out_panels, temp, salt, depth, to_dg, to_z, to_core, to_gy = call(
        outbound_kernel,
        [
            jax.ShapeDtypeStruct((64, 1024), BF16),
            jax.ShapeDtypeStruct(out_tables.shape, jnp.int32),
            jax.ShapeDtypeStruct((4, 1024, 128), BF16),
            temp.shape,
            salt.shape,
            jax.ShapeDtypeStruct(depth.shape, jnp.int32),
            (rows + 24, 128),
            (rows + 16, 128),
            (rows, 128),
            (rows + 8, 128),
        ],
        [air, out_tables, out_panels, temp, salt, depth],
        [pltpu.VMEM(air.shape, BF16), pltpu.SemaphoreType.DMA((9,))],
        hbm_in=range(6),
    )
    dg = send(to_dg, lambda i, j: (i - 1, j - 1) if j else (i, j - 1))
    zpair = send(to_z, lambda i, j: (other_pair(i), j))
    gy = send(to_gy, lambda i, j: (i, j - 1))
    core = send(to_core, lambda i, j: (pair(i), j))
    ones = jax.ShapeDtypeStruct((4, 64, 64), BF16)
    own, partial, *maps = call(
        inner_kernel,
        [(LIST_ROWS, 128), field, ones, ones, jax.ShapeDtypeStruct((512, 128), BF16)],
        [tiled, out_tables, out_panels, temp, salt, depth, in_tables],
        [pltpu.VMEM(in_tables.shape, jnp.int32), pltpu.SemaphoreType.DMA],
        hbm_in=(6,),
    )
    base, west, east, depths, partial = call(
        edge_kernel,
        [(LIST_ROWS, 128), (ROWS, 128), (ROWS, 128), (4, ROWS, COLS), field],
        [own, core, zpair, partial, temp, salt, depth],
    )
    stepped, cols, planes = call(
        first_kernel,
        [field, (ROWS, 128), (4, ROWS, COLS)],
        [dg, gy, base, partial, temp, salt, depth],
    )
    row_e, row_o, keep = call(
        rows_kernel,
        [(48, COLS), (43, COLS), (44, COLS)],
        [stepped, temp, salt, depth, west, east],
    )
    xo = send(row_o, row_pair)
    xe = send(row_e, lambda i, j: (i, pair(j)))
    zpair = send(cols, lambda i, j: (other_pair(i), j))
    core = send(cols, lambda i, j: (pair(i), j))
    state = [stepped, core, zpair, xe, xo, planes, depths, keep, depth]
    top_temp, top_salt, blocks, to_dg, to_gy, to_gx = call(
        second_kernel,
        [
            (TOP_LEVELS[0][1], ROWS, COLS),
            (TOP_LEVELS[1][1], ROWS, COLS),
            jax.ShapeDtypeStruct((64, COLS), BF16),
            (32, 128),
            (32, 128),
            (32, 128),
        ],
        state + maps + [in_panels],
    )
    dg = send(to_dg, lambda i, j: (i + 1, j + 1) if j + 1 < lax.axis_size("gy") else (i, j + 1))
    gy = send(to_gy, lambda i, j: (i, j + 1))
    gx = send(to_gx, lambda i, j: (i + 1, j))
    new_temp, new_salt, own = call(
        outer_kernel,
        [temp.shape, salt.shape, (32, 128)],
        state + [top_temp, top_salt, blocks, *maps, in_panels],
        [pltpu.VMEM(field, F32), pltpu.SemaphoreType.DMA((4,))],
        hbm_out=(0, 1),
    )
    (surface,) = call(final_kernel, [(4, 8, 128)], [dg, gy, gx, own])
    return new_temp, new_salt, surface


def solution(mesh):
    in_specs = (
        P(None, "gy", "gx"),
        P("gy", "gx", None, None, None, None),
        P("gy", "gx", None, None, None, None, None),
        P("gy", "gx"),
        P(None, "gy", "gx"),
        P(None, "gy", "gx"),
        P("gy", "gx", None, None, None, None),
        P("gy", "gx", None, None, None, None, None),
    )
    out_specs = (P(None, "gy", "gx"), P(None, "gy", "gx"), P(None, "gy", "gx"))
    return jax.shard_map(
        per_device, mesh=mesh, in_specs=in_specs, out_specs=out_specs, check_vma=False
    )
```
